32 devices in a mesh: pair: 16 (over z, x, core), virt: 2 (over y).
Axes of the slice: x: 2, y: 2, z: 4, core: 2. Of those that a mesh axis runs over, the one named last changes fastest.
Arguments:
- amplitudes: bfloat16 [64, 1024, 1024], P('pair', None, 'virt'), may hold values from -0.1796875 to 0.1796875
- cholesky: bfloat16 [8, 1024, 1792], P(None, 'virt', 'pair'), may hold values from -0.1640625 to 0.1640625
- energy_first: float32 [8], replicated, may hold values from -3 to -0.3
- energy_second: float32 [8], replicated, may hold values from -3 to -0.3
- energy_virtual: float32 [1024], replicated, may hold values from 0.2 to 4
Outputs:
- residual: bfloat16 [64, 1024, 1024], P('pair', None, 'virt')
The draws below stay inside these ranges and needn't reach their ends.
All inputs are finite; a program needn't handle non-finite values.
Results may differ from the reference program's by a relative error of at most 0.0095.
Values may be sent and summed in bfloat16 or wider, within the bound.
No kernel may reach another device: no remote copies, remote signals or barrier semaphores. Data moves between devices by JAX's collectives and lax.ppermute only.
A program may use at most 128 MiB of HBM per device.

```python
import jax
import jax.numpy as jnp
from jax import lax

OCC = 8
VIRT = 1024
NCHOL = 1792
PAIR_DEV = 4
PAIRS = 64
OCC_ROWS = 8
N_VIRT = 2


def block_levels(stream_key, extent, split, least, high):
    loudness = 1.0
    for position, blocks in split:
        steps = jax.random.uniform(jax.random.fold_in(jax.random.fold_in(stream_key, 6), position), (blocks,), jnp.float32, least / len(split), high / len(split))
        loudness = loudness * jnp.repeat(jnp.exp(steps), extent[position] // blocks).reshape((-1,) + (1,) * (len(extent) - 1 - position))
    return loudness


def normal_values(own_key, extent, width, most, split=(), kind=jnp.bfloat16):
    drawn = width * jax.random.normal(own_key, extent, jnp.float32)
    if split:
        drawn = drawn * block_levels(own_key, extent, split, -0.22, 0.18)
    return jnp.clip(drawn, -most, most).astype(kind)


def setup_inputs(seed: int = 0) -> dict:
    streams_of = jax.random.split(jax.random.key(seed), 6)
    return {
        "amplitudes": normal_values(streams_of[0], (PAIRS, VIRT, VIRT), 0.03, 0.1796875, ((0, 16), (2, 2))),
        "cholesky": normal_values(streams_of[1], (OCC, VIRT, NCHOL), (1.7 * (OCC * VIRT * NCHOL) ** -0.25), 0.1640625, ((1, 2), (2, 16))),
        "energy_first": jnp.clip(jax.random.uniform(streams_of[2], (OCC_ROWS,), jnp.float32, -3.0, -0.3), -3.0, -0.3),
        "energy_second": jnp.clip(jax.random.uniform(streams_of[3], (OCC,), jnp.float32, -3.0, -0.3), -3.0, -0.3),
        "energy_virtual": jnp.clip(jax.random.uniform(streams_of[4], (VIRT,), jnp.float32, 0.2, 4.0), 0.2, 4.0),
    }


def reference(amplitudes, cholesky, energy_first, energy_second, energy_virtual):
    vectors = cholesky.astype(jnp.float32)
    group_width = min(PAIR_DEV, OCC)
    group_count = OCC // group_width
    tile_width = VIRT // N_VIRT
    split_vectors = vectors.reshape(group_count, group_width, N_VIRT, tile_width, NCHOL)
    blocks = amplitudes.reshape(OCC_ROWS, OCC, VIRT, VIRT)
    virtual_pairs = energy_virtual[:, None] + energy_virtual[None, :]

    def one_row(inputs):
        block, first_energy = inputs
        values = block.astype(jnp.float32)
        combined = (2.0 * values - jnp.swapaxes(values, 1, 2)).astype(jnp.bfloat16)
        combined = lax.optimization_barrier(combined).astype(jnp.float32)
        split_combined = combined.reshape(group_count, group_width, VIRT, N_VIRT, tile_width)
        terms = jnp.einsum("gsatd,gstdq->gtaq", split_combined, split_vectors)
        terms = lax.optimization_barrier(terms.astype(jnp.bfloat16)).astype(jnp.float32)
        tile_sum = jnp.sum(terms, axis=1)
        tile_sum = lax.optimization_barrier(tile_sum.astype(jnp.bfloat16)).astype(jnp.float32)
        middle = jnp.sum(tile_sum, axis=0)
        middle = lax.optimization_barrier(middle.astype(jnp.bfloat16)).astype(jnp.float32)
        cycle_term = jnp.einsum("aq,lbq->lab", middle, vectors)
        diagonal = virtual_pairs[None, :, :] - first_energy - energy_second[:, None, None]
        return (diagonal * values + cycle_term).astype(jnp.bfloat16)

    results = lax.map(one_row, (blocks, energy_first))
    return results.reshape(OCC_ROWS * OCC, VIRT, VIRT)
```

```python
import functools

import jax
import jax.numpy as jnp
from jax import lax
from jax.experimental import pallas as pl
from jax.experimental.pallas import tpu as pltpu
from jax.sharding import PartitionSpec as P

OCC = 8
BF16, F32 = jnp.bfloat16, jnp.float32
VMEM_LIMIT = 48 * 2**20


def params(steps=1):
    return pltpu.CompilerParams(
        dimension_semantics=("arbitrary",) * steps, vmem_limit_bytes=VMEM_LIMIT
    )


def anywhere(count):
    return [pl.BlockSpec(memory_space=pl.ANY)] * count


def swap(x, axis, bit):
    return lax.ppermute(x, axis, [(i, i ^ 1 << bit) for i in range(lax.axis_size(axis))])


def ring_of(count, groups):
    places = count // groups
    return list(range(0, places, 2)) + list(range(places - 1, 0, -2))


def along_ring(x, step, groups):
    order = ring_of(lax.axis_size("pair"), groups)
    pairs = [
        (a * groups + g, order[(n + step) % len(order)] * groups + g)
        for n, a in enumerate(order)
        for g in range(groups)
    ]
    return lax.ppermute(x, "pair", pairs)


def turn_kernel(tile, own, other, near, far):
    x = own[0].astype(F32)
    near[0] = (2.0 * x.T - x).astype(BF16)
    far[0] = other[0].T


def turn(tile, amplitudes):
    count, rows, width = amplitudes.shape
    block = (1, width, width)
    return pl.pallas_call(
        turn_kernel,
        grid_spec=pltpu.PrefetchScalarGridSpec(
            num_scalar_prefetch=1,
            grid=(count,),
            in_specs=[
                pl.BlockSpec(block, lambda j, t: (j, t[0], 0)),
                pl.BlockSpec(block, lambda j, t: (j, 1 - t[0], 0)),
            ],
            out_specs=[pl.BlockSpec(block, lambda j, t: (j, 0, 0))] * 2,
        ),
        out_shape=[jax.ShapeDtypeStruct((count, width, width), BF16)] * 2,
        compiler_params=params(),
        name="turn",
    )(tile, amplitudes, amplitudes)


def mix_kernel(far, arrived, out):
    out[...] = (2.0 * far[...].astype(F32) - arrived[...].astype(F32)).astype(BF16)


def mix(far, arrived):
    count, width, _ = far.shape
    spec = pl.BlockSpec((1, width, width), lambda j: (j, 0, 0))
    return pl.pallas_call(
        mix_kernel,
        grid=(count,),
        in_specs=[spec, spec],
        out_specs=spec,
        out_shape=jax.ShapeDtypeStruct(far.shape, BF16),
        compiler_params=params(),
        name="mix",
    )(far, arrived)


def partial_kernel(shards, halves, *refs):
    same, cross = refs[:shards], refs[shards : 2 * shards]
    mine, theirs = refs[2 * shards : 2 * shards + halves], refs[2 * shards + halves : 2 * shards + 2 * halves]
    outs, total = refs[-1 - halves : -1], refs[-1]
    j = pl.program_id(0)
    left = jnp.concatenate([r[0] for r in same], axis=0)
    right = jnp.concatenate([r[0] for r in cross], axis=0)
    for h in range(halves):
        value = jnp.dot(left, mine[h][0], preferred_element_type=F32)
        value += jnp.dot(right, theirs[h][0], preferred_element_type=F32)

        @pl.when(j == 0)
        def _():
            total[h] = value

        @pl.when(j > 0)
        def _():
            total[h] += value

        @pl.when(j == pl.num_programs(0) - 1)
        def _():
            outs[h][...] = total[h].astype(BF16)


def partial(same, cross, mine, theirs, after=()):
    shards, halves = len(same), len(mine)
    count, width, columns = mine[0].shape
    depth = same[0].shape[1]
    rows = shards * depth

    def body(*refs):
        keep = 2 * shards + 2 * halves
        partial_kernel(shards, halves, *refs[:keep], *refs[keep + len(after) :])

    return pl.pallas_call(
        body,
        grid=(count,),
        in_specs=[pl.BlockSpec((1, depth, width), lambda j: (j, 0, 0))] * (2 * shards)
        + [pl.BlockSpec((1, width, columns), lambda j: (j, 0, 0))] * (2 * halves)
        + anywhere(len(after)),
        out_specs=[pl.BlockSpec((rows, columns), lambda j: (0, 0))] * halves,
        out_shape=[jax.ShapeDtypeStruct((rows, columns), BF16)] * halves,
        scratch_shapes=[pltpu.VMEM((halves, rows, columns), F32)],
        compiler_params=params(),
        name="partial",
    )(*same, *cross, *mine, *theirs, *after)


def gate_kernel(count, *refs):
    pass


def gate(values, after):
    count = len(values)
    return pl.pallas_call(
        functools.partial(gate_kernel, count),
        in_specs=anywhere(count + len(after)),
        out_specs=anywhere(count),
        out_shape=[jax.ShapeDtypeStruct(v.shape, v.dtype) for v in values],
        input_output_aliases={n: n for n in range(count)},
        name="gate",
    )(*values, *after)


def join_kernel(near, far, near_sent, far_sent, out):
    out[0] = (near[...].astype(F32) + far_sent[...].astype(F32)).astype(BF16)
    out[1] = (far[...].astype(F32) + near_sent[...].astype(F32)).astype(BF16)


def join(near, far, near_sent, far_sent):
    rows, columns = near.shape
    return pl.pallas_call(
        join_kernel,
        in_specs=[pl.BlockSpec(memory_space=pltpu.VMEM)] * 4,
        out_specs=pl.BlockSpec(memory_space=pltpu.VMEM),
        out_shape=jax.ShapeDtypeStruct((2, rows, columns), BF16),
        compiler_params=pltpu.CompilerParams(vmem_limit_bytes=VMEM_LIMIT),
        name="join",
    )(near, far, near_sent, far_sent)


def residual_kernel(chunks, shards, first, last, after, tile, *refs):
    middles = refs[:chunks]
    vectors = refs[chunks : chunks + shards]
    rest = refs[chunks + shards :]
    if first:
        values, row_energy, column_energy, small = rest[:4]
        rest = rest[4:]
    else:
        before = rest[0]
        rest = rest[1:]
    out, turned, stacked = rest[after:]
    j, h = pl.program_id(0), pl.program_id(1)

    @pl.when(j == 0)
    def _():
        turned[h] = jnp.concatenate([m[h] for m in middles], axis=0).T

    @pl.when(h == 0)
    def _():
        stacked[...] = jnp.concatenate([v[0] for v in vectors], axis=0)

    total = jnp.dot(turned[h], stacked[...], preferred_element_type=F32)
    if first:
        diagonal = row_energy[...] + column_energy[...] - small[0] - small[1 + j]
        total += diagonal * values[0].astype(F32)
    else:
        total += before[0]
    out[0] = total.astype(out.dtype)


def residual(tile, middles, vectors, first=None, before=None, last=True, after=()):
    count, depth, width = vectors[0].shape
    columns = middles[0].shape[2]
    total_rows = sum(m.shape[1] for m in middles)
    assert total_rows == depth * len(vectors)
    by_row = pl.BlockSpec((1, columns, width), lambda j, h, t: (j, (t[0] + h) % 2, 0))
    in_specs = [pl.BlockSpec(m.shape, lambda j, h, t: (0, 0, 0)) for m in middles]
    in_specs += [pl.BlockSpec((1, depth, width), lambda j, h, t: (j, 0, 0))] * len(vectors)
    args = [*middles, *vectors]
    if first is not None:
        in_specs += [
            by_row,
            pl.BlockSpec((columns, 1), lambda j, h, t: ((t[0] + h) % 2, 0)),
            pl.BlockSpec((1, width), lambda j, h, t: (0, 0)),
            pl.BlockSpec(memory_space=pltpu.SMEM),
        ]
        args += first
    else:
        in_specs += [by_row]
        args += [before]
    return pl.pallas_call(
        functools.partial(
            residual_kernel, len(middles), len(vectors), first is not None, last, len(after)
        ),
        grid_spec=pltpu.PrefetchScalarGridSpec(
            num_scalar_prefetch=1,
            grid=(count, 2),
            in_specs=in_specs + anywhere(len(after)),
            out_specs=by_row,
            scratch_shapes=[
                pltpu.VMEM((2, columns, total_rows), BF16),
                pltpu.VMEM((total_rows, width), BF16),
            ],
        ),
        out_shape=jax.ShapeDtypeStruct((count, 2 * columns, width), BF16 if last else F32),
        compiler_params=params(2),
        name="residual",
    )(tile, *args, *after)


def two_tiles(amplitudes, cholesky, energy_first, energy_second, energy_virtual):
    count, virtual, width = amplitudes.shape
    groups = OCC // count
    places = lax.axis_size("pair") // groups
    place, group = lax.axis_index("pair") // groups, lax.axis_index("pair") % groups
    y = lax.axis_index("virt")
    tile = y.astype(jnp.int32).reshape(1)

    vectors = jnp.swapaxes(cholesky, 1, 2)
    same = [lax.dynamic_slice_in_dim(vectors, group * count, count, 0)]
    cross = [lax.dynamic_slice_in_dim(vectors, (1 - group) * count, count, 0)]

    ring = functools.partial(along_ring, groups=groups)
    half = places // 2
    forth_same, back_same = same[0], same[0]
    forth_cross, back_cross = cross[0], cross[0]
    for step in range(1, half):
        forth_same, back_same = ring(forth_same, 1), ring(back_same, -1)
        forth_cross, back_cross = ring(forth_cross, 1), ring(back_cross, -1)
        same += [forth_same, back_same]
        cross += [forth_cross, back_cross]
    same += [ring(forth_same, 1)]
    cross += [ring(back_cross, -1)]

    sent = lax.dynamic_slice_in_dim(amplitudes, (1 - y) * width, width, 1)
    arrived = swap(sent, "virt", 0)

    near, far_turned = turn(tile, amplitudes)
    near_theirs = swap(near, "pair", 0)

    (n1,) = partial(same[:3], cross[:3], [near], [near_theirs])
    (n2,) = partial(same[3:5], cross[3:5], [near], [near_theirs])
    far = mix(far_turned, arrived)
    far_theirs = swap(far, "pair", 0)
    n1, n2 = gate([n1, n2], [arrived])
    n1_sent, n2_sent = swap(n1, "virt", 0), swap(n2, "virt", 0)
    (f1,) = partial(same[:3], cross[:3], [far], [far_theirs])
    (f2,) = partial(same[3:5], cross[3:5], [far], [far_theirs])
    f1_sent, f2_sent = swap(f1, "virt", 0), swap(f2, "virt", 0)
    n3, f3 = partial(same[5:7], cross[5:7], [near, far], [near_theirs, far_theirs])
    n3_sent, f3_sent = swap(n3, "virt", 0), swap(f3, "virt", 0)
    n4, f4 = partial(same[7:], cross[7:], [near, far], [near_theirs, far_theirs])
    n4_sent, f4_sent = swap(n4, "virt", 0), swap(f4, "virt", 0)

    handed = [swap(v, "pair", 0) for v in cross]
    m1 = join(n1, f1, n1_sent, f1_sent)
    m2 = join(n2, f2, n2_sent, f2_sent)
    h1, h2 = swap(m1, "pair", 0), swap(m2, "pair", 0)
    m3 = join(n3, f3, n3_sent, f3_sent)
    h3 = swap(m3, "pair", 0)
    m4 = join(n4, f4, n4_sent, f4_sent)
    h4 = swap(m4, "pair", 0)

    small = jnp.concatenate(
        [
            lax.dynamic_slice_in_dim(energy_first, place, 1, 0),
            lax.dynamic_slice_in_dim(energy_second, group * count, count, 0),
        ]
    )
    column_energy = lax.dynamic_slice_in_dim(energy_virtual, y * width, width, 0)
    diagonal = [amplitudes, energy_virtual[:, None], column_energy[None, :], small]
    started = residual(
        tile, [m1, m2, h1, h2], same[:5] + handed[:5], first=diagonal, last=False
    )
    return residual(tile, [m3, m4, h3, h4], same[5:] + handed[5:], before=started)


def from_partner(x, axis, bit):
    return lax.ppermute(x, axis, [(i, i ^ 1 << bit) for i in range(lax.axis_size(axis))])


def any_tiles(amplitudes, cholesky, energy_first, energy_second, energy_virtual):
    pair_count, virtual_count, local_virtual = amplitudes.shape
    tiles_count = lax.axis_size("virt")
    first_count = max(pair_count // OCC, 1)
    second_count = pair_count // first_count
    offset = lax.axis_index("pair") * pair_count
    first_start = offset // OCC
    second_start = offset % OCC
    column_start = lax.axis_index("virt") * local_virtual
    blocks = amplitudes.reshape(pair_count, tiles_count, local_virtual, local_virtual)
    arrived = lax.all_to_all(blocks, "virt", split_axis=1, concat_axis=1, tiled=True)
    mirrored = jnp.swapaxes(arrived, 2, 3).reshape(pair_count, virtual_count, local_virtual)
    combined = (2.0 * amplitudes.astype(F32) - mirrored.astype(F32)).astype(BF16)
    combined = combined.reshape(first_count, second_count, virtual_count, local_virtual)
    vectors = lax.all_gather(cholesky, "pair", axis=2, tiled=True)
    chosen = lax.dynamic_slice_in_dim(vectors, second_start, second_count, 0)
    partial_value = jnp.einsum("ilad,ldq->iaq", combined, chosen, preferred_element_type=F32)
    collected = lax.psum(partial_value.astype(BF16), "virt").astype(F32)
    for bit in range((OCC // second_count).bit_length() - 1):
        collected = collected + from_partner(collected.astype(BF16), "pair", bit).astype(F32)
    reduced = collected.astype(BF16)
    cycle_term = jnp.einsum("iaq,lbq->ilab", reduced, chosen, preferred_element_type=F32)
    first_energy = lax.dynamic_slice_in_dim(energy_first, first_start, first_count, 0)
    second_energy = lax.dynamic_slice_in_dim(energy_second, second_start, second_count, 0)
    column_energy = lax.dynamic_slice_in_dim(energy_virtual, column_start, local_virtual, 0)
    virtual_pairs = energy_virtual[:, None] + column_energy[None, :]
    diagonal = (
        virtual_pairs[None, None, :, :]
        - first_energy[:, None, None, None]
        - second_energy[None, :, None, None]
    )
    values = amplitudes.reshape(first_count, second_count, virtual_count, local_virtual)
    result = diagonal * values.astype(F32) + cycle_term
    return result.reshape(pair_count, virtual_count, local_virtual).astype(BF16)


def on_device(amplitudes, *others):
    ring = lax.axis_size("pair") * amplitudes.shape[0] // OCC
    fits = lax.axis_size("virt") == 2 and amplitudes.shape[0] * 2 == OCC and ring == 8
    return (two_tiles if fits else any_tiles)(amplitudes, *others)


def solution(mesh):
    return jax.shard_map(
        on_device,
        mesh=mesh,
        in_specs=(P("pair", None, "virt"), P(None, "virt", "pair"), P(), P(), P()),
        out_specs=P("pair", None, "virt"),
        check_vma=False,
    )
```

```python
import functools

import jax
import jax.numpy as jnp
from jax import lax
from jax.experimental import pallas as pl
from jax.experimental.pallas import tpu as pltpu
from jax.sharding import PartitionSpec as P

OCC = 8
BF16, F32 = jnp.bfloat16, jnp.float32
VMEM_LIMIT = 20 * 2**20
WORK = pl.CostEstimate(flops=1, bytes_accessed=1, transcendentals=0)
RING = 20
WHOLE = pl.BlockSpec(memory_space=pltpu.VMEM)
ANYWHERE = pl.BlockSpec(memory_space=pl.ANY)


def kernel_call(
    body, name, grid, in_specs, out_specs, out_shapes, scratch=(), tile=None, after=(), far=(), out=pltpu.VMEM
):
    scalars = 0 if tile is None else 1
    extra = len(after)

    def kernel(*refs):
        keep = scalars + len(in_specs)
        body(*refs[:keep], *refs[keep + extra :])

    def call(*args):
        held = [
            a if n in far else pltpu.with_memory_space_constraint(a, pltpu.VMEM)
            for n, a in enumerate((*args, *after))
        ]
        return pl.pallas_call(
            kernel,
            grid_spec=pltpu.PrefetchScalarGridSpec(
                num_scalar_prefetch=scalars,
                grid=grid,
                in_specs=[*in_specs, *[ANYWHERE] * extra],
                out_specs=list(out_specs),
                scratch_shapes=list(scratch),
            ),
            out_shape=[out(shape, kind) for shape, kind in out_shapes],
            compiler_params=pltpu.CompilerParams(
                dimension_semantics=("arbitrary",) * len(grid), vmem_limit_bytes=VMEM_LIMIT
            ),
            cost_estimate=WORK,
            name=name,
        )(*([] if tile is None else [tile]), *held)

    return call


def swap(x, axis, bit):
    return lax.ppermute(x, axis, [(i, i ^ 1 << bit) for i in range(lax.axis_size(axis))])


def ring_of(count, groups):
    places = count // groups
    return list(range(0, places, 2)) + list(range(places - 1, 0, -2))


def along_ring(x, step, groups):
    order = ring_of(lax.axis_size("pair"), groups)
    pairs = [
        (a * groups + g, order[(n + step) % len(order)] * groups + g)
        for n, a in enumerate(order)
        for g in range(groups)
    ]
    return lax.ppermute(x, "pair", pairs)


def turn_kernel(where, own, other, near, far):
    x = own[0].astype(F32)
    near[0] = (2.0 * x.T - x).astype(BF16)
    far[0] = other[0].T


def turn(where, amplitudes, part, count, after=()):
    _, rows, width = amplitudes.shape
    block = (1, width, width)
    return kernel_call(
        turn_kernel,
        "turn",
        (count,),
        [
            pl.BlockSpec(block, lambda j, t: (j + part * count, t[0], 0)),
            pl.BlockSpec(block, lambda j, t: (j + part * count, 1 - t[0], 0)),
        ],
        [pl.BlockSpec(block, lambda j, t: (j, 0, 0))] * 2,
        [((count, width, width), BF16)] * 2,
        tile=where,
        after=after,
        far=(0, 1),
    )(amplitudes, amplitudes)


def mix_kernel(parts, *refs):
    far, arrived, out = refs[:parts], refs[parts:-1], refs[-1]
    for j, f in enumerate(far):
        start = 0
        for r in arrived:
            rows = pl.ds(start, r.shape[1])
            out[j, rows] = (2.0 * f[0, rows].astype(F32) - r[j].astype(F32)).astype(BF16)
            start += r.shape[1]


def mix(far, arrived, after=()):
    shape = (len(far),) + far[0].shape[1:]
    (out,) = kernel_call(
        functools.partial(mix_kernel, len(far)),
        "mix",
        (1,),
        [WHOLE] * (len(far) + len(arrived)),
        [WHOLE],
        [(shape, BF16)],
        after=after,
    )(*far, *arrived)
    return out


def partial_kernel(shards, parts, joined, where, *refs):
    same, cross = refs[:shards], refs[shards : 2 * shards]
    refs = refs[2 * shards :]
    arrays = sum(parts)
    mine, theirs, refs = refs[:arrays], refs[arrays : 2 * arrays], refs[2 * arrays :]
    out, total = refs[0], refs[-1]
    j = pl.program_id(0)
    left = jnp.concatenate([r[0] for r in same], axis=0)
    right = jnp.concatenate([r[0] for r in cross], axis=0)
    if joined:
        refs[1][0] = left
        refs[2][0] = right
    at = 0
    for h, split in enumerate(parts):
        for part in range(split):

            @pl.when(j // (pl.num_programs(0) // split) == part)
            def _():
                value = jnp.dot(left, mine[at + part][0], preferred_element_type=F32)
                value += jnp.dot(right, theirs[at + part][0], preferred_element_type=F32)
                before = jnp.where(j == 0, 0.0, total[h])
                total[h] = value + before

        at += split

    @pl.when(j == pl.num_programs(0) - 1)
    def _():
        out[...] = total[...].astype(BF16)


def partial(where, same, cross, mine, theirs, joined=False, after=()):
    mine = [m if isinstance(m, list) else [m] for m in mine]
    theirs = [m if isinstance(m, list) else [m] for m in theirs]
    parts = [len(m) for m in mine]
    shards, halves = len(same), len(mine)
    count = sum(m.shape[0] for m in mine[0])
    width, columns = mine[0][0].shape[1:]
    depths = [v.shape[1] for v in same]
    rows = sum(depths)
    by_j = lambda n, m: pl.BlockSpec((1, n, m), lambda j, t: (j, 0, 0))

    def shard_spec(v, other):
        if v.shape[0] == count:
            return by_j(v.shape[1], width)
        if other:
            return pl.BlockSpec((1, v.shape[1], width), lambda j, t: (j + count * (1 - t[1]), 0, 0))
        return pl.BlockSpec((1, v.shape[1], width), lambda j, t: (j + count * t[1], 0, 0))

    def half_spec(part, split):
        block = count // split
        return pl.BlockSpec(
            (1, width, columns),
            lambda j, t: (jnp.clip(j - part * block, 0, block - 1), 0, 0),
        )

    out_shapes = [((halves, rows, columns), BF16)]
    out_specs = [pl.BlockSpec((halves, rows, columns), lambda j, t: (0, 0, 0))]
    if joined:
        out_shapes += [((count, rows, width), BF16)] * 2
        out_specs += [by_j(rows, width)] * 2
    return kernel_call(
        functools.partial(partial_kernel, shards, parts, joined),
        "partial",
        (count,),
        [shard_spec(v, False) for v in same]
        + [shard_spec(v, True) for v in cross]
        + [half_spec(part, split) for split in parts * 2 for part in range(split)],
        out_specs,
        out_shapes,
        [pltpu.VMEM((halves, rows, columns), F32)],
        tile=where,
        after=after,
    )(*same, *cross, *sum(mine, []), *sum(theirs, []))


def pick_kernel(where, forth, back, same, cross):
    same[...] = forth[...]
    cross[...] = back[...]


def pick(where, forth, back, after=()):
    block = (forth.shape[0] // 2,) + forth.shape[1:]
    return kernel_call(
        pick_kernel,
        "pick",
        (1,),
        [
            pl.BlockSpec(block, lambda k, t: (t[1], 0, 0)),
            pl.BlockSpec(block, lambda k, t: (1 - t[1], 0, 0)),
        ],
        [pl.BlockSpec(block, lambda k, t: (0, 0, 0))] * 2,
        [(block, BF16)] * 2,
        tile=where,
        after=after,
    )(forth, back)


def nothing(*refs):
    pass


def wall(*arrays, cost=0.1):
    held = [pltpu.with_memory_space_constraint(a, pltpu.VMEM) for a in arrays]
    return pl.pallas_call(
        nothing,
        in_specs=[ANYWHERE] * len(held),
        out_specs=ANYWHERE,
        out_shape=pltpu.VMEM((8, 128), F32),
        compiler_params=pltpu.CompilerParams(vmem_limit_bytes=2**20),
        cost_estimate=pl.CostEstimate(flops=int(cost * 10**9), bytes_accessed=1, transcendentals=0),
        name="wall",
    )(*held)


def gate(value, after):
    held = [pltpu.with_memory_space_constraint(a, pltpu.VMEM) for a in (value, *after)]
    return pl.pallas_call(
        nothing,
        in_specs=[ANYWHERE] * len(held),
        out_specs=ANYWHERE,
        out_shape=pltpu.VMEM(value.shape, value.dtype),
        input_output_aliases={0: 0},
        compiler_params=pltpu.CompilerParams(vmem_limit_bytes=2**20),
        cost_estimate=WORK,
        name="gate",
    )(*held)


def join(near, near_sent, far, far_sent, after=()):
    arrays = [v for v, _ in near + far_sent + far + near_sent]
    rows, columns = sum(v.shape[1] for v, _ in near), near[0][0].shape[2]
    n, f, fs = len(near), len(far), len(far_sent)

    def body(*refs):
        at = lambda first, items: [(refs[first + k], h) for k, (_, h) in enumerate(items)]
        own_near, got_far = at(0, near), at(n, far_sent)
        own_far, got_near = at(n + fs, far), at(n + fs + f, near_sent)
        out = refs[-1]
        for h, own, got in ((0, own_near, got_far), (1, own_far, got_near)):
            left = jnp.concatenate([r[k] for r, k in own], axis=0)
            right = jnp.concatenate([r[k] for r, k in got], axis=0)
            out[h] = (left.astype(F32) + right.astype(F32)).astype(BF16)

    whole = lambda shape: pl.BlockSpec(shape, lambda k: (0, 0, 0))
    (out,) = kernel_call(
        body,
        "join",
        (1,),
        [whole(v.shape) for v in arrays],
        [whole((2, rows, columns))],
        [((2, rows, columns), BF16)],
        after=after,
    )(*arrays)
    return out


def residual_kernel(chunks, shards, first, where, *refs):
    middles, vectors = refs[:chunks], refs[chunks : chunks + shards]
    rest, out, turned = refs[chunks + shards : -2], refs[-2], refs[-1]
    j = pl.program_id(0)
    columns = middles[0].shape[2]

    @pl.when(j == 0)
    def _():
        for h in range(2):
            rows = pl.ds(pl.multiple_of(lax.rem(where[0] + h, 2) * columns, columns), columns)
            turned[rows] = jnp.concatenate([m[h] for m in middles], axis=0).T

    if first:
        values, row_energy, column_energy, first_energy, second_energy = rest
        own = first_energy[where[2]] + second_energy[where[1] * pl.num_programs(0) + j]
        rows = jnp.broadcast_to(row_energy[...] - own, (128, row_energy.shape[1])).T[:, :1]
        total = (rows + column_energy[0]) * values[0].astype(F32)
    else:
        total = rest[0][j]
    right = jnp.concatenate([v[j] for v in vectors], axis=0)
    total += jnp.dot(turned[...], right, preferred_element_type=F32)
    out[0] = total.astype(out.dtype)


def residual(where, middles, vectors, first=None, before=None, last=True, after=()):
    count, _, width = vectors[0].shape
    rows = 2 * middles[0].shape[2]
    depth = sum(m.shape[1] for m in middles)
    by_j = pl.BlockSpec((1, rows, width), lambda j, t: (j, 0, 0))
    in_specs = [WHOLE] * (len(middles) + len(vectors))
    args = [*middles, *vectors]
    if first is not None:
        in_specs += [
            by_j,
            pl.BlockSpec((1, rows), lambda j, t: (0, 0)),
            pl.BlockSpec((1, 1, width), lambda j, t: (t[0], 0, 0)),
            pl.BlockSpec(memory_space=pltpu.SMEM),
            pl.BlockSpec(memory_space=pltpu.SMEM),
        ]
        args += first
    else:
        in_specs += [WHOLE]
        args += [before]
    (out,) = kernel_call(
        functools.partial(residual_kernel, len(middles), len(vectors), first is not None),
        "residual",
        (count,),
        in_specs,
        [by_j],
        [((count, rows, width), BF16 if last else F32)],
        [pltpu.VMEM((rows, depth), BF16)],
        tile=where,
        after=after,
        far=range(len(middles) + len(vectors), len(args)) if first is not None else (),
        out=pltpu.HBM if last else pltpu.VMEM,
    )(*args)
    return out


def two_tiles(amplitudes, cholesky, energy_first, energy_second, energy_virtual):
    count, virtual, width = amplitudes.shape
    groups = OCC // count
    places = lax.axis_size("pair") // groups
    place, group = lax.axis_index("pair") // groups, lax.axis_index("pair") % groups
    y = lax.axis_index("virt")
    where = jnp.stack([y, group, place]).astype(jnp.int32)
    ring = functools.partial(along_ring, groups=groups)
    to_core = functools.partial(swap, axis="pair", bit=0)
    to_tile = functools.partial(swap, axis="virt", bit=0)

    vectors = [jnp.swapaxes(cholesky, 1, 2)]
    forth, back = vectors[0], vectors[0]
    for step in range(1, places // 2):
        forth, back = ring(forth, 1), ring(back, -1)
        vectors += [forth, back]

    cut = width * 7 // 16 // 16 * 16
    sent, start = [], 0
    for rows in (cut, cut, width - 2 * cut):
        at = (0, (1 - y) * width + start, 0)
        sent.append(lax.dynamic_slice(amplitudes, at, (count, rows, width)))
        start += rows
    arrived = [to_tile(v) for v in sent]
    diagonal = [
        amplitudes,
        energy_virtual.reshape(1, virtual),
        energy_virtual.reshape(2, 1, width),
        energy_first,
        energy_second,
    ]
    near, near_theirs, far_turned = [], [], []
    held = []
    for j in range(count):
        v, w = turn(where, amplitudes, j, 1, after=held)
        near.append(v)
        far_turned.append(w)
        near_theirs.append(to_core(v))
        if j == count // 2 - 1:
            wall_1 = wall(*vectors[1:3], arrived[0], *near_theirs, cost=RING)
            held = [wall_1]
    wall_2 = wall(*vectors[3:5], arrived[1], *near_theirs[count // 2 :], cost=RING)
    near, near_theirs = [near], [near_theirs]
    n_1, same_1, cross_1 = partial(
        where, vectors[:3], vectors[:3], near, near_theirs, joined=True, after=[wall_2]
    )
    n_1_sent = to_tile(n_1)
    far = mix(far_turned, arrived, after=[n_1])
    far_theirs = to_core(far)
    n_2, same_2, cross_2 = partial(
        where, vectors[3:5], vectors[3:5], near, near_theirs, joined=True, after=[far]
    )
    n_2_sent = to_tile(n_2)
    (f_1,) = partial(where, [same_1], [cross_1], [far], [far_theirs], after=[n_2])
    f_1_sent = to_tile(f_1)
    handed_1, handed_2 = to_core(cross_1), to_core(cross_2)
    (f_2,) = partial(where, [same_2], [cross_2], [far], [far_theirs], after=[f_1, n_1_sent])
    f_2_sent = to_tile(f_2)
    picked = pick(where, *vectors[5:7], after=[f_2])
    same_c, cross_c = ring(picked[0], 1), ring(picked[1], -1)
    wall_3 = wall(*picked, handed_1, cost=RING)
    halves, halves_theirs = near + [far], near_theirs + [far_theirs]
    p_b, same_b, cross_b = partial(
        where, vectors[5:7], vectors[5:7], halves, halves_theirs, joined=True, after=[wall_3]
    )
    p_b_sent = to_tile(p_b)
    handed_b = to_core(cross_b)
    m_a = join(
        [(n_1, 0), (n_2, 0)],
        [(n_1_sent, 0), (n_2_sent, 0)],
        [(f_1, 0), (f_2, 0)],
        [(f_1_sent, 0), (f_2_sent, 0)],
        after=[p_b, handed_2],
    )
    m_a_theirs = to_core(m_a)
    wall_4 = wall(same_c, cross_c, m_a, cost=RING)
    (p_c,) = partial(where, [same_c], [cross_c], halves, halves_theirs, after=[wall_4])
    p_c_sent = to_tile(p_c)
    handed_c = to_core(cross_c)
    m_b = join([(p_b, 0)], [(p_b_sent, 0)], [(p_b, 1)], [(p_b_sent, 1)], after=[p_c])
    m_b_theirs = to_core(m_b)
    started = residual(
        where,
        [m_a, m_a_theirs],
        [same_1, same_2, handed_1, handed_2],
        first=diagonal,
        last=False,
        after=[m_b],
    )
    m_c = join([(p_c, 0)], [(p_c_sent, 0)], [(p_c, 1)], [(p_c_sent, 1)], after=[started])
    m_c_theirs = to_core(m_c)
    return residual(
        where,
        [m_b, m_b_theirs, m_c, m_c_theirs],
        [same_b, handed_b, same_c, handed_c],
        before=started,
    )


def from_partner(x, axis, bit):
    return lax.ppermute(x, axis, [(i, i ^ 1 << bit) for i in range(lax.axis_size(axis))])


def any_tiles(amplitudes, cholesky, energy_first, energy_second, energy_virtual):
    pair_count, virtual_count, local_virtual = amplitudes.shape
    tiles_count = lax.axis_size("virt")
    first_count = max(pair_count // OCC, 1)
    second_count = pair_count // first_count
    offset = lax.axis_index("pair") * pair_count
    first_start = offset // OCC
    second_start = offset % OCC
    column_start = lax.axis_index("virt") * local_virtual
    blocks = amplitudes.reshape(pair_count, tiles_count, local_virtual, local_virtual)
    arrived = lax.all_to_all(blocks, "virt", split_axis=1, concat_axis=1, tiled=True)
    mirrored = jnp.swapaxes(arrived, 2, 3).reshape(pair_count, virtual_count, local_virtual)
    combined = (2.0 * amplitudes.astype(F32) - mirrored.astype(F32)).astype(BF16)
    combined = combined.reshape(first_count, second_count, virtual_count, local_virtual)
    vectors = lax.all_gather(cholesky, "pair", axis=2, tiled=True)
    chosen = lax.dynamic_slice_in_dim(vectors, second_start, second_count, 0)
    partial_value = jnp.einsum("ilad,ldq->iaq", combined, chosen, preferred_element_type=F32)
    collected = lax.psum(partial_value.astype(BF16), "virt").astype(F32)
    for bit in range((OCC // second_count).bit_length() - 1):
        collected = collected + from_partner(collected.astype(BF16), "pair", bit).astype(F32)
    reduced = collected.astype(BF16)
    cycle_term = jnp.einsum("iaq,lbq->ilab", reduced, chosen, preferred_element_type=F32)
    first_energy = lax.dynamic_slice_in_dim(energy_first, first_start, first_count, 0)
    second_energy = lax.dynamic_slice_in_dim(energy_second, second_start, second_count, 0)
    column_energy = lax.dynamic_slice_in_dim(energy_virtual, column_start, local_virtual, 0)
    virtual_pairs = energy_virtual[:, None] + column_energy[None, :]
    diagonal = (
        virtual_pairs[None, None, :, :]
        - first_energy[:, None, None, None]
        - second_energy[None, :, None, None]
    )
    values = amplitudes.reshape(first_count, second_count, virtual_count, local_virtual)
    result = diagonal * values.astype(F32) + cycle_term
    return result.reshape(pair_count, virtual_count, local_virtual).astype(BF16)


def on_device(amplitudes, *others):
    ring = lax.axis_size("pair") * amplitudes.shape[0] // OCC
    fits = lax.axis_size("virt") == 2 and amplitudes.shape[0] * 2 == OCC and ring == 8
    return (two_tiles if fits else any_tiles)(amplitudes, *others)


def solution(mesh):
    return jax.shard_map(
        on_device,
        mesh=mesh,
        in_specs=(P("pair", None, "virt"), P(None, "virt", "pair"), P(), P(), P()),
        out_specs=P("pair", None, "virt"),
        check_vma=False,
    )
```

```python
import functools

import jax
import jax.numpy as jnp
from jax import lax
from jax.experimental import pallas as pl
from jax.experimental.pallas import tpu as pltpu
from jax.sharding import PartitionSpec as P

OCC = 8
BF16, F32 = jnp.bfloat16, jnp.float32
VMEM_LIMIT = 20 * 2**20
WORK = pl.CostEstimate(flops=1, bytes_accessed=1, transcendentals=0)
WALLS = (1, 1, 1, 6, 12)
WHOLE = pl.BlockSpec(memory_space=pltpu.VMEM)
ANYWHERE = pl.BlockSpec(memory_space=pl.ANY)


def kernel_call(
    body, name, grid, in_specs, out_specs, out_shapes, scratch=(), tile=None, after=(), far=(), out=pltpu.VMEM
):
    scalars = 0 if tile is None else 1
    extra = len(after)

    def kernel(*refs):
        keep = scalars + len(in_specs)
        body(*refs[:keep], *refs[keep + extra :])

    def call(*args):
        held = [
            pltpu.with_memory_space_constraint(a, pltpu.HBM if n in far else pltpu.VMEM)
            for n, a in enumerate((*args, *after))
        ]
        return pl.pallas_call(
            kernel,
            grid_spec=pltpu.PrefetchScalarGridSpec(
                num_scalar_prefetch=scalars,
                grid=grid,
                in_specs=[*in_specs, *[ANYWHERE] * extra],
                out_specs=list(out_specs),
                scratch_shapes=list(scratch),
            ),
            out_shape=[out(shape, kind) for shape, kind in out_shapes],
            compiler_params=pltpu.CompilerParams(
                dimension_semantics=("arbitrary",) * len(grid), vmem_limit_bytes=VMEM_LIMIT
            ),
            cost_estimate=WORK,
            name=name,
        )(*([] if tile is None else [tile]), *held)

    return call


def swap(x, axis, bit):
    return lax.ppermute(x, axis, [(i, i ^ 1 << bit) for i in range(lax.axis_size(axis))])


def ring_of(count, groups):
    places = count // groups
    return list(range(0, places, 2)) + list(range(places - 1, 0, -2))


def along_ring(x, step, groups):
    order = ring_of(lax.axis_size("pair"), groups)
    pairs = [
        (a * groups + g, order[(n + step) % len(order)] * groups + g)
        for n, a in enumerate(order)
        for g in range(groups)
    ]
    return lax.ppermute(x, "pair", pairs)


def turn_kernel(where, own, own_rows, other, near, far):
    near[0] = (2.0 * own[0].astype(F32).T - own_rows[0].astype(F32)).astype(BF16)
    far[0] = other[0].T


def turn(where, amplitudes, part, parts, after=()):
    count, _, width = amplitudes.shape
    rows = width // parts
    block = (1, width, rows)
    out = pl.BlockSpec((1, rows, width), lambda j, t: (j, 0, 0))
    return kernel_call(
        turn_kernel,
        "turn",
        (count,),
        [
            pl.BlockSpec(block, lambda j, t: (j, t[0], part)),
            pl.BlockSpec((1, rows, width), lambda j, t: (j, t[0] * parts + part, 0)),
            pl.BlockSpec(block, lambda j, t: (j, 1 - t[0], part)),
        ],
        [out] * 2,
        [((count, rows, width), BF16)] * 2,
        tile=where,
        after=after,
        far=(0, 1, 2),
    )(amplitudes, amplitudes, amplitudes)


def cut_kernel(starts, where, *refs):
    outs, done = refs[-1 - len(starts) : -1], refs[-1]
    copies = []
    for n, (start, out) in enumerate(zip(starts, outs)):
        at = pl.multiple_of((1 - where[0]) * out.shape[2] + start, 16)
        source = refs[0].at[:, pl.ds(at, out.shape[1]), :]
        copies.append(pltpu.make_async_copy(source, out, done.at[n]))
    for copy in copies:
        copy.start()
    for copy in copies:
        copy.wait()


def cut(where, amplitudes, pieces, after=()):
    count, _, width = amplitudes.shape
    return kernel_call(
        functools.partial(cut_kernel, [start for start, _ in pieces]),
        "cut",
        (1,),
        [ANYWHERE],
        [WHOLE] * len(pieces),
        [((count, rows, width), BF16) for _, rows in pieces],
        [pltpu.SemaphoreType.DMA((len(pieces),))],
        tile=where,
        after=after,
        far=(0,),
    )(amplitudes)


def mix_kernel(parts, start, *refs):
    far, arrived, out = refs[:parts], refs[parts:-1], refs[-1]
    step = far[0].shape[1]
    first = 0
    for r in arrived:
        rows = r.shape[1]
        while rows:
            part, at = divmod(start + first, step)
            here = min(rows, step - at)
            came = r.shape[1] - rows
            value = 2.0 * far[part][:, at : at + here].astype(F32)
            value -= r[:, came : came + here].astype(F32)
            out[:, first : first + here] = value.astype(BF16)
            first, rows = first + here, rows - here


def mix(far, arrived, start, after=()):
    count, _, width = far[0].shape
    shape = (count, sum(r.shape[1] for r in arrived), width)
    (out,) = kernel_call(
        functools.partial(mix_kernel, len(far), start),
        "mix",
        (1,),
        [WHOLE] * (len(far) + len(arrived)),
        [WHOLE],
        [(shape, BF16)],
        after=after,
    )(*far, *arrived)
    return out


def partial_kernel(shards, parts, joined, extras, where, *refs):
    same, cross = refs[:shards], refs[shards : 2 * shards]
    refs = refs[2 * shards :]
    arrays = sum(parts)
    mine, theirs, refs = refs[:arrays], refs[arrays : 2 * arrays], refs[2 * arrays :]
    extra_refs, refs = refs[:extras], refs[extras:]
    out, total = refs[0], refs[-1]
    j = pl.program_id(0)
    left = jnp.concatenate([r[0] for r in same], axis=0)
    right = jnp.concatenate([r[0] for r in cross], axis=0)
    extra = list(extra_refs)
    for n in range(joined):
        before = [extra.pop(0)[0]] if extra_refs else []
        refs[1 + n][0] = jnp.concatenate([*before, (left, right)[n - joined]], axis=0)
    first = j == 0
    at = 0
    for h, split in enumerate(parts):
        whole = [jnp.concatenate([r[0] for r in v[at : at + split]], axis=0) for v in (mine, theirs)]
        value = jnp.dot(left, whole[0], preferred_element_type=F32)
        value += jnp.dot(right, whole[1], preferred_element_type=F32)
        total[h] = value + jnp.where(first, 0.0, total[h])
        at += split

    @pl.when(j == pl.num_programs(0) - 1)
    def _():
        out[...] = total[...].astype(BF16)


def partial(where, same, cross, mine, theirs, joined=0, behind=(), after=()):
    parts = [len(m) for m in mine]
    shards, halves = len(same), len(mine)
    count, _, columns = mine[0][0].shape
    width = same[0].shape[2]
    depths = [v.shape[1] for v in same]
    rows = sum(depths)
    by_j = lambda n, m: pl.BlockSpec((1, n, m), lambda j, t: (j, 0, 0))

    def shard_spec(v, other):
        if v.shape[0] == count:
            return by_j(v.shape[1], width)
        if other:
            return pl.BlockSpec((1, v.shape[1], width), lambda j, t: (j + count * (1 - t[1]), 0, 0))
        return pl.BlockSpec((1, v.shape[1], width), lambda j, t: (j + count * t[1], 0, 0))

    out_shapes = [((halves, rows, columns), BF16)]
    out_specs = [pl.BlockSpec((halves, rows, columns), lambda j, t: (0, 0, 0))]
    for n in range(joined):
        more = rows + (behind[n].shape[1] if behind else 0)
        out_shapes.append(((count, more, width), BF16))
        out_specs.append(by_j(more, width))
    return kernel_call(
        functools.partial(partial_kernel, shards, parts, joined, len(behind)),
        "partial",
        (count,),
        [shard_spec(v, False) for v in same]
        + [shard_spec(v, True) for v in cross]
        + [by_j(m.shape[1], columns) for v in (mine, theirs) for m in sum(v, [])]
        + [by_j(v.shape[1], width) for v in behind],
        out_specs,
        out_shapes,
        [pltpu.VMEM((halves, rows, columns), F32)],
        tile=where,
        after=after,
    )(*same, *cross, *sum(mine, []), *sum(theirs, []), *behind)


def pick_kernel(where, forth, back, same, cross):
    same[...] = forth[...]
    cross[...] = back[...]


def pick(where, forth, back, after=()):
    block = (forth.shape[0] // 2,) + forth.shape[1:]
    return kernel_call(
        pick_kernel,
        "pick",
        (1,),
        [
            pl.BlockSpec(block, lambda k, t: (t[1], 0, 0)),
            pl.BlockSpec(block, lambda k, t: (1 - t[1], 0, 0)),
        ],
        [pl.BlockSpec(block, lambda k, t: (0, 0, 0))] * 2,
        [(block, BF16)] * 2,
        tile=where,
        after=after,
    )(forth, back)


def nothing(*refs):
    pass


def wall(*arrays, cost=0.1):
    held = [pltpu.with_memory_space_constraint(a, pltpu.VMEM) for a in arrays]
    return pl.pallas_call(
        nothing,
        in_specs=[ANYWHERE] * len(held),
        out_specs=ANYWHERE,
        out_shape=pltpu.VMEM((8, 128), F32),
        compiler_params=pltpu.CompilerParams(vmem_limit_bytes=2**20),
        cost_estimate=pl.CostEstimate(flops=int(cost * 10**9), bytes_accessed=1, transcendentals=0),
        name="wall",
    )(*held)


def gate(value, after):
    held = [pltpu.with_memory_space_constraint(a, pltpu.VMEM) for a in (value, *after)]
    return pl.pallas_call(
        nothing,
        in_specs=[ANYWHERE] * len(held),
        out_specs=ANYWHERE,
        out_shape=pltpu.VMEM(value.shape, value.dtype),
        input_output_aliases={0: 0},
        compiler_params=pltpu.CompilerParams(vmem_limit_bytes=2**20),
        cost_estimate=WORK,
        name="gate",
    )(*held)


def join(near, near_sent, far, far_sent, after=()):
    arrays = [v for v, _ in near + far_sent + far + near_sent]
    rows, columns = sum(v.shape[1] for v, _ in near), near[0][0].shape[2]
    n, f, fs = len(near), len(far), len(far_sent)

    def body(*refs):
        at = lambda first, items: [(refs[first + k], h) for k, (_, h) in enumerate(items)]
        own_near, got_far = at(0, near), at(n, far_sent)
        own_far, got_near = at(n + fs, far), at(n + fs + f, near_sent)
        out = refs[-1]
        for h, own, got in ((0, own_near, got_far), (1, own_far, got_near)):
            left = jnp.concatenate([r[k] for r, k in own], axis=0)
            right = jnp.concatenate([r[k] for r, k in got], axis=0)
            out[h] = (left.astype(F32) + right.astype(F32)).astype(BF16)

    whole = lambda shape: pl.BlockSpec(shape, lambda k: (0, 0, 0))
    (out,) = kernel_call(
        body,
        "join",
        (1,),
        [whole(v.shape) for v in arrays],
        [whole((2, rows, columns))],
        [((2, rows, columns), BF16)],
        after=after,
    )(*arrays)
    return out


def residual_kernel(chunks, shards, first, where, *refs):
    middles, vectors = refs[:chunks], refs[chunks : chunks + shards]
    rest, out, turned = refs[chunks + shards : -2], refs[-2], refs[-1]
    j = pl.program_id(0)
    columns = middles[0].shape[2]

    @pl.when(j == 0)
    def _():
        for h in range(2):
            rows = pl.ds(pl.multiple_of(lax.rem(where[0] + h, 2) * columns, columns), columns)
            turned[rows] = jnp.concatenate([m[h] for m in middles], axis=0).T

    if first:
        values, row_energy, column_energy, first_energy, second_energy = rest
        own = first_energy[where[2]] + second_energy[where[1] * pl.num_programs(0) + j]
        rows = jnp.broadcast_to(row_energy[...] - own, (128, row_energy.shape[1])).T[:, :1]
        total = (rows + column_energy[0]) * values[0].astype(F32)
    else:
        total = rest[0][j]
    right = jnp.concatenate([v[j] for v in vectors], axis=0)
    total += jnp.dot(turned[...], right, preferred_element_type=F32)
    out[0] = total.astype(out.dtype)


def residual(where, middles, vectors, first=None, before=None, last=True, after=()):
    count, _, width = vectors[0].shape
    rows = 2 * middles[0].shape[2]
    depth = sum(m.shape[1] for m in middles)
    by_j = pl.BlockSpec((1, rows, width), lambda j, t: (j, 0, 0))
    in_specs = [WHOLE] * (len(middles) + len(vectors))
    args = [*middles, *vectors]
    if first is not None:
        in_specs += [
            by_j,
            pl.BlockSpec((1, rows), lambda j, t: (0, 0)),
            pl.BlockSpec((1, 1, width), lambda j, t: (t[0], 0, 0)),
            pl.BlockSpec(memory_space=pltpu.SMEM),
            pl.BlockSpec(memory_space=pltpu.SMEM),
        ]
        args += first
    else:
        in_specs += [WHOLE]
        args += [before]
    (out,) = kernel_call(
        functools.partial(residual_kernel, len(middles), len(vectors), first is not None),
        "residual",
        (count,),
        in_specs,
        [by_j],
        [((count, rows, width), BF16 if last else F32)],
        [pltpu.VMEM((rows, depth), BF16)],
        tile=where,
        after=after,
        far=range(len(middles) + len(vectors), len(args)) if first is not None else (),
        out=pltpu.HBM if last else pltpu.VMEM,
    )(*args)
    return out


def two_tiles(amplitudes, cholesky, energy_first, energy_second, energy_virtual):
    count, virtual, width = amplitudes.shape
    groups = OCC // count
    places = lax.axis_size("pair") // groups
    place, group = lax.axis_index("pair") // groups, lax.axis_index("pair") % groups
    y = lax.axis_index("virt")
    where = jnp.stack([y, group, place]).astype(jnp.int32)
    ring = functools.partial(along_ring, groups=groups)
    to_core = functools.partial(swap, axis="pair", bit=0)
    to_tile = functools.partial(swap, axis="virt", bit=0)

    unit = width // 32
    pieces = [(0, 15 * unit), (15 * unit, 13 * unit), (28 * unit, 4 * unit)]
    sent = cut(where, amplitudes, pieces[:1])
    sent += cut(where, amplitudes, pieces[1:], after=sent)
    arrived = [to_tile(v) for v in sent]

    own = jnp.swapaxes(cholesky, 1, 2)
    vectors = [own]
    forth, back = own, own
    for step in range(1, places // 2):
        forth, back = ring(forth, 1), ring(back, -1)
        vectors += [forth, back]

    diagonal = [
        amplitudes,
        energy_virtual.reshape(1, virtual),
        energy_virtual.reshape(2, 1, width),
        energy_first,
        energy_second,
    ]
    near, near_theirs, far_turned = [], [], []
    held = sent[1:]
    parts = 4
    for part in range(parts):
        v, w = turn(where, amplitudes, part, parts, after=held)
        near.append(v)
        far_turned.append(w)
        near_theirs.append(to_core(v))
        if part == parts // 2 - 1:
            wall_1 = wall(*vectors[1:3], arrived[0], *near_theirs, cost=WALLS[0])
            held = [wall_1]
    wall_2 = wall(*vectors[3:5], arrived[1], *near_theirs[parts // 2 :], cost=WALLS[1])
    far_0 = mix(far_turned, arrived[:2], 0, after=[wall_2])
    far_0_theirs = to_core(far_0)
    near, near_theirs = [near], [near_theirs]
    n_a, same_a, cross_a = partial(
        where, vectors[:5], vectors[:5], near, near_theirs, joined=2, after=[far_0]
    )
    n_a_sent = to_tile(n_a)
    far_1 = mix(far_turned, arrived[2:], far_0.shape[1], after=[n_a])
    far_1_theirs = to_core(far_1)
    far, far_theirs = [far_0, far_1], [far_0_theirs, far_1_theirs]
    f_a, cross_a = partial(where, [same_a], [cross_a], [far], [far_theirs], joined=1)
    f_a_sent = to_tile(f_a)
    handed_a = to_core(cross_a)
    picked = pick(where, *vectors[5:7], after=[f_a, n_a_sent])
    same_c, cross_c = ring(picked[0], 1), ring(picked[1], -1)
    wall_3 = wall(*picked, cost=WALLS[2])
    halves, halves_theirs = near + [far], near_theirs + [far_theirs]
    p_b, same_b, cross_b = partial(
        where, vectors[5:7], vectors[5:7], halves, halves_theirs, joined=2, after=[wall_3]
    )
    p_b_sent = to_tile(p_b)
    m_a = join([(n_a, 0)], [(n_a_sent, 0)], [(f_a, 0)], [(f_a_sent, 0)], after=[p_b])
    m_a_theirs = to_core(m_a)
    wall_4 = wall(same_c, cross_c, m_a, cost=WALLS[3])
    p_c, same_d, cross_d = partial(
        where,
        [same_c],
        [cross_c],
        halves,
        halves_theirs,
        joined=2,
        behind=[same_b, cross_b],
        after=[wall_4],
    )
    p_c_sent = to_tile(p_c)
    handed_d = to_core(cross_d)
    wall_5 = wall(p_c, p_b_sent, cost=WALLS[4])
    started = residual(
        where,
        [m_a, m_a_theirs],
        [same_a, handed_a],
        first=diagonal,
        last=False,
        after=[wall_5],
    )
    m_d = join(
        [(p_b, 0), (p_c, 0)],
        [(p_b_sent, 0), (p_c_sent, 0)],
        [(p_b, 1), (p_c, 1)],
        [(p_b_sent, 1), (p_c_sent, 1)],
        after=[started],
    )
    m_d_theirs = to_core(m_d)
    return residual(where, [m_d, m_d_theirs], [same_d, handed_d], before=started)


def from_partner(x, axis, bit):
    return lax.ppermute(x, axis, [(i, i ^ 1 << bit) for i in range(lax.axis_size(axis))])


def any_tiles(amplitudes, cholesky, energy_first, energy_second, energy_virtual):
    pair_count, virtual_count, local_virtual = amplitudes.shape
    tiles_count = lax.axis_size("virt")
    first_count = max(pair_count // OCC, 1)
    second_count = pair_count // first_count
    offset = lax.axis_index("pair") * pair_count
    first_start = offset // OCC
    second_start = offset % OCC
    column_start = lax.axis_index("virt") * local_virtual
    blocks = amplitudes.reshape(pair_count, tiles_count, local_virtual, local_virtual)
    arrived = lax.all_to_all(blocks, "virt", split_axis=1, concat_axis=1, tiled=True)
    mirrored = jnp.swapaxes(arrived, 2, 3).reshape(pair_count, virtual_count, local_virtual)
    combined = (2.0 * amplitudes.astype(F32) - mirrored.astype(F32)).astype(BF16)
    combined = combined.reshape(first_count, second_count, virtual_count, local_virtual)
    vectors = lax.all_gather(cholesky, "pair", axis=2, tiled=True)
    chosen = lax.dynamic_slice_in_dim(vectors, second_start, second_count, 0)
    partial_value = jnp.einsum("ilad,ldq->iaq", combined, chosen, preferred_element_type=F32)
    collected = lax.psum(partial_value.astype(BF16), "virt").astype(F32)
    for bit in range((OCC // second_count).bit_length() - 1):
        collected = collected + from_partner(collected.astype(BF16), "pair", bit).astype(F32)
    reduced = collected.astype(BF16)
    cycle_term = jnp.einsum("iaq,lbq->ilab", reduced, chosen, preferred_element_type=F32)
    first_energy = lax.dynamic_slice_in_dim(energy_first, first_start, first_count, 0)
    second_energy = lax.dynamic_slice_in_dim(energy_second, second_start, second_count, 0)
    column_energy = lax.dynamic_slice_in_dim(energy_virtual, column_start, local_virtual, 0)
    virtual_pairs = energy_virtual[:, None] + column_energy[None, :]
    diagonal = (
        virtual_pairs[None, None, :, :]
        - first_energy[:, None, None, None]
        - second_energy[None, :, None, None]
    )
    values = amplitudes.reshape(first_count, second_count, virtual_count, local_virtual)
    result = diagonal * values.astype(F32) + cycle_term
    return result.reshape(pair_count, virtual_count, local_virtual).astype(BF16)


def on_device(amplitudes, *others):
    ring = lax.axis_size("pair") * amplitudes.shape[0] // OCC
    fits = lax.axis_size("virt") == 2 and amplitudes.shape[0] * 2 == OCC and ring == 8
    return (two_tiles if fits else any_tiles)(amplitudes, *others)


def solution(mesh):
    return jax.shard_map(
        on_device,
        mesh=mesh,
        in_specs=(P("pair", None, "virt"), P(None, "virt", "pair"), P(), P(), P()),
        out_specs=P("pair", None, "virt"),
        check_vma=False,
    )
```

```python
import functools

import jax
import jax.numpy as jnp
from jax import lax
from jax.experimental import pallas as pl
from jax.experimental.pallas import tpu as pltpu
from jax.sharding import PartitionSpec as P

OCC = 8
BF16, F32 = jnp.bfloat16, jnp.float32
VMEM_LIMIT = 20 * 2**20
WORK = pl.CostEstimate(flops=1, bytes_accessed=1, transcendentals=0)
WALLS = (1, 1, 1, 1, 16)
WHOLE = pl.BlockSpec(memory_space=pltpu.VMEM)
ANYWHERE = pl.BlockSpec(memory_space=pl.ANY)


def kernel_call(
    body, name, grid, in_specs, out_specs, out_shapes, scratch=(), tile=None, after=(), far=(), out=pltpu.VMEM
):
    scalars = 0 if tile is None else 1
    extra = len(after)

    def kernel(*refs):
        keep = scalars + len(in_specs)
        body(*refs[:keep], *refs[keep + extra :])

    def call(*args):
        held = [
            a if a.ndim == 1 else pltpu.with_memory_space_constraint(a, pltpu.HBM if n in far else pltpu.VMEM)
            for n, a in enumerate((*args, *after))
        ]
        return pl.pallas_call(
            kernel,
            grid_spec=pltpu.PrefetchScalarGridSpec(
                num_scalar_prefetch=scalars,
                grid=grid,
                in_specs=[*in_specs, *[ANYWHERE] * extra],
                out_specs=list(out_specs),
                scratch_shapes=list(scratch),
            ),
            out_shape=[out(shape, kind) for shape, kind in out_shapes],
            compiler_params=pltpu.CompilerParams(
                dimension_semantics=("arbitrary",) * len(grid), vmem_limit_bytes=VMEM_LIMIT
            ),
            cost_estimate=WORK,
            name=name,
        )(*([] if tile is None else [tile]), *held)

    return call


def swap(x, axis, bit):
    return lax.ppermute(x, axis, [(i, i ^ 1 << bit) for i in range(lax.axis_size(axis))])


def ring_of(count, groups):
    places = count // groups
    return list(range(0, places, 2)) + list(range(places - 1, 0, -2))


def along_ring(x, step, groups):
    order = ring_of(lax.axis_size("pair"), groups)
    pairs = [
        (a * groups + g, order[(n + step) % len(order)] * groups + g)
        for n, a in enumerate(order)
        for g in range(groups)
    ]
    return lax.ppermute(x, "pair", pairs)


def turn_kernel(where, own, own_rows, other, near, far):
    near[0] = (2.0 * own[0].astype(F32).T - own_rows[0].astype(F32)).astype(BF16)
    far[0] = other[0].T


def turn(where, amplitudes, part, parts, after=()):
    count, _, width = amplitudes.shape
    rows = width // parts
    block = (1, width, rows)
    out = pl.BlockSpec((1, rows, width), lambda j, t: (j, 0, 0))
    return kernel_call(
        turn_kernel,
        "turn",
        (count,),
        [
            pl.BlockSpec(block, lambda j, t: (j, t[0], part)),
            pl.BlockSpec((1, rows, width), lambda j, t: (j, t[0] * parts + part, 0)),
            pl.BlockSpec(block, lambda j, t: (j, 1 - t[0], part)),
        ],
        [out] * 2,
        [((count, rows, width), BF16)] * 2,
        tile=where,
        after=after,
        far=(0, 1, 2),
    )(amplitudes, amplitudes, amplitudes)


def cut_kernel(starts, where, *refs):
    outs, done = refs[-1 - len(starts) : -1], refs[-1]
    copies = []
    for n, (start, out) in enumerate(zip(starts, outs)):
        at = pl.multiple_of((1 - where[0]) * out.shape[2] + start, 16)
        source = refs[0].at[:, pl.ds(at, out.shape[1]), :]
        copies.append(pltpu.make_async_copy(source, out, done.at[n]))
    for copy in copies:
        copy.start()
    for copy in copies:
        copy.wait()


def cut(where, amplitudes, pieces, after=()):
    count, _, width = amplitudes.shape
    return kernel_call(
        functools.partial(cut_kernel, [start for start, _ in pieces]),
        "cut",
        (1,),
        [ANYWHERE],
        [WHOLE] * len(pieces),
        [((count, rows, width), BF16) for _, rows in pieces],
        [pltpu.SemaphoreType.DMA((len(pieces),))],
        tile=where,
        after=after,
        far=(0,),
    )(amplitudes)


def mix_kernel(parts, start, *refs):
    far, arrived, out = refs[:parts], refs[parts:-1], refs[-1]
    step = far[0].shape[1]
    first = 0
    for r in arrived:
        rows = r.shape[1]
        while rows:
            part, at = divmod(start + first, step)
            here = min(rows, step - at)
            came = r.shape[1] - rows
            value = 2.0 * far[part][:, at : at + here].astype(F32)
            value -= r[:, came : came + here].astype(F32)
            out[:, first : first + here] = value.astype(BF16)
            first, rows = first + here, rows - here


def mix(far, arrived, start, after=()):
    count, _, width = far[0].shape
    shape = (count, sum(r.shape[1] for r in arrived), width)
    (out,) = kernel_call(
        functools.partial(mix_kernel, len(far), start),
        "mix",
        (1,),
        [WHOLE] * (len(far) + len(arrived)),
        [WHOLE],
        [(shape, BF16)],
        after=after,
    )(*far, *arrived)
    return out


def partial_kernel(shards, parts, joined, extras, where, *refs):
    same, cross = refs[:shards], refs[shards : 2 * shards]
    refs = refs[2 * shards :]
    arrays = sum(parts)
    mine, theirs, refs = refs[:arrays], refs[arrays : 2 * arrays], refs[2 * arrays :]
    extra, outs = refs[:extras], refs[extras:]
    count = mine[0].shape[0]

    def together(arrays, j, group=0):
        pieces = [r[j + (group * count if r.shape[0] > count else 0)] for r in arrays]
        return jnp.concatenate(pieces, axis=0) if len(pieces) > 1 else pieces[0]

    totals = [None] * len(parts)
    for j in range(count):
        left, right = together(same, j, where[1]), together(cross, j, 1 - where[1])
        for n in range(joined):
            value = (left, right)[n - joined]
            outs[1 + n][j] = jnp.concatenate([extra[n][j], value], axis=0) if extras else value
        at = 0
        for h, split in enumerate(parts):
            for shard, half in ((left, mine), (right, theirs)):
                half = together(half[at : at + split], j)
                value = jnp.dot(shard, half, preferred_element_type=F32)
                totals[h] = value if totals[h] is None else totals[h] + value
            at += split
    for h, total in enumerate(totals):
        outs[0][h] = total.astype(BF16)


def partial(where, same, cross, mine, theirs, joined=0, behind=(), after=()):
    parts = [len(m) for m in mine]
    shards, halves = len(same), len(mine)
    count, _, columns = mine[0][0].shape
    width = same[0].shape[2]
    rows = sum(v.shape[1] for v in same)
    args = [*same, *cross, *sum(mine, []), *sum(theirs, []), *behind]
    out_shapes = [((halves, rows, columns), BF16)]
    for n in range(joined):
        more = rows + (behind[n].shape[1] if behind else 0)
        out_shapes.append(((count, more, width), BF16))
    return kernel_call(
        functools.partial(partial_kernel, shards, parts, joined, len(behind)),
        "partial",
        (1,),
        [WHOLE] * len(args),
        [WHOLE] * len(out_shapes),
        out_shapes,
        tile=where,
        after=after,
    )(*args)


def pick_kernel(where, forth, back, same, cross):
    same[...] = forth[...]
    cross[...] = back[...]


def pick(where, forth, back, after=()):
    block = (forth.shape[0] // 2,) + forth.shape[1:]
    return kernel_call(
        pick_kernel,
        "pick",
        (1,),
        [
            pl.BlockSpec(block, lambda k, t: (t[1], 0, 0)),
            pl.BlockSpec(block, lambda k, t: (1 - t[1], 0, 0)),
        ],
        [pl.BlockSpec(block, lambda k, t: (0, 0, 0))] * 2,
        [(block, BF16)] * 2,
        tile=where,
        after=after,
    )(forth, back)


def nothing(*refs):
    pass


def wall(*arrays, cost=0.1):
    held = [pltpu.with_memory_space_constraint(a, pltpu.VMEM) for a in arrays]
    return pl.pallas_call(
        nothing,
        in_specs=[ANYWHERE] * len(held),
        out_specs=ANYWHERE,
        out_shape=pltpu.VMEM((8, 128), F32),
        compiler_params=pltpu.CompilerParams(vmem_limit_bytes=2**20),
        cost_estimate=pl.CostEstimate(flops=int(cost * 10**9), bytes_accessed=1, transcendentals=0),
        name="wall",
    )(*held)


def gate(value, after):
    held = [pltpu.with_memory_space_constraint(a, pltpu.VMEM) for a in (value, *after)]
    return pl.pallas_call(
        nothing,
        in_specs=[ANYWHERE] * len(held),
        out_specs=ANYWHERE,
        out_shape=pltpu.VMEM(value.shape, value.dtype),
        input_output_aliases={0: 0},
        compiler_params=pltpu.CompilerParams(vmem_limit_bytes=2**20),
        cost_estimate=WORK,
        name="gate",
    )(*held)


def join_kernel(counts, *refs):
    out, at = refs[-1], 0
    for h, count in enumerate(counts):
        own, sent = refs[at : at + count], refs[at + count : at + 2 * count]
        at += 2 * count
        left, right = [
            jnp.concatenate([r[...] for r in v], axis=0) if count > 1 else v[0][...]
            for v in (own, sent)
        ]
        out[h] = (left.astype(F32) + right.astype(F32)).astype(BF16)


def join(*halves, after=()):
    args, in_specs = [], []
    for pairs in halves:
        for side in range(2):
            for pair in pairs:
                v, h = pair[side]
                args.append(v)
                in_specs.append(pl.BlockSpec((None,) + v.shape[1:], functools.partial(lambda h, k: (h, 0, 0), h)))
    rows = sum(pair[0][0].shape[1] for pair in halves[0])
    shape = (len(halves), rows, args[0].shape[2])
    (out,) = kernel_call(
        functools.partial(join_kernel, [len(pairs) for pairs in halves]),
        "join",
        (1,),
        in_specs,
        [WHOLE],
        [(shape, BF16)],
        after=after,
    )(*args)
    return out


def joined_rows(pieces):
    return jnp.concatenate(pieces, axis=0) if len(pieces) > 1 else pieces[0]


def diagonal_kernel(where, values, energy, first_energy, second_energy, own, off, held, done):
    count, columns, width = own.shape
    copies = []
    for h in range(2):
        tile = lax.rem(where[0] + h, 2)
        rows = pl.ds(pl.multiple_of(tile * columns, 16), columns)
        for j in range(count):
            copies.append(pltpu.make_async_copy(values.at[j, rows], held.at[h, j], done.at[h, j]))
            copies[-1].start()
    for h, out in enumerate((own, off)):
        row_energy = energy[lax.rem(where[0] + h, 2)]
        row_energy = jnp.broadcast_to(row_energy, (128, columns)).T[:, :1]
        for j in range(count):
            occupied = first_energy[where[2]] + second_energy[where[1] * count + j]
            copies[h * count + j].wait()
            out[j] = (row_energy - occupied + energy[where[0]]) * held[h, j].astype(F32)


def diagonal(where, amplitudes, energy_virtual, energy_first, energy_second, after=()):
    count, rows, width = amplitudes.shape
    block = (count, rows // 2, width)
    return kernel_call(
        diagonal_kernel,
        "diagonal",
        (1,),
        [ANYWHERE, WHOLE] + [pl.BlockSpec(memory_space=pltpu.SMEM)] * 2,
        [WHOLE] * 2,
        [(block, F32)] * 2,
        [pltpu.VMEM((2,) + block, BF16), pltpu.SemaphoreType.DMA((2, count))],
        tile=where,
        after=after,
        far=(0,),
    )(amplitudes, energy_virtual.reshape(2, 1, width), energy_first, energy_second)


def residual_kernel(chunks, shards, halves, last, where, *refs):
    middles, vectors, refs = refs[:chunks], refs[chunks : chunks + shards], refs[chunks + shards :]
    count, _, width = vectors[0].shape
    before, outs = refs[: len(halves)], refs[len(halves) :]
    if last:
        out, held, done = outs
    columns = middles[0].shape[2]
    copies = []
    for n, h in enumerate(halves):
        rows = pl.ds(pl.multiple_of(lax.rem(where[0] + h, 2) * columns, 16), columns)
        left = joined_rows([m[h if m.shape[0] > 1 else 0] for m in middles]).T
        for j in range(count):
            total = jnp.dot(left, joined_rows([v[j] for v in vectors]), preferred_element_type=F32)
            total += before[n][j]
            if last:
                held[n, j] = total.astype(BF16)
                copies.append(pltpu.make_async_copy(held.at[n, j], out.at[j, rows], done.at[n, j]))
                copies[-1].start()
            else:
                outs[n][j] = total
    for copy in copies:
        copy.wait()


def residual(where, middles, vectors, halves, before, last=False, after=()):
    count, _, width = vectors[0].shape
    block = (count, middles[0].shape[2], width)
    args = [*middles, *vectors, *before]
    out_shapes, scratch = [(block, F32)] * len(halves), []
    if last:
        out_shapes = [((count, 2 * block[1], width), BF16)]
        scratch = [pltpu.VMEM((2,) + block, BF16), pltpu.SemaphoreType.DMA((2, count))]
    return kernel_call(
        functools.partial(residual_kernel, len(middles), len(vectors), halves, last),
        "residual",
        (1,),
        [WHOLE] * len(args),
        [ANYWHERE if last else WHOLE] * len(out_shapes),
        out_shapes,
        scratch,
        tile=where,
        after=after,
        out=pltpu.HBM if last else pltpu.VMEM,
    )(*args)


def two_tiles(amplitudes, cholesky, energy_first, energy_second, energy_virtual):
    count, virtual, width = amplitudes.shape
    groups = OCC // count
    places = lax.axis_size("pair") // groups
    place, group = lax.axis_index("pair") // groups, lax.axis_index("pair") % groups
    y = lax.axis_index("virt")
    where = jnp.stack([y, group, place]).astype(jnp.int32)
    ring = functools.partial(along_ring, groups=groups)
    to_core = functools.partial(swap, axis="pair", bit=0)
    to_tile = functools.partial(swap, axis="virt", bit=0)

    unit = width // 32
    pieces = [(0, 15 * unit), (15 * unit, 13 * unit), (28 * unit, 4 * unit)]
    sent = cut(where, amplitudes, pieces[:1])
    sent += cut(where, amplitudes, pieces[1:], after=sent)
    arrived = [to_tile(v) for v in sent]

    own = jnp.swapaxes(cholesky, 1, 2)
    vectors = [own]
    forth, back = own, own
    for step in range(1, places // 2):
        forth, back = ring(forth, 1), ring(back, -1)
        vectors += [forth, back]

    near, near_theirs, far_turned = [], [], []
    held = sent[1:]
    parts = 4
    for part in range(parts):
        v, w = turn(where, amplitudes, part, parts, after=held)
        near.append(v)
        far_turned.append(w)
        near_theirs.append(to_core(v))
        if part == parts // 2 - 1:
            wall_1 = wall(*vectors[1:3], arrived[0], *near_theirs, cost=WALLS[0])
            held = [wall_1]
    begun = diagonal(
        where, amplitudes, energy_virtual, energy_first, energy_second, after=near
    )
    wall_2 = wall(*vectors[3:5], arrived[1], *near_theirs[parts // 2 :], *begun, cost=WALLS[1])
    far_0 = mix(far_turned, arrived[:2], 0, after=[wall_2])
    far_0_theirs = to_core(far_0)
    near, near_theirs = [near], [near_theirs]
    n_a, same_a, cross_a = partial(
        where, vectors[:5], vectors[:5], near, near_theirs, joined=2, after=[far_0]
    )
    n_a_sent = to_tile(n_a)
    far_1 = mix(far_turned, arrived[2:], far_0.shape[1], after=[n_a])
    far_1_theirs = to_core(far_1)
    far, far_theirs = [far_0, far_1], [far_0_theirs, far_1_theirs]
    f_a, cross_a = partial(where, [same_a], [cross_a], [far], [far_theirs], joined=1)
    f_a_sent = to_tile(f_a)
    handed_a = to_core(cross_a)
    picked = pick(where, *vectors[5:7], after=[f_a, n_a_sent])
    same_c, cross_c = ring(picked[0], 1), ring(picked[1], -1)
    wall_3 = wall(*picked, cost=WALLS[2])
    halves, halves_theirs = near + [far], near_theirs + [far_theirs]
    p_b, same_b, cross_b = partial(
        where, vectors[5:7], vectors[5:7], halves, halves_theirs, joined=2, after=[wall_3]
    )
    p_b_sent = to_tile(p_b)
    m_off = join([((f_a, 0), (n_a_sent, 0))], after=[p_b])
    (begun_off,) = residual(where, [m_off], [same_a], [1], begun[1:])
    m_a = join([((n_a, 0), (f_a_sent, 0))], [((f_a, 0), (n_a_sent, 0))], after=[begun_off])
    m_a_theirs = to_core(m_a)
    (begun_own,) = residual(where, [m_a], [same_a], [0], begun[:1])
    wall_4 = wall(same_c, cross_c, begun_own, cost=WALLS[3])
    p_c, same_d, cross_d = partial(
        where,
        [same_c],
        [cross_c],
        halves,
        halves_theirs,
        joined=2,
        behind=[same_b, cross_b],
        after=[wall_4],
    )
    p_c_sent = to_tile(p_c)
    handed_d = to_core(cross_d)
    wall_5 = wall(p_c, p_b_sent, cost=WALLS[4])
    begun = residual(
        where,
        [m_a_theirs],
        [handed_a],
        [0, 1],
        [begun_own, begun_off],
        after=[wall_5],
    )
    m_d = join(
        *[[((p_b, h), (p_b_sent, 1 - h)), ((p_c, h), (p_c_sent, 1 - h))] for h in range(2)],
        after=begun,
    )
    m_d_theirs = to_core(m_d)
    (out,) = residual(where, [m_d, m_d_theirs], [same_d, handed_d], [0, 1], begun, last=True)
    return out


def from_partner(x, axis, bit):
    return lax.ppermute(x, axis, [(i, i ^ 1 << bit) for i in range(lax.axis_size(axis))])


def any_tiles(amplitudes, cholesky, energy_first, energy_second, energy_virtual):
    pair_count, virtual_count, local_virtual = amplitudes.shape
    tiles_count = lax.axis_size("virt")
    first_count = max(pair_count // OCC, 1)
    second_count = pair_count // first_count
    offset = lax.axis_index("pair") * pair_count
    first_start = offset // OCC
    second_start = offset % OCC
    column_start = lax.axis_index("virt") * local_virtual
    blocks = amplitudes.reshape(pair_count, tiles_count, local_virtual, local_virtual)
    arrived = lax.all_to_all(blocks, "virt", split_axis=1, concat_axis=1, tiled=True)
    mirrored = jnp.swapaxes(arrived, 2, 3).reshape(pair_count, virtual_count, local_virtual)
    combined = (2.0 * amplitudes.astype(F32) - mirrored.astype(F32)).astype(BF16)
    combined = combined.reshape(first_count, second_count, virtual_count, local_virtual)
    vectors = lax.all_gather(cholesky, "pair", axis=2, tiled=True)
    chosen = lax.dynamic_slice_in_dim(vectors, second_start, second_count, 0)
    partial_value = jnp.einsum("ilad,ldq->iaq", combined, chosen, preferred_element_type=F32)
    collected = lax.psum(partial_value.astype(BF16), "virt").astype(F32)
    for bit in range((OCC // second_count).bit_length() - 1):
        collected = collected + from_partner(collected.astype(BF16), "pair", bit).astype(F32)
    reduced = collected.astype(BF16)
    cycle_term = jnp.einsum("iaq,lbq->ilab", reduced, chosen, preferred_element_type=F32)
    first_energy = lax.dynamic_slice_in_dim(energy_first, first_start, first_count, 0)
    second_energy = lax.dynamic_slice_in_dim(energy_second, second_start, second_count, 0)
    column_energy = lax.dynamic_slice_in_dim(energy_virtual, column_start, local_virtual, 0)
    virtual_pairs = energy_virtual[:, None] + column_energy[None, :]
    diagonal = (
        virtual_pairs[None, None, :, :]
        - first_energy[:, None, None, None]
        - second_energy[None, :, None, None]
    )
    values = amplitudes.reshape(first_count, second_count, virtual_count, local_virtual)
    result = diagonal * values.astype(F32) + cycle_term
    return result.reshape(pair_count, virtual_count, local_virtual).astype(BF16)


def on_device(amplitudes, *others):
    ring = lax.axis_size("pair") * amplitudes.shape[0] // OCC
    fits = lax.axis_size("virt") == 2 and amplitudes.shape[0] * 2 == OCC and ring == 8
    return (two_tiles if fits else any_tiles)(amplitudes, *others)


def solution(mesh):
    return jax.shard_map(
        on_device,
        mesh=mesh,
        in_specs=(P("pair", None, "virt"), P(None, "virt", "pair"), P(), P(), P()),
        out_specs=P("pair", None, "virt"),
        check_vma=False,
    )
```

```python
import functools

import jax
import jax.numpy as jnp
from jax import lax
from jax.experimental import pallas as pl
from jax.experimental.pallas import tpu as pltpu
from jax.sharding import PartitionSpec as P

OCC = 8
BF16, F32 = jnp.bfloat16, jnp.float32
VMEM_LIMIT = 20 * 2**20
WALLS = (1, 1, 1, 1, 16)
MIXED = 3
WHOLE = pl.BlockSpec(memory_space=pltpu.VMEM)
ANYWHERE = pl.BlockSpec(memory_space=pl.ANY)


def estimate(cost):
    return pl.CostEstimate(flops=int(cost * 10**9) + 1, bytes_accessed=1, transcendentals=0)


def kernel_call(
    body,
    name,
    grid,
    in_specs,
    out_specs,
    out_shapes,
    scratch=(),
    tile=None,
    after=(),
    far=(),
    out=pltpu.VMEM,
    cost=0,
):
    scalars = 0 if tile is None else 1
    extra = len(after)

    def kernel(*refs):
        keep = scalars + len(in_specs)
        body(*refs[:keep], *refs[keep + extra :])

    def call(*args):
        held = [
            a if a.ndim == 1 else pltpu.with_memory_space_constraint(a, pltpu.HBM if n in far else pltpu.VMEM)
            for n, a in enumerate((*args, *after))
        ]
        return pl.pallas_call(
            kernel,
            grid_spec=pltpu.PrefetchScalarGridSpec(
                num_scalar_prefetch=scalars,
                grid=grid,
                in_specs=[*in_specs, *[ANYWHERE] * extra],
                out_specs=list(out_specs),
                scratch_shapes=list(scratch),
            ),
            out_shape=[out(shape, kind) for shape, kind in out_shapes],
            compiler_params=pltpu.CompilerParams(
                dimension_semantics=("arbitrary",) * len(grid), vmem_limit_bytes=VMEM_LIMIT
            ),
            cost_estimate=estimate(cost),
            name=name,
        )(*([] if tile is None else [tile]), *held)

    return call


def swap(x, axis, bit):
    return lax.ppermute(x, axis, [(i, i ^ 1 << bit) for i in range(lax.axis_size(axis))])


def ring_of(count, groups):
    places = count // groups
    return list(range(0, places, 2)) + list(range(places - 1, 0, -2))


def along_ring(x, step, groups):
    order = ring_of(lax.axis_size("pair"), groups)
    pairs = [
        (a * groups + g, order[(n + step) % len(order)] * groups + g)
        for n, a in enumerate(order)
        for g in range(groups)
    ]
    return lax.ppermute(x, "pair", pairs)


def turn_kernel(where, own, own_rows, other, near, far):
    near[0] = (2.0 * own[0].astype(F32).T - own_rows[0].astype(F32)).astype(BF16)
    far[0] = other[0].T


def turn(where, amplitudes, part, parts, after=()):
    count, _, width = amplitudes.shape
    rows = width // parts
    block = (1, width, rows)
    out = pl.BlockSpec((1, rows, width), lambda j, t: (j, 0, 0))
    return kernel_call(
        turn_kernel,
        "turn",
        (count,),
        [
            pl.BlockSpec(block, lambda j, t: (j, t[0], part)),
            pl.BlockSpec((1, rows, width), lambda j, t: (j, t[0] * parts + part, 0)),
            pl.BlockSpec(block, lambda j, t: (j, 1 - t[0], part)),
        ],
        [out] * 2,
        [((count, rows, width), BF16)] * 2,
        tile=where,
        after=after,
        far=(0, 1, 2),
    )(amplitudes, amplitudes, amplitudes)


def cut_kernel(starts, where, *refs):
    outs, done = refs[-1 - len(starts) : -1], refs[-1]
    copies = []
    for n, (start, out) in enumerate(zip(starts, outs)):
        at = pl.multiple_of((1 - where[0]) * out.shape[2] + start, 16)
        source = refs[0].at[:, pl.ds(at, out.shape[1]), :]
        copies.append(pltpu.make_async_copy(source, out, done.at[n]))
    for copy in copies:
        copy.start()
    for copy in copies:
        copy.wait()


def cut(where, amplitudes, pieces, after=()):
    count, _, width = amplitudes.shape
    return kernel_call(
        functools.partial(cut_kernel, [start for start, _ in pieces]),
        "cut",
        (1,),
        [ANYWHERE],
        [WHOLE] * len(pieces),
        [((count, rows, width), BF16) for _, rows in pieces],
        [pltpu.SemaphoreType.DMA((len(pieces),))],
        tile=where,
        after=after,
        far=(0,),
    )(amplitudes)


def mix_kernel(parts, start, *refs):
    far, arrived, out = refs[:parts], refs[parts:-1], refs[-1]
    step = far[0].shape[1]
    first = 0
    for r in arrived:
        rows = r.shape[1]
        while rows:
            part, at = divmod(start + first, step)
            here = min(rows, step - at)
            came = r.shape[1] - rows
            value = 2.0 * far[part][:, at : at + here].astype(F32)
            value -= r[:, came : came + here].astype(F32)
            out[:, first : first + here] = value.astype(BF16)
            first, rows = first + here, rows - here


def mix(far, arrived, start, after=(), cost=0):
    count, _, width = far[0].shape
    shape = (count, sum(r.shape[1] for r in arrived), width)
    (out,) = kernel_call(
        functools.partial(mix_kernel, len(far), start),
        "mix",
        (1,),
        [WHOLE] * (len(far) + len(arrived)),
        [WHOLE],
        [(shape, BF16)],
        after=after,
        cost=cost,
    )(*far, *arrived)
    return out


def partial_kernel(shards, parts, joined, extras, where, *refs):
    same, cross = refs[:shards], refs[shards : 2 * shards]
    refs = refs[2 * shards :]
    arrays = sum(parts)
    mine, theirs, refs = refs[:arrays], refs[arrays : 2 * arrays], refs[2 * arrays :]
    extra, outs = refs[:extras], refs[extras:]
    count = mine[0].shape[0]

    def together(arrays, j, group=0):
        pieces = [r[j + (group * count if r.shape[0] > count else 0)] for r in arrays]
        return jnp.concatenate(pieces, axis=0) if len(pieces) > 1 else pieces[0]

    totals = [None] * len(parts)
    for j in range(count):
        left, right = together(same, j, where[1]), together(cross, j, 1 - where[1])
        for n in range(joined):
            value = (left, right)[n - joined]
            outs[1 + n][j] = jnp.concatenate([extra[n][j], value], axis=0) if extras else value
        at = 0
        for h, split in enumerate(parts):
            for shard, half in ((left, mine), (right, theirs)):
                half = together(half[at : at + split], j)
                value = jnp.dot(shard, half, preferred_element_type=F32)
                totals[h] = value if totals[h] is None else totals[h] + value
            at += split
    for h, total in enumerate(totals):
        outs[0][h] = total.astype(BF16)


def partial(where, same, cross, mine, theirs, joined=0, behind=(), after=()):
    parts = [len(m) for m in mine]
    shards, halves = len(same), len(mine)
    count, _, columns = mine[0][0].shape
    width = same[0].shape[2]
    rows = sum(v.shape[1] for v in same)
    args = [*same, *cross, *sum(mine, []), *sum(theirs, []), *behind]
    out_shapes = [((halves, rows, columns), BF16)]
    for n in range(joined):
        more = rows + (behind[n].shape[1] if behind else 0)
        out_shapes.append(((count, more, width), BF16))
    return kernel_call(
        functools.partial(partial_kernel, shards, parts, joined, len(behind)),
        "partial",
        (1,),
        [WHOLE] * len(args),
        [WHOLE] * len(out_shapes),
        out_shapes,
        tile=where,
        after=after,
    )(*args)


def pick_kernel(where, forth, back, same, cross):
    same[...] = forth[...]
    cross[...] = back[...]


def pick(where, forth, back, after=()):
    block = (forth.shape[0] // 2,) + forth.shape[1:]
    return kernel_call(
        pick_kernel,
        "pick",
        (1,),
        [
            pl.BlockSpec(block, lambda k, t: (t[1], 0, 0)),
            pl.BlockSpec(block, lambda k, t: (1 - t[1], 0, 0)),
        ],
        [pl.BlockSpec(block, lambda k, t: (0, 0, 0))] * 2,
        [(block, BF16)] * 2,
        tile=where,
        after=after,
    )(forth, back)


def nothing(*refs):
    pass


def wall(*arrays, cost=0.1):
    held = [pltpu.with_memory_space_constraint(a, pltpu.VMEM) for a in arrays]
    return pl.pallas_call(
        nothing,
        in_specs=[ANYWHERE] * len(held),
        out_specs=ANYWHERE,
        out_shape=pltpu.VMEM((8, 128), F32),
        compiler_params=pltpu.CompilerParams(vmem_limit_bytes=2**20),
        cost_estimate=estimate(cost),
        name="wall",
    )(*held)


def join_kernel(counts, *refs):
    out, at = refs[-1], 0
    for h, count in enumerate(counts):
        own, sent = refs[at : at + count], refs[at + count : at + 2 * count]
        at += 2 * count
        left, right = [
            jnp.concatenate([r[...] for r in v], axis=0) if count > 1 else v[0][...]
            for v in (own, sent)
        ]
        out[h] = (left.astype(F32) + right.astype(F32)).astype(BF16)


def join(*halves, after=()):
    args, in_specs = [], []
    for pairs in halves:
        for side in range(2):
            for pair in pairs:
                v, h = pair[side]
                args.append(v)
                in_specs.append(pl.BlockSpec((None,) + v.shape[1:], functools.partial(lambda h, k: (h, 0, 0), h)))
    rows = sum(pair[0][0].shape[1] for pair in halves[0])
    shape = (len(halves), rows, args[0].shape[2])
    (out,) = kernel_call(
        functools.partial(join_kernel, [len(pairs) for pairs in halves]),
        "join",
        (1,),
        in_specs,
        [WHOLE],
        [(shape, BF16)],
        after=after,
    )(*args)
    return out


def joined_rows(pieces):
    return jnp.concatenate(pieces, axis=0) if len(pieces) > 1 else pieces[0]


def diagonal_kernel(where, values, energy, first_energy, second_energy, own, off, held, done):
    count, columns, width = own.shape
    copies = []
    for h in range(2):
        tile = lax.rem(where[0] + h, 2)
        rows = pl.ds(pl.multiple_of(tile * columns, 16), columns)
        for j in range(count):
            copies.append(pltpu.make_async_copy(values.at[j, rows], held.at[h, j], done.at[h, j]))
            copies[-1].start()
    for h, out in enumerate((own, off)):
        row_energy = energy[lax.rem(where[0] + h, 2)]
        row_energy = jnp.broadcast_to(row_energy, (128, columns)).T[:, :1]
        for j in range(count):
            occupied = first_energy[where[2]] + second_energy[where[1] * count + j]
            copies[h * count + j].wait()
            out[j] = (row_energy - occupied + energy[where[0]]) * held[h, j].astype(F32)


def diagonal(where, amplitudes, energy_virtual, energy_first, energy_second, after=()):
    count, rows, width = amplitudes.shape
    block = (count, rows // 2, width)
    return kernel_call(
        diagonal_kernel,
        "diagonal",
        (1,),
        [ANYWHERE, WHOLE] + [pl.BlockSpec(memory_space=pltpu.SMEM)] * 2,
        [WHOLE] * 2,
        [(block, F32)] * 2,
        [pltpu.VMEM((2,) + block, BF16), pltpu.SemaphoreType.DMA((2, count))],
        tile=where,
        after=after,
        far=(0,),
    )(amplitudes, energy_virtual.reshape(2, 1, width), energy_first, energy_second)


def residual_kernel(chunks, shards, halves, last, where, *refs):
    middles, vectors, refs = refs[:chunks], refs[chunks : chunks + shards], refs[chunks + shards :]
    count, _, width = vectors[0].shape
    before, outs = refs[: len(halves)], refs[len(halves) :]
    if last:
        out, held, done = outs
    columns = middles[0].shape[2]
    copies = []
    for n, h in enumerate(halves):
        rows = pl.ds(pl.multiple_of(lax.rem(where[0] + h, 2) * columns, 16), columns)
        left = joined_rows([m[h if m.shape[0] > 1 else 0] for m in middles]).T
        for j in range(count):
            total = jnp.dot(left, joined_rows([v[j] for v in vectors]), preferred_element_type=F32)
            total += before[n][j]
            if last:
                held[n, j] = total.astype(BF16)
                copies.append(pltpu.make_async_copy(held.at[n, j], out.at[j, rows], done.at[n, j]))
                copies[-1].start()
            else:
                outs[n][j] = total
    for copy in copies:
        copy.wait()


def residual(where, middles, vectors, halves, before, last=False, after=()):
    count, _, width = vectors[0].shape
    block = (count, middles[0].shape[2], width)
    args = [*middles, *vectors, *before]
    out_shapes, scratch = [(block, F32)] * len(halves), []
    if last:
        out_shapes = [((count, 2 * block[1], width), BF16)]
        scratch = [pltpu.VMEM((2,) + block, BF16), pltpu.SemaphoreType.DMA((2, count))]
    return kernel_call(
        functools.partial(residual_kernel, len(middles), len(vectors), halves, last),
        "residual",
        (1,),
        [WHOLE] * len(args),
        [ANYWHERE if last else WHOLE] * len(out_shapes),
        out_shapes,
        scratch,
        tile=where,
        after=after,
        out=pltpu.HBM if last else pltpu.VMEM,
    )(*args)


def two_tiles(amplitudes, cholesky, energy_first, energy_second, energy_virtual):
    count, virtual, width = amplitudes.shape
    groups = OCC // count
    places = lax.axis_size("pair") // groups
    place, group = lax.axis_index("pair") // groups, lax.axis_index("pair") % groups
    y = lax.axis_index("virt")
    where = jnp.stack([y, group, place]).astype(jnp.int32)
    ring = functools.partial(along_ring, groups=groups)
    to_core = functools.partial(swap, axis="pair", bit=0)
    to_tile = functools.partial(swap, axis="virt", bit=0)

    unit = width // 32
    pieces = [(0, 15 * unit), (15 * unit, 13 * unit), (28 * unit, 4 * unit)]
    sent = cut(where, amplitudes, pieces[:1])
    sent += cut(where, amplitudes, pieces[1:], after=sent)
    arrived = [to_tile(v) for v in sent]

    own = jnp.swapaxes(cholesky, 1, 2)
    vectors = [own]
    forth, back = own, own
    for step in range(1, places // 2):
        forth, back = ring(forth, 1), ring(back, -1)
        vectors += [forth, back]

    near, near_theirs, far_turned = [], [], []
    held = sent[1:]
    parts = 4
    for part in range(parts):
        v, w = turn(where, amplitudes, part, parts, after=held)
        near.append(v)
        far_turned.append(w)
        near_theirs.append(to_core(v))
        if part == parts // 2 - 1:
            wall_1 = wall(*vectors[1:3], arrived[0], *near_theirs, cost=WALLS[0])
            held = [wall_1]
    begun = diagonal(
        where, amplitudes, energy_virtual, energy_first, energy_second, after=near
    )
    wall_2 = wall(*vectors[3:5], arrived[1], *near_theirs[parts // 2 :], *begun, cost=WALLS[1])
    far_0 = mix(far_turned, arrived[:2], 0, after=[wall_2])
    far_0_theirs = to_core(far_0)
    near, near_theirs = [near], [near_theirs]
    n_a, same_a, cross_a = partial(
        where, vectors[:5], vectors[:5], near, near_theirs, joined=2, after=[far_0]
    )
    n_a_sent = to_tile(n_a)
    far_1 = mix(far_turned, arrived[2:], far_0.shape[1], after=[n_a], cost=MIXED)
    far_1_theirs = to_core(far_1)
    far, far_theirs = [far_0, far_1], [far_0_theirs, far_1_theirs]
    f_a, cross_a = partial(where, [same_a], [cross_a], [far], [far_theirs], joined=1)
    f_a_sent = to_tile(f_a)
    handed_a = to_core(cross_a)
    picked = pick(where, *vectors[5:7], after=[f_a, n_a_sent])
    same_c, cross_c = ring(picked[0], 1), ring(picked[1], -1)
    wall_3 = wall(*picked, cost=WALLS[2])
    halves, halves_theirs = near + [far], near_theirs + [far_theirs]
    p_b, same_b, cross_b = partial(
        where, vectors[5:7], vectors[5:7], halves, halves_theirs, joined=2, after=[wall_3]
    )
    p_b_sent = to_tile(p_b)
    m_off = join([((f_a, 0), (n_a_sent, 0))], after=[p_b])
    (begun_off,) = residual(where, [m_off], [same_a], [1], begun[1:])
    m_a = join([((n_a, 0), (f_a_sent, 0))], [((f_a, 0), (n_a_sent, 0))], after=[begun_off])
    m_a_theirs = to_core(m_a)
    (begun_own,) = residual(where, [m_a], [same_a], [0], begun[:1])
    wall_4 = wall(same_c, cross_c, begun_own, cost=WALLS[3])
    p_c, same_d, cross_d = partial(
        where,
        [same_c],
        [cross_c],
        halves,
        halves_theirs,
        joined=2,
        behind=[same_b, cross_b],
        after=[wall_4],
    )
    p_c_sent = to_tile(p_c)
    handed_d = to_core(cross_d)
    m_b = join(*[[((p_b, h), (p_b_sent, 1 - h))] for h in range(2)], after=[p_c])
    m_b_theirs = to_core(m_b)
    wall_5 = wall(m_b, cost=WALLS[4])
    begun = residual(
        where,
        [m_a_theirs],
        [handed_a],
        [0, 1],
        [begun_own, begun_off],
        after=[wall_5],
    )
    m_c = join(*[[((p_c, h), (p_c_sent, 1 - h))] for h in range(2)], after=begun)
    m_c_theirs = to_core(m_c)
    middles = [m_b, m_c, m_b_theirs, m_c_theirs]
    (out,) = residual(where, middles, [same_d, handed_d], [0, 1], begun, last=True)
    return out


def from_partner(x, axis, bit):
    return lax.ppermute(x, axis, [(i, i ^ 1 << bit) for i in range(lax.axis_size(axis))])


def any_tiles(amplitudes, cholesky, energy_first, energy_second, energy_virtual):
    pair_count, virtual_count, local_virtual = amplitudes.shape
    tiles_count = lax.axis_size("virt")
    first_count = max(pair_count // OCC, 1)
    second_count = pair_count // first_count
    offset = lax.axis_index("pair") * pair_count
    first_start = offset // OCC
    second_start = offset % OCC
    column_start = lax.axis_index("virt") * local_virtual
    blocks = amplitudes.reshape(pair_count, tiles_count, local_virtual, local_virtual)
    arrived = lax.all_to_all(blocks, "virt", split_axis=1, concat_axis=1, tiled=True)
    mirrored = jnp.swapaxes(arrived, 2, 3).reshape(pair_count, virtual_count, local_virtual)
    combined = (2.0 * amplitudes.astype(F32) - mirrored.astype(F32)).astype(BF16)
    combined = combined.reshape(first_count, second_count, virtual_count, local_virtual)
    vectors = lax.all_gather(cholesky, "pair", axis=2, tiled=True)
    chosen = lax.dynamic_slice_in_dim(vectors, second_start, second_count, 0)
    partial_value = jnp.einsum("ilad,ldq->iaq", combined, chosen, preferred_element_type=F32)
    collected = lax.psum(partial_value.astype(BF16), "virt").astype(F32)
    for bit in range((OCC // second_count).bit_length() - 1):
        collected = collected + from_partner(collected.astype(BF16), "pair", bit).astype(F32)
    reduced = collected.astype(BF16)
    cycle_term = jnp.einsum("iaq,lbq->ilab", reduced, chosen, preferred_element_type=F32)
    first_energy = lax.dynamic_slice_in_dim(energy_first, first_start, first_count, 0)
    second_energy = lax.dynamic_slice_in_dim(energy_second, second_start, second_count, 0)
    column_energy = lax.dynamic_slice_in_dim(energy_virtual, column_start, local_virtual, 0)
    virtual_pairs = energy_virtual[:, None] + column_energy[None, :]
    diagonal = (
        virtual_pairs[None, None, :, :]
        - first_energy[:, None, None, None]
        - second_energy[None, :, None, None]
    )
    values = amplitudes.reshape(first_count, second_count, virtual_count, local_virtual)
    result = diagonal * values.astype(F32) + cycle_term
    return result.reshape(pair_count, virtual_count, local_virtual).astype(BF16)


def on_device(amplitudes, *others):
    ring = lax.axis_size("pair") * amplitudes.shape[0] // OCC
    fits = lax.axis_size("virt") == 2 and amplitudes.shape[0] * 2 == OCC and ring == 8
    return (two_tiles if fits else any_tiles)(amplitudes, *others)


def solution(mesh):
    return jax.shard_map(
        on_device,
        mesh=mesh,
        in_specs=(P("pair", None, "virt"), P(None, "virt", "pair"), P(), P(), P()),
        out_specs=P("pair", None, "virt"),
        check_vma=False,
    )
```

```python
import functools

import jax
import jax.numpy as jnp
from jax import lax
from jax.experimental import pallas as pl
from jax.experimental.pallas import tpu as pltpu
from jax.sharding import PartitionSpec as P

OCC = 8
BF16, F32 = jnp.bfloat16, jnp.float32
VMEM_LIMIT = 20 * 2**20
WALLS = (1, 1, 1, 1, 16)
MIXED = 3
WHOLE = pl.BlockSpec(memory_space=pltpu.VMEM)
ANYWHERE = pl.BlockSpec(memory_space=pl.ANY)


def estimate(cost):
    return pl.CostEstimate(flops=int(cost * 10**9) + 1, bytes_accessed=1, transcendentals=0)


def kernel_call(
    body,
    name,
    grid,
    in_specs,
    out_specs,
    out_shapes,
    scratch=(),
    tile=None,
    after=(),
    far=(),
    out=pltpu.VMEM,
    cost=0,
):
    scalars = 0 if tile is None else 1
    extra = len(after)

    def kernel(*refs):
        keep = scalars + len(in_specs)
        body(*refs[:keep], *refs[keep + extra :])

    def call(*args):
        held = [
            a if a.ndim == 1 else pltpu.with_memory_space_constraint(a, pltpu.HBM if n in far else pltpu.VMEM)
            for n, a in enumerate((*args, *after))
        ]
        return pl.pallas_call(
            kernel,
            grid_spec=pltpu.PrefetchScalarGridSpec(
                num_scalar_prefetch=scalars,
                grid=grid,
                in_specs=[*in_specs, *[ANYWHERE] * extra],
                out_specs=list(out_specs),
                scratch_shapes=list(scratch),
            ),
            out_shape=[out(shape, kind) for shape, kind in out_shapes],
            compiler_params=pltpu.CompilerParams(
                dimension_semantics=("arbitrary",) * len(grid), vmem_limit_bytes=VMEM_LIMIT
            ),
            cost_estimate=estimate(cost),
            name=name,
        )(*([] if tile is None else [tile]), *held)

    return call


def swap(x, axis, bit):
    return lax.ppermute(x, axis, [(i, i ^ 1 << bit) for i in range(lax.axis_size(axis))])


def ring_of(count, groups):
    places = count // groups
    return list(range(0, places, 2)) + list(range(places - 1, 0, -2))


def along_ring(x, step, groups):
    order = ring_of(lax.axis_size("pair"), groups)
    pairs = [
        (a * groups + g, order[(n + step) % len(order)] * groups + g)
        for n, a in enumerate(order)
        for g in range(groups)
    ]
    return lax.ppermute(x, "pair", pairs)


def turn_kernel(where, own, own_rows, other, near, far):
    near[0] = (2.0 * own[0].astype(F32).T - own_rows[0].astype(F32)).astype(BF16)
    far[0] = other[0].T


def turn(where, amplitudes, part, parts, after=()):
    count, _, width = amplitudes.shape
    rows = width // parts
    block = (1, width, rows)
    out = pl.BlockSpec((1, rows, width), lambda j, t: (j, 0, 0))
    return kernel_call(
        turn_kernel,
        "turn",
        (count,),
        [
            pl.BlockSpec(block, lambda j, t: (j, t[0], part)),
            pl.BlockSpec((1, rows, width), lambda j, t: (j, t[0] * parts + part, 0)),
            pl.BlockSpec(block, lambda j, t: (j, 1 - t[0], part)),
        ],
        [out] * 2,
        [((count, rows, width), BF16)] * 2,
        tile=where,
        after=after,
        far=(0, 1, 2),
    )(amplitudes, amplitudes, amplitudes)


def cut_kernel(starts, where, *refs):
    outs, done = refs[-1 - len(starts) : -1], refs[-1]
    copies = []
    for n, (start, out) in enumerate(zip(starts, outs)):
        at = pl.multiple_of((1 - where[0]) * out.shape[2] + start, 16)
        source = refs[0].at[:, pl.ds(at, out.shape[1]), :]
        copies.append(pltpu.make_async_copy(source, out, done.at[n]))
    for copy in copies:
        copy.start()
    for copy in copies:
        copy.wait()


def cut(where, amplitudes, pieces, after=()):
    count, _, width = amplitudes.shape
    return kernel_call(
        functools.partial(cut_kernel, [start for start, _ in pieces]),
        "cut",
        (1,),
        [ANYWHERE],
        [WHOLE] * len(pieces),
        [((count, rows, width), BF16) for _, rows in pieces],
        [pltpu.SemaphoreType.DMA((len(pieces),))],
        tile=where,
        after=after,
        far=(0,),
    )(amplitudes)


def mix_kernel(parts, start, *refs):
    far, arrived, out = refs[:parts], refs[parts:-1], refs[-1]
    step = far[0].shape[1]
    first = 0
    for r in arrived:
        rows = r.shape[1]
        while rows:
            part, at = divmod(start + first, step)
            here = min(rows, step - at)
            came = r.shape[1] - rows
            value = 2.0 * far[part][:, at : at + here].astype(F32)
            value -= r[:, came : came + here].astype(F32)
            out[:, first : first + here] = value.astype(BF16)
            first, rows = first + here, rows - here


def mix(far, arrived, start, after=(), cost=0):
    count, _, width = far[0].shape
    shape = (count, sum(r.shape[1] for r in arrived), width)
    (out,) = kernel_call(
        functools.partial(mix_kernel, len(far), start),
        "mix",
        (1,),
        [WHOLE] * (len(far) + len(arrived)),
        [WHOLE],
        [(shape, BF16)],
        after=after,
        cost=cost,
    )(*far, *arrived)
    return out


def partial_kernel(shards, parts, joined, extras, where, *refs):
    same, cross = refs[:shards], refs[shards : 2 * shards]
    refs = refs[2 * shards :]
    arrays = sum(parts)
    mine, theirs, refs = refs[:arrays], refs[arrays : 2 * arrays], refs[2 * arrays :]
    extra, outs = refs[:extras], refs[extras:]
    count = mine[0].shape[0]

    def together(arrays, j, group=0):
        pieces = [r[j + (group * count if r.shape[0] > count else 0)] for r in arrays]
        return jnp.concatenate(pieces, axis=0) if len(pieces) > 1 else pieces[0]

    totals = [None] * len(parts)
    for j in range(count):
        left, right = together(same, j, where[1]), together(cross, j, 1 - where[1])
        for n in range(joined):
            value = (left, right)[n - joined]
            outs[1 + n][j] = jnp.concatenate([extra[n][j], value], axis=0) if extras else value
        at = 0
        for h, split in enumerate(parts):
            for shard, half in ((left, mine), (right, theirs)):
                half = together(half[at : at + split], j)
                value = jnp.dot(shard, half, preferred_element_type=F32)
                totals[h] = value if totals[h] is None else totals[h] + value
            at += split
    for h, total in enumerate(totals):
        outs[0][h] = total.astype(BF16)


def partial(where, same, cross, mine, theirs, joined=0, behind=(), after=()):
    parts = [len(m) for m in mine]
    shards, halves = len(same), len(mine)
    count, _, columns = mine[0][0].shape
    width = same[0].shape[2]
    rows = sum(v.shape[1] for v in same)
    args = [*same, *cross, *sum(mine, []), *sum(theirs, []), *behind]
    out_shapes = [((halves, rows, columns), BF16)]
    for n in range(joined):
        more = rows + (behind[n].shape[1] if behind else 0)
        out_shapes.append(((count, more, width), BF16))
    return kernel_call(
        functools.partial(partial_kernel, shards, parts, joined, len(behind)),
        "partial",
        (1,),
        [WHOLE] * len(args),
        [WHOLE] * len(out_shapes),
        out_shapes,
        tile=where,
        after=after,
    )(*args)


def pick_kernel(where, forth, back, same, cross):
    same[...] = forth[...]
    cross[...] = back[...]


def pick(where, forth, back, after=()):
    block = (forth.shape[0] // 2,) + forth.shape[1:]
    return kernel_call(
        pick_kernel,
        "pick",
        (1,),
        [
            pl.BlockSpec(block, lambda k, t: (t[1], 0, 0)),
            pl.BlockSpec(block, lambda k, t: (1 - t[1], 0, 0)),
        ],
        [pl.BlockSpec(block, lambda k, t: (0, 0, 0))] * 2,
        [(block, BF16)] * 2,
        tile=where,
        after=after,
    )(forth, back)


def nothing(*refs):
    pass


def wall(*arrays, cost=0.1):
    held = [pltpu.with_memory_space_constraint(a, pltpu.VMEM) for a in arrays]
    return pl.pallas_call(
        nothing,
        in_specs=[ANYWHERE] * len(held),
        out_specs=ANYWHERE,
        out_shape=pltpu.VMEM((8, 128), F32),
        compiler_params=pltpu.CompilerParams(vmem_limit_bytes=2**20),
        cost_estimate=estimate(cost),
        name="wall",
    )(*held)


def join_kernel(counts, *refs):
    out, at = refs[-1], 0
    for h, count in enumerate(counts):
        own, sent = refs[at : at + count], refs[at + count : at + 2 * count]
        at += 2 * count
        left, right = [
            jnp.concatenate([r[...] for r in v], axis=0) if count > 1 else v[0][...]
            for v in (own, sent)
        ]
        out[h] = (left.astype(F32) + right.astype(F32)).astype(BF16)


def join(*halves, after=()):
    args, in_specs = [], []
    for pairs in halves:
        for side in range(2):
            for pair in pairs:
                v, h = pair[side]
                args.append(v)
                in_specs.append(pl.BlockSpec((None,) + v.shape[1:], functools.partial(lambda h, k: (h, 0, 0), h)))
    rows = sum(pair[0][0].shape[1] for pair in halves[0])
    shape = (len(halves), rows, args[0].shape[2])
    (out,) = kernel_call(
        functools.partial(join_kernel, [len(pairs) for pairs in halves]),
        "join",
        (1,),
        in_specs,
        [WHOLE],
        [(shape, BF16)],
        after=after,
    )(*args)
    return out


def joined_rows(pieces):
    return jnp.concatenate(pieces, axis=0) if len(pieces) > 1 else pieces[0]


def diagonal_kernel(where, values, energy, first_energy, second_energy, own, off, held, done):
    count, columns, width = own.shape
    copies = []
    for h in range(2):
        tile = lax.rem(where[0] + h, 2)
        rows = pl.ds(pl.multiple_of(tile * columns, 16), columns)
        for j in range(count):
            copies.append(pltpu.make_async_copy(values.at[j, rows], held.at[h, j], done.at[h, j]))
            copies[-1].start()
    for h, out in enumerate((own, off)):
        row_energy = energy[lax.rem(where[0] + h, 2)]
        row_energy = jnp.broadcast_to(row_energy, (128, columns)).T[:, :1]
        for j in range(count):
            occupied = first_energy[where[2]] + second_energy[where[1] * count + j]
            copies[h * count + j].wait()
            out[j] = (row_energy - occupied + energy[where[0]]) * held[h, j].astype(F32)


def diagonal(where, amplitudes, energy_virtual, energy_first, energy_second, after=()):
    count, rows, width = amplitudes.shape
    block = (count, rows // 2, width)
    return kernel_call(
        diagonal_kernel,
        "diagonal",
        (1,),
        [ANYWHERE, WHOLE] + [pl.BlockSpec(memory_space=pltpu.SMEM)] * 2,
        [WHOLE] * 2,
        [(block, F32)] * 2,
        [pltpu.VMEM((2,) + block, BF16), pltpu.SemaphoreType.DMA((2, count))],
        tile=where,
        after=after,
        far=(0,),
    )(amplitudes, energy_virtual.reshape(2, 1, width), energy_first, energy_second)


def residual_kernel(rows_of, depths_of, halves, last, where, *refs):
    chunks, shards = len(rows_of), len(depths_of)
    middles, vectors, refs = refs[:chunks], refs[chunks : chunks + shards], refs[chunks + shards :]
    count, _, width = vectors[0].shape
    before, outs = refs[: len(halves)], refs[len(halves) :]
    if last:
        out, held, done = outs
    columns = middles[0].shape[2]
    copies = []
    for n, h in enumerate(halves):
        rows = pl.ds(pl.multiple_of(lax.rem(where[0] + h, 2) * columns, 16), columns)
        parts = [m[h if m.shape[0] > 1 else 0, a:b] for m, (a, b) in zip(middles, rows_of)]
        left = joined_rows(parts).T
        for j in range(count):
            right = joined_rows([v[j, a:b] for v, (a, b) in zip(vectors, depths_of)])
            total = jnp.dot(left, right, preferred_element_type=F32)
            total += before[n][j]
            if last:
                held[n, j] = total.astype(BF16)
                copies.append(pltpu.make_async_copy(held.at[n, j], out.at[j, rows], done.at[n, j]))
                copies[-1].start()
            else:
                outs[n][j] = total
    for copy in copies:
        copy.wait()


def residual(where, middles, vectors, halves, before, last=False, after=()):
    whole = lambda v: v if isinstance(v, tuple) else (v, 0, v.shape[1])
    middles, rows_of = zip(*[(v, (a, b)) for v, a, b in map(whole, middles)])
    vectors, depths_of = zip(*[(v, (a, b)) for v, a, b in map(whole, vectors)])
    count, _, width = vectors[0].shape
    block = (count, middles[0].shape[2], width)
    args = [*middles, *vectors, *before]
    out_shapes, scratch = [(block, F32)] * len(halves), []
    if last:
        out_shapes = [((count, 2 * block[1], width), BF16)]
        scratch = [pltpu.VMEM((2,) + block, BF16), pltpu.SemaphoreType.DMA((2, count))]
    return kernel_call(
        functools.partial(residual_kernel, rows_of, depths_of, halves, last),
        "residual",
        (1,),
        [WHOLE] * len(args),
        [ANYWHERE if last else WHOLE] * len(out_shapes),
        out_shapes,
        scratch,
        tile=where,
        after=after,
        out=pltpu.HBM if last else pltpu.VMEM,
    )(*args)


def two_tiles(amplitudes, cholesky, energy_first, energy_second, energy_virtual):
    count, virtual, width = amplitudes.shape
    groups = OCC // count
    places = lax.axis_size("pair") // groups
    place, group = lax.axis_index("pair") // groups, lax.axis_index("pair") % groups
    y = lax.axis_index("virt")
    where = jnp.stack([y, group, place]).astype(jnp.int32)
    ring = functools.partial(along_ring, groups=groups)
    to_core = functools.partial(swap, axis="pair", bit=0)
    to_tile = functools.partial(swap, axis="virt", bit=0)

    unit = width // 32
    pieces = [(0, 15 * unit), (15 * unit, 13 * unit), (28 * unit, 4 * unit)]
    sent = cut(where, amplitudes, pieces[:1])
    sent += cut(where, amplitudes, pieces[1:], after=sent)
    arrived = [to_tile(v) for v in sent]

    own = jnp.swapaxes(cholesky, 1, 2)
    vectors = [own]
    forth, back = own, own
    for step in range(1, places // 2):
        forth, back = ring(forth, 1), ring(back, -1)
        vectors += [forth, back]

    near, near_theirs, far_turned = [], [], []
    held = sent[1:]
    parts = 4
    for part in range(parts):
        v, w = turn(where, amplitudes, part, parts, after=held)
        near.append(v)
        far_turned.append(w)
        near_theirs.append(to_core(v))
        if part == parts // 2 - 1:
            wall_1 = wall(*vectors[1:3], arrived[0], *near_theirs, cost=WALLS[0])
            held = [wall_1]
    begun = diagonal(
        where, amplitudes, energy_virtual, energy_first, energy_second, after=near
    )
    wall_2 = wall(*vectors[3:5], arrived[1], *near_theirs[parts // 2 :], *begun, cost=WALLS[1])
    far_0 = mix(far_turned, arrived[:2], 0, after=[wall_2])
    far_0_theirs = to_core(far_0)
    near, near_theirs = [near], [near_theirs]
    n_a, same_a, cross_a = partial(
        where, vectors[:5], vectors[:5], near, near_theirs, joined=2, after=[far_0]
    )
    n_a_sent = to_tile(n_a)
    far_1 = mix(far_turned, arrived[2:], far_0.shape[1], after=[n_a], cost=MIXED)
    far_1_theirs = to_core(far_1)
    far, far_theirs = [far_0, far_1], [far_0_theirs, far_1_theirs]
    f_a, cross_a = partial(where, [same_a], [cross_a], [far], [far_theirs], joined=1)
    f_a_sent = to_tile(f_a)
    handed_a = to_core(cross_a)
    picked = pick(where, *vectors[5:7], after=[f_a, n_a_sent])
    same_c, cross_c = ring(picked[0], 1), ring(picked[1], -1)
    wall_3 = wall(*picked, cost=WALLS[2])
    halves, halves_theirs = near + [far], near_theirs + [far_theirs]
    p_b, same_b, cross_b = partial(
        where, vectors[5:7], vectors[5:7], halves, halves_theirs, joined=2, after=[wall_3]
    )
    p_b_sent = to_tile(p_b)
    m_off = join([((f_a, 0), (n_a_sent, 0))], after=[p_b])
    (begun_off,) = residual(where, [m_off], [same_a], [1], begun[1:])
    m_a = join([((n_a, 0), (f_a_sent, 0))], [((f_a, 0), (n_a_sent, 0))], after=[begun_off])
    m_a_theirs = to_core(m_a)
    (begun_own,) = residual(where, [m_a], [same_a], [0], begun[:1])
    wall_4 = wall(same_c, cross_c, begun_own, cost=WALLS[3])
    p_c, same_d, cross_d = partial(
        where,
        [same_c],
        [cross_c],
        halves,
        halves_theirs,
        joined=2,
        behind=[same_b, cross_b],
        after=[wall_4],
    )
    p_c_sent = to_tile(p_c)
    handed_d = to_core(cross_d)
    m_b = join(*[[((p_b, h), (p_b_sent, 1 - h))] for h in range(2)], after=[p_c])
    m_b_theirs = to_core(m_b)
    wall_5 = wall(m_b, cost=WALLS[4])
    rows_b = m_b.shape[1]
    taken = min(-m_a.shape[1] % 256 // 16 * 16, rows_b)
    extra = bool(taken)
    begun = residual(
        where,
        [m_a_theirs] + [(m_b, 0, taken)] * extra,
        [handed_a] + [(same_d, 0, taken)] * extra,
        [0, 1],
        [begun_own, begun_off],
        after=[wall_5],
    )
    m_c = join(*[[((p_c, h), (p_c_sent, 1 - h))] for h in range(2)], after=begun)
    m_c_theirs = to_core(m_c)
    middles = [m_c, m_b_theirs, m_c_theirs]
    vectors = [(same_d, taken, same_d.shape[1]), handed_d]
    if taken < rows_b:
        middles = [(m_b, taken, rows_b)] + middles
    (out,) = residual(where, middles, vectors, [0, 1], begun, last=True)
    return out


def from_partner(x, axis, bit):
    return lax.ppermute(x, axis, [(i, i ^ 1 << bit) for i in range(lax.axis_size(axis))])


def any_tiles(amplitudes, cholesky, energy_first, energy_second, energy_virtual):
    pair_count, virtual_count, local_virtual = amplitudes.shape
    tiles_count = lax.axis_size("virt")
    first_count = max(pair_count // OCC, 1)
    second_count = pair_count // first_count
    offset = lax.axis_index("pair") * pair_count
    first_start = offset // OCC
    second_start = offset % OCC
    column_start = lax.axis_index("virt") * local_virtual
    blocks = amplitudes.reshape(pair_count, tiles_count, local_virtual, local_virtual)
    arrived = lax.all_to_all(blocks, "virt", split_axis=1, concat_axis=1, tiled=True)
    mirrored = jnp.swapaxes(arrived, 2, 3).reshape(pair_count, virtual_count, local_virtual)
    combined = (2.0 * amplitudes.astype(F32) - mirrored.astype(F32)).astype(BF16)
    combined = combined.reshape(first_count, second_count, virtual_count, local_virtual)
    vectors = lax.all_gather(cholesky, "pair", axis=2, tiled=True)
    chosen = lax.dynamic_slice_in_dim(vectors, second_start, second_count, 0)
    partial_value = jnp.einsum("ilad,ldq->iaq", combined, chosen, preferred_element_type=F32)
    collected = lax.psum(partial_value.astype(BF16), "virt").astype(F32)
    for bit in range((OCC // second_count).bit_length() - 1):
        collected = collected + from_partner(collected.astype(BF16), "pair", bit).astype(F32)
    reduced = collected.astype(BF16)
    cycle_term = jnp.einsum("iaq,lbq->ilab", reduced, chosen, preferred_element_type=F32)
    first_energy = lax.dynamic_slice_in_dim(energy_first, first_start, first_count, 0)
    second_energy = lax.dynamic_slice_in_dim(energy_second, second_start, second_count, 0)
    column_energy = lax.dynamic_slice_in_dim(energy_virtual, column_start, local_virtual, 0)
    virtual_pairs = energy_virtual[:, None] + column_energy[None, :]
    diagonal = (
        virtual_pairs[None, None, :, :]
        - first_energy[:, None, None, None]
        - second_energy[None, :, None, None]
    )
    values = amplitudes.reshape(first_count, second_count, virtual_count, local_virtual)
    result = diagonal * values.astype(F32) + cycle_term
    return result.reshape(pair_count, virtual_count, local_virtual).astype(BF16)


def on_device(amplitudes, *others):
    ring = lax.axis_size("pair") * amplitudes.shape[0] // OCC
    fits = lax.axis_size("virt") == 2 and amplitudes.shape[0] * 2 == OCC and ring == 8
    return (two_tiles if fits else any_tiles)(amplitudes, *others)


def solution(mesh):
    return jax.shard_map(
        on_device,
        mesh=mesh,
        in_specs=(P("pair", None, "virt"), P(None, "virt", "pair"), P(), P(), P()),
        out_specs=P("pair", None, "virt"),
        check_vma=False,
    )
```

```python
import functools

import jax
import jax.numpy as jnp
from jax import lax
from jax.experimental import pallas as pl
from jax.experimental.pallas import tpu as pltpu
from jax.sharding import PartitionSpec as P

OCC = 8
BF16, F32 = jnp.bfloat16, jnp.float32
VMEM_LIMIT = 20 * 2**20
WALLS = (1, 1, 1, 1, 16)
MIXED = 3
WHOLE = pl.BlockSpec(memory_space=pltpu.VMEM)
ANYWHERE = pl.BlockSpec(memory_space=pl.ANY)


def estimate(cost):
    return pl.CostEstimate(flops=int(cost * 10**9) + 1, bytes_accessed=1, transcendentals=0)


def kernel_call(
    body,
    name,
    grid,
    in_specs,
    out_specs,
    out_shapes,
    scratch=(),
    after=(),
    far=(),
    out=pltpu.VMEM,
    cost=0,
):
    extra = len(after)

    def kernel(*refs):
        keep = len(in_specs)
        body(*refs[:keep], *refs[keep + extra :])

    def call(*args):
        held = [
            a if a.ndim == 1 else pltpu.with_memory_space_constraint(a, pltpu.HBM if n in far else pltpu.VMEM)
            for n, a in enumerate((*args, *after))
        ]
        return pl.pallas_call(
            kernel,
            grid=grid,
            in_specs=[*in_specs, *[ANYWHERE] * extra],
            out_specs=list(out_specs),
            scratch_shapes=list(scratch),
            out_shape=[out(shape, kind) for shape, kind in out_shapes],
            compiler_params=pltpu.CompilerParams(
                dimension_semantics=("arbitrary",) * len(grid), vmem_limit_bytes=VMEM_LIMIT
            ),
            cost_estimate=estimate(cost),
            name=name,
        )(*held)

    return call


def position(count):
    groups = OCC // count
    pair = lax.axis_index("pair")
    return lax.axis_index("virt"), lax.rem(pair, groups), lax.div(pair, groups)


def swap(x, axis, bit):
    return lax.ppermute(x, axis, [(i, i ^ 1 << bit) for i in range(lax.axis_size(axis))])


def ring_of(count, groups):
    places = count // groups
    return list(range(0, places, 2)) + list(range(places - 1, 0, -2))


def along_ring(x, step, groups):
    order = ring_of(lax.axis_size("pair"), groups)
    pairs = [
        (a * groups + g, order[(n + step) % len(order)] * groups + g)
        for n, a in enumerate(order)
        for g in range(groups)
    ]
    return lax.ppermute(x, "pair", pairs)


def turn_kernel(part, amplitudes, near, far, own, own_rows, other, done):
    count, rows, width = near.shape
    tile = lax.axis_index("virt")
    first, second = pl.multiple_of(tile * width, 16), pl.multiple_of((1 - tile) * width, 16)
    columns = pl.ds(part * rows, rows)
    copies = []
    for j in range(count):
        sources = [
            (amplitudes.at[j, pl.ds(first, width), columns], own),
            (amplitudes.at[j, pl.ds(pl.multiple_of(first + part * rows, 16), rows)], own_rows),
            (amplitudes.at[j, pl.ds(second, width), columns], other),
        ]
        for n, (source, held) in enumerate(sources):
            copies.append(pltpu.make_async_copy(source, held.at[j], done.at[n, j]))
            copies[-1].start()
    for j in range(count):
        for copy in copies[3 * j : 3 * j + 3]:
            copy.wait()
        near[j] = (2.0 * own[j].astype(F32).T - own_rows[j].astype(F32)).astype(BF16)
        far[j] = other[j].T


def turn(amplitudes, part, parts, after=()):
    count, _, width = amplitudes.shape
    rows = width // parts
    tall, flat = (count, width, rows), (count, rows, width)
    return kernel_call(
        functools.partial(turn_kernel, part),
        "turn",
        (1,),
        [ANYWHERE],
        [WHOLE] * 2,
        [(flat, BF16)] * 2,
        [
            pltpu.VMEM(tall, BF16),
            pltpu.VMEM(flat, BF16),
            pltpu.VMEM(tall, BF16),
            pltpu.SemaphoreType.DMA((3, count)),
        ],
        after=after,
        far=(0,),
    )(amplitudes)


def cut_kernel(starts, *refs):
    outs, done = refs[-1 - len(starts) : -1], refs[-1]
    tile = lax.axis_index("virt")
    copies = []
    for n, (start, out) in enumerate(zip(starts, outs)):
        at = pl.multiple_of((1 - tile) * out.shape[2] + start, 16)
        source = refs[0].at[:, pl.ds(at, out.shape[1]), :]
        copies.append(pltpu.make_async_copy(source, out, done.at[n]))
    for copy in copies:
        copy.start()
    for copy in copies:
        copy.wait()


def cut(amplitudes, pieces, after=()):
    count, _, width = amplitudes.shape
    return kernel_call(
        functools.partial(cut_kernel, [start for start, _ in pieces]),
        "cut",
        (1,),
        [ANYWHERE],
        [WHOLE] * len(pieces),
        [((count, rows, width), BF16) for _, rows in pieces],
        [pltpu.SemaphoreType.DMA((len(pieces),))],
        after=after,
        far=(0,),
    )(amplitudes)


def mix_kernel(parts, start, *refs):
    far, arrived, out = refs[:parts], refs[parts:-1], refs[-1]
    step = far[0].shape[1]
    first = 0
    for r in arrived:
        rows = r.shape[1]
        while rows:
            part, at = divmod(start + first, step)
            here = min(rows, step - at)
            came = r.shape[1] - rows
            value = 2.0 * far[part][:, at : at + here].astype(F32)
            value -= r[:, came : came + here].astype(F32)
            out[:, first : first + here] = value.astype(BF16)
            first, rows = first + here, rows - here


def mix(far, arrived, start, after=(), cost=0):
    count, _, width = far[0].shape
    shape = (count, sum(r.shape[1] for r in arrived), width)
    (out,) = kernel_call(
        functools.partial(mix_kernel, len(far), start),
        "mix",
        (1,),
        [WHOLE] * (len(far) + len(arrived)),
        [WHOLE],
        [(shape, BF16)],
        after=after,
        cost=cost,
    )(*far, *arrived)
    return out


def partial_kernel(shards, parts, joined, extras, *refs):
    same, cross = refs[:shards], refs[shards : 2 * shards]
    refs = refs[2 * shards :]
    arrays = sum(parts)
    mine, theirs, refs = refs[:arrays], refs[arrays : 2 * arrays], refs[2 * arrays :]
    extra, outs = refs[:extras], refs[extras:]
    count = mine[0].shape[0]
    _, group, _ = position(count)

    def together(arrays, j, group=0):
        pieces = [r[j + (group * count if r.shape[0] > count else 0)] for r in arrays]
        return jnp.concatenate(pieces, axis=0) if len(pieces) > 1 else pieces[0]

    totals = [None] * len(parts)
    for j in range(count):
        left, right = together(same, j, group), together(cross, j, 1 - group)
        for n in range(joined):
            value = (left, right)[n - joined]
            outs[1 + n][j] = jnp.concatenate([extra[n][j], value], axis=0) if extras else value
        at = 0
        for h, split in enumerate(parts):
            for shard, half in ((left, mine), (right, theirs)):
                half = together(half[at : at + split], j)
                value = jnp.dot(shard, half, preferred_element_type=F32)
                totals[h] = value if totals[h] is None else totals[h] + value
            at += split
    for h, total in enumerate(totals):
        outs[0][h] = total.astype(BF16)


def partial(same, cross, mine, theirs, joined=0, behind=(), after=()):
    parts = [len(m) for m in mine]
    shards, halves = len(same), len(mine)
    count, _, columns = mine[0][0].shape
    width = same[0].shape[2]
    rows = sum(v.shape[1] for v in same)
    args = [*same, *cross, *sum(mine, []), *sum(theirs, []), *behind]
    out_shapes = [((halves, rows, columns), BF16)]
    for n in range(joined):
        more = rows + (behind[n].shape[1] if behind else 0)
        out_shapes.append(((count, more, width), BF16))
    return kernel_call(
        functools.partial(partial_kernel, shards, parts, joined, len(behind)),
        "partial",
        (1,),
        [WHOLE] * len(args),
        [WHOLE] * len(out_shapes),
        out_shapes,
        after=after,
    )(*args)


def pick_kernel(forth, back, same, cross):
    count = same.shape[0]
    _, group, _ = position(count)
    for j in range(count):
        same[j] = forth[group * count + j]
        cross[j] = back[(1 - group) * count + j]


def pick(forth, back, after=()):
    shape = (forth.shape[0] // 2,) + forth.shape[1:]
    return kernel_call(
        pick_kernel, "pick", (1,), [WHOLE] * 2, [WHOLE] * 2, [(shape, BF16)] * 2, after=after
    )(forth, back)


def nothing(*refs):
    pass


def wall(*arrays, cost=0.1):
    held = [pltpu.with_memory_space_constraint(a, pltpu.VMEM) for a in arrays]
    return pl.pallas_call(
        nothing,
        in_specs=[ANYWHERE] * len(held),
        out_specs=ANYWHERE,
        out_shape=pltpu.VMEM((8, 128), F32),
        compiler_params=pltpu.CompilerParams(vmem_limit_bytes=2**20),
        cost_estimate=estimate(cost),
        name="wall",
    )(*held)


def join_kernel(counts, *refs):
    out, at = refs[-1], 0
    for h, count in enumerate(counts):
        own, sent = refs[at : at + count], refs[at + count : at + 2 * count]
        at += 2 * count
        left, right = [
            jnp.concatenate([r[...] for r in v], axis=0) if count > 1 else v[0][...]
            for v in (own, sent)
        ]
        out[h] = (left.astype(F32) + right.astype(F32)).astype(BF16)


def join(*halves, after=()):
    args, in_specs = [], []
    for pairs in halves:
        for side in range(2):
            for pair in pairs:
                v, h = pair[side]
                args.append(v)
                in_specs.append(pl.BlockSpec((None,) + v.shape[1:], functools.partial(lambda h, k: (h, 0, 0), h)))
    rows = sum(pair[0][0].shape[1] for pair in halves[0])
    shape = (len(halves), rows, args[0].shape[2])
    (out,) = kernel_call(
        functools.partial(join_kernel, [len(pairs) for pairs in halves]),
        "join",
        (1,),
        in_specs,
        [WHOLE],
        [(shape, BF16)],
        after=after,
    )(*args)
    return out


def joined_rows(pieces):
    return jnp.concatenate(pieces, axis=0) if len(pieces) > 1 else pieces[0]


def diagonal_kernel(values, energy, first_energy, second_energy, own, off, held, done):
    count, columns, width = own.shape
    here, group, place = position(count)
    copies = []
    for h in range(2):
        tile = lax.rem(here + h, 2)
        rows = pl.ds(pl.multiple_of(tile * columns, 16), columns)
        for j in range(count):
            copies.append(pltpu.make_async_copy(values.at[j, rows], held.at[h, j], done.at[h, j]))
            copies[-1].start()
    for h, out in enumerate((own, off)):
        row_energy = energy[lax.rem(here + h, 2)]
        row_energy = jnp.broadcast_to(row_energy, (128, columns)).T[:, :1]
        for j in range(count):
            occupied = first_energy[place] + second_energy[group * count + j]
            copies[h * count + j].wait()
            out[j] = (row_energy - occupied + energy[here]) * held[h, j].astype(F32)


def diagonal(amplitudes, energy_virtual, energy_first, energy_second, after=()):
    count, rows, width = amplitudes.shape
    block = (count, rows // 2, width)
    return kernel_call(
        diagonal_kernel,
        "diagonal",
        (1,),
        [ANYWHERE, WHOLE] + [pl.BlockSpec(memory_space=pltpu.SMEM)] * 2,
        [WHOLE] * 2,
        [(block, F32)] * 2,
        [pltpu.VMEM((2,) + block, BF16), pltpu.SemaphoreType.DMA((2, count))],
        after=after,
        far=(0,),
    )(amplitudes, energy_virtual.reshape(2, 1, width), energy_first, energy_second)


def residual_kernel(rows_of, depths_of, halves, last, *refs):
    chunks, shards = len(rows_of), len(depths_of)
    middles, vectors, refs = refs[:chunks], refs[chunks : chunks + shards], refs[chunks + shards :]
    count, _, width = vectors[0].shape
    before, outs = refs[: len(halves)], refs[len(halves) :]
    if last:
        out, held, done = outs
    columns = middles[0].shape[2]
    copies = []
    for n, h in enumerate(halves):
        rows = pl.ds(pl.multiple_of(lax.rem(lax.axis_index("virt") + h, 2) * columns, 16), columns)
        parts = [m[h if m.shape[0] > 1 else 0, a:b] for m, (a, b) in zip(middles, rows_of)]
        left = joined_rows(parts).T
        for j in range(count):
            right = joined_rows([v[j, a:b] for v, (a, b) in zip(vectors, depths_of)])
            total = jnp.dot(left, right, preferred_element_type=F32)
            total += before[n][j]
            if last:
                held[n, j] = total.astype(BF16)
                copies.append(pltpu.make_async_copy(held.at[n, j], out.at[j, rows], done.at[n, j]))
                copies[-1].start()
            else:
                outs[n][j] = total
    for copy in copies:
        copy.wait()


def residual(middles, vectors, halves, before, last=False, after=()):
    whole = lambda v: v if isinstance(v, tuple) else (v, 0, v.shape[1])
    middles, rows_of = zip(*[(v, (a, b)) for v, a, b in map(whole, middles)])
    vectors, depths_of = zip(*[(v, (a, b)) for v, a, b in map(whole, vectors)])
    count, _, width = vectors[0].shape
    block = (count, middles[0].shape[2], width)
    args = [*middles, *vectors, *before]
    out_shapes, scratch = [(block, F32)] * len(halves), []
    if last:
        out_shapes = [((count, 2 * block[1], width), BF16)]
        scratch = [pltpu.VMEM((2,) + block, BF16), pltpu.SemaphoreType.DMA((2, count))]
    return kernel_call(
        functools.partial(residual_kernel, rows_of, depths_of, halves, last),
        "residual",
        (1,),
        [WHOLE] * len(args),
        [ANYWHERE if last else WHOLE] * len(out_shapes),
        out_shapes,
        scratch,
        after=after,
        out=pltpu.HBM if last else pltpu.VMEM,
    )(*args)


def two_tiles(amplitudes, cholesky, energy_first, energy_second, energy_virtual):
    count, virtual, width = amplitudes.shape
    groups = OCC // count
    places = lax.axis_size("pair") // groups
    ring = functools.partial(along_ring, groups=groups)
    to_core = functools.partial(swap, axis="pair", bit=0)
    to_tile = functools.partial(swap, axis="virt", bit=0)

    unit = width // 32
    pieces = [(0, 15 * unit), (15 * unit, 13 * unit), (28 * unit, 4 * unit)]
    sent = cut(amplitudes, pieces[:1])
    sent += cut(amplitudes, pieces[1:], after=sent)
    arrived = [to_tile(v) for v in sent]

    own = jnp.swapaxes(cholesky, 1, 2)
    vectors = [own]
    forth, back = own, own
    for step in range(1, places // 2):
        forth, back = ring(forth, 1), ring(back, -1)
        vectors += [forth, back]

    near, near_theirs, far_turned = [], [], []
    held = sent[1:]
    parts = 4
    for part in range(parts):
        v, w = turn(amplitudes, part, parts, after=held)
        near.append(v)
        far_turned.append(w)
        near_theirs.append(to_core(v))
        if part == parts // 2 - 1:
            wall_1 = wall(*vectors[1:3], arrived[0], *near_theirs, cost=WALLS[0])
            held = [wall_1]
    begun = diagonal(
        amplitudes, energy_virtual, energy_first, energy_second, after=near
    )
    wall_2 = wall(*vectors[3:5], arrived[1], *near_theirs[parts // 2 :], *begun, cost=WALLS[1])
    far_0 = mix(far_turned, arrived[:2], 0, after=[wall_2])
    far_0_theirs = to_core(far_0)
    near, near_theirs = [near], [near_theirs]
    n_a, same_a, cross_a = partial(
        vectors[:5], vectors[:5], near, near_theirs, joined=2, after=[far_0]
    )
    n_a_sent = to_tile(n_a)
    far_1 = mix(far_turned, arrived[2:], far_0.shape[1], after=[n_a], cost=MIXED)
    far_1_theirs = to_core(far_1)
    far, far_theirs = [far_0, far_1], [far_0_theirs, far_1_theirs]
    f_a, cross_a = partial([same_a], [cross_a], [far], [far_theirs], joined=1)
    f_a_sent = to_tile(f_a)
    handed_a = to_core(cross_a)
    picked = pick(*vectors[5:7], after=[f_a, n_a_sent])
    same_c, cross_c = ring(picked[0], 1), ring(picked[1], -1)
    wall_3 = wall(*picked, cost=WALLS[2])
    halves, halves_theirs = near + [far], near_theirs + [far_theirs]
    p_b, same_b, cross_b = partial(
        vectors[5:7], vectors[5:7], halves, halves_theirs, joined=2, after=[wall_3]
    )
    p_b_sent = to_tile(p_b)
    m_off = join([((f_a, 0), (n_a_sent, 0))], after=[p_b])
    (begun_off,) = residual([m_off], [same_a], [1], begun[1:])
    m_a = join([((n_a, 0), (f_a_sent, 0))], [((f_a, 0), (n_a_sent, 0))], after=[begun_off])
    m_a_theirs = to_core(m_a)
    (begun_own,) = residual([m_a], [same_a], [0], begun[:1])
    wall_4 = wall(same_c, cross_c, begun_own, cost=WALLS[3])
    p_c, same_d, cross_d = partial(
        [same_c],
        [cross_c],
        halves,
        halves_theirs,
        joined=2,
        behind=[same_b, cross_b],
        after=[wall_4],
    )
    p_c_sent = to_tile(p_c)
    handed_d = to_core(cross_d)
    m_b = join(*[[((p_b, h), (p_b_sent, 1 - h))] for h in range(2)], after=[p_c])
    m_b_theirs = to_core(m_b)
    wall_5 = wall(m_b, cost=WALLS[4])
    rows_b = m_b.shape[1]
    taken = min(-m_a.shape[1] % 256 // 16 * 16, rows_b)
    extra = bool(taken)
    begun = residual(
        [m_a_theirs] + [(m_b, 0, taken)] * extra,
        [handed_a] + [(same_d, 0, taken)] * extra,
        [0, 1],
        [begun_own, begun_off],
        after=[wall_5],
    )
    m_c = join(*[[((p_c, h), (p_c_sent, 1 - h))] for h in range(2)], after=begun)
    m_c_theirs = to_core(m_c)
    middles = [m_c, m_b_theirs, m_c_theirs]
    vectors = [(same_d, taken, same_d.shape[1]), handed_d]
    if taken < rows_b:
        middles = [(m_b, taken, rows_b)] + middles
    (out,) = residual(middles, vectors, [0, 1], begun, last=True)
    return out


def from_partner(x, axis, bit):
    return lax.ppermute(x, axis, [(i, i ^ 1 << bit) for i in range(lax.axis_size(axis))])


def any_tiles(amplitudes, cholesky, energy_first, energy_second, energy_virtual):
    pair_count, virtual_count, local_virtual = amplitudes.shape
    tiles_count = lax.axis_size("virt")
    first_count = max(pair_count // OCC, 1)
    second_count = pair_count // first_count
    offset = lax.axis_index("pair") * pair_count
    first_start = offset // OCC
    second_start = offset % OCC
    column_start = lax.axis_index("virt") * local_virtual
    blocks = amplitudes.reshape(pair_count, tiles_count, local_virtual, local_virtual)
    arrived = lax.all_to_all(blocks, "virt", split_axis=1, concat_axis=1, tiled=True)
    mirrored = jnp.swapaxes(arrived, 2, 3).reshape(pair_count, virtual_count, local_virtual)
    combined = (2.0 * amplitudes.astype(F32) - mirrored.astype(F32)).astype(BF16)
    combined = combined.reshape(first_count, second_count, virtual_count, local_virtual)
    vectors = lax.all_gather(cholesky, "pair", axis=2, tiled=True)
    chosen = lax.dynamic_slice_in_dim(vectors, second_start, second_count, 0)
    partial_value = jnp.einsum("ilad,ldq->iaq", combined, chosen, preferred_element_type=F32)
    collected = lax.psum(partial_value.astype(BF16), "virt").astype(F32)
    for bit in range((OCC // second_count).bit_length() - 1):
        collected = collected + from_partner(collected.astype(BF16), "pair", bit).astype(F32)
    reduced = collected.astype(BF16)
    cycle_term = jnp.einsum("iaq,lbq->ilab", reduced, chosen, preferred_element_type=F32)
    first_energy = lax.dynamic_slice_in_dim(energy_first, first_start, first_count, 0)
    second_energy = lax.dynamic_slice_in_dim(energy_second, second_start, second_count, 0)
    column_energy = lax.dynamic_slice_in_dim(energy_virtual, column_start, local_virtual, 0)
    virtual_pairs = energy_virtual[:, None] + column_energy[None, :]
    diagonal = (
        virtual_pairs[None, None, :, :]
        - first_energy[:, None, None, None]
        - second_energy[None, :, None, None]
    )
    values = amplitudes.reshape(first_count, second_count, virtual_count, local_virtual)
    result = diagonal * values.astype(F32) + cycle_term
    return result.reshape(pair_count, virtual_count, local_virtual).astype(BF16)


def on_device(amplitudes, *others):
    ring = lax.axis_size("pair") * amplitudes.shape[0] // OCC
    fits = lax.axis_size("virt") == 2 and amplitudes.shape[0] * 2 == OCC and ring == 8
    return (two_tiles if fits else any_tiles)(amplitudes, *others)


def solution(mesh):
    return jax.shard_map(
        on_device,
        mesh=mesh,
        in_specs=(P("pair", None, "virt"), P(None, "virt", "pair"), P(), P(), P()),
        out_specs=P("pair", None, "virt"),
        check_vma=False,
    )
```

```python
import functools

import jax
import jax.numpy as jnp
from jax import lax
from jax.experimental import pallas as pl
from jax.experimental.pallas import tpu as pltpu
from jax.sharding import PartitionSpec as P

OCC = 8
BF16, F32 = jnp.bfloat16, jnp.float32
VMEM_LIMIT = 20 * 2**20
WALLS = (1, 1, 1, 1, 16)
MIXED = 3
WHOLE = pl.BlockSpec(memory_space=pltpu.VMEM)
ANYWHERE = pl.BlockSpec(memory_space=pl.ANY)


def estimate(cost):
    return pl.CostEstimate(flops=int(cost * 10**9) + 1, bytes_accessed=1, transcendentals=0)


def kernel_call(
    body,
    name,
    grid,
    in_specs,
    out_specs,
    out_shapes,
    scratch=(),
    after=(),
    far=(),
    out=pltpu.VMEM,
    cost=0,
):
    extra = len(after)

    def kernel(*refs):
        keep = len(in_specs)
        body(*refs[:keep], *refs[keep + extra :])

    def call(*args):
        held = [
            a if a.ndim == 1 else pltpu.with_memory_space_constraint(a, pltpu.HBM if n in far else pltpu.VMEM)
            for n, a in enumerate((*args, *after))
        ]
        return pl.pallas_call(
            kernel,
            grid=grid,
            in_specs=[*in_specs, *[ANYWHERE] * extra],
            out_specs=list(out_specs),
            scratch_shapes=list(scratch),
            out_shape=[out(shape, kind) for shape, kind in out_shapes],
            compiler_params=pltpu.CompilerParams(
                dimension_semantics=("arbitrary",) * len(grid), vmem_limit_bytes=VMEM_LIMIT
            ),
            cost_estimate=estimate(cost),
            name=name,
        )(*held)

    return call


def position(count):
    groups = OCC // count
    pair = lax.axis_index("pair")
    return lax.axis_index("virt"), lax.rem(pair, groups), lax.div(pair, groups)


def swap(x, axis, bit):
    return lax.ppermute(x, axis, [(i, i ^ 1 << bit) for i in range(lax.axis_size(axis))])


def ring_of(count, groups):
    places = count // groups
    return list(range(0, places, 2)) + list(range(places - 1, 0, -2))


def along_ring(x, step, groups):
    order = ring_of(lax.axis_size("pair"), groups)
    pairs = [
        (a * groups + g, order[(n + step) % len(order)] * groups + g)
        for n, a in enumerate(order)
        for g in range(groups)
    ]
    return lax.ppermute(x, "pair", pairs)


def turn_kernel(part, amplitudes, near, far, own, own_rows, other, done):
    count, rows, width = near.shape
    tile = lax.axis_index("virt")
    first, second = pl.multiple_of(tile * width, 16), pl.multiple_of((1 - tile) * width, 16)
    columns = pl.ds(part * rows, rows)
    copies = []
    for j in range(count):
        sources = [
            (amplitudes.at[j, pl.ds(first, width), columns], own),
            (amplitudes.at[j, pl.ds(pl.multiple_of(first + part * rows, 16), rows)], own_rows),
            (amplitudes.at[j, pl.ds(second, width), columns], other),
        ]
        for n, (source, held) in enumerate(sources):
            copies.append(pltpu.make_async_copy(source, held.at[j], done.at[n, j]))
            copies[-1].start()
    for j in range(count):
        for copy in copies[3 * j : 3 * j + 3]:
            copy.wait()
        near[j] = (2.0 * own[j].astype(F32).T - own_rows[j].astype(F32)).astype(BF16)
        far[j] = other[j].T


def turn(amplitudes, part, parts, after=()):
    count, _, width = amplitudes.shape
    rows = width // parts
    tall, flat = (count, width, rows), (count, rows, width)
    return kernel_call(
        functools.partial(turn_kernel, part),
        "turn",
        (1,),
        [ANYWHERE],
        [WHOLE] * 2,
        [(flat, BF16)] * 2,
        [
            pltpu.VMEM(tall, BF16),
            pltpu.VMEM(flat, BF16),
            pltpu.VMEM(tall, BF16),
            pltpu.SemaphoreType.DMA((3, count)),
        ],
        after=after,
        far=(0,),
    )(amplitudes)


def cut_kernel(starts, *refs):
    outs, done = refs[-1 - len(starts) : -1], refs[-1]
    tile = lax.axis_index("virt")
    copies = []
    for n, (start, out) in enumerate(zip(starts, outs)):
        at = pl.multiple_of((1 - tile) * out.shape[2] + start, 16)
        source = refs[0].at[:, pl.ds(at, out.shape[1]), :]
        copies.append(pltpu.make_async_copy(source, out, done.at[n]))
    for copy in copies:
        copy.start()
    for copy in copies:
        copy.wait()


def cut(amplitudes, pieces, after=()):
    count, _, width = amplitudes.shape
    return kernel_call(
        functools.partial(cut_kernel, [start for start, _ in pieces]),
        "cut",
        (1,),
        [ANYWHERE],
        [WHOLE] * len(pieces),
        [((count, rows, width), BF16) for _, rows in pieces],
        [pltpu.SemaphoreType.DMA((len(pieces),))],
        after=after,
        far=(0,),
    )(amplitudes)


def mix_kernel(parts, start, *refs):
    far, arrived, out = refs[:parts], refs[parts:-1], refs[-1]
    step = far[0].shape[1]
    first = 0
    for r in arrived:
        rows = r.shape[1]
        while rows:
            part, at = divmod(start + first, step)
            here = min(rows, step - at)
            came = r.shape[1] - rows
            value = 2.0 * far[part][:, at : at + here].astype(F32)
            value -= r[:, came : came + here].astype(F32)
            out[:, first : first + here] = value.astype(BF16)
            first, rows = first + here, rows - here


def mix(far, arrived, start, after=(), cost=0):
    count, _, width = far[0].shape
    shape = (count, sum(r.shape[1] for r in arrived), width)
    (out,) = kernel_call(
        functools.partial(mix_kernel, len(far), start),
        "mix",
        (1,),
        [WHOLE] * (len(far) + len(arrived)),
        [WHOLE],
        [(shape, BF16)],
        after=after,
        cost=cost,
    )(*far, *arrived)
    return out


def partial_kernel(shards, parts, joined, extras, *refs):
    same, cross = refs[:shards], refs[shards : 2 * shards]
    refs = refs[2 * shards :]
    arrays = sum(parts)
    mine, theirs, refs = refs[:arrays], refs[arrays : 2 * arrays], refs[2 * arrays :]
    extra, outs = refs[:extras], refs[extras:]
    count = mine[0].shape[0]
    _, group, _ = position(count)

    def together(arrays, j, group=0):
        pieces = [r[j + (group * count if r.shape[0] > count else 0)] for r in arrays]
        return jnp.concatenate(pieces, axis=0) if len(pieces) > 1 else pieces[0]

    totals = [None] * len(parts)
    for j in range(count):
        left, right = together(same, j, group), together(cross, j, 1 - group)
        for n in range(joined):
            value = (left, right)[n - joined]
            outs[1 + n][j] = jnp.concatenate([extra[n][j], value], axis=0) if extras else value
        at = 0
        for h, split in enumerate(parts):
            for shard, half in ((left, mine), (right, theirs)):
                half = together(half[at : at + split], j)
                value = jnp.dot(shard, half, preferred_element_type=F32)
                totals[h] = value if totals[h] is None else totals[h] + value
            at += split
    for h, total in enumerate(totals):
        outs[0][h] = total.astype(BF16)


def partial(same, cross, mine, theirs, joined=0, behind=(), after=()):
    parts = [len(m) for m in mine]
    shards, halves = len(same), len(mine)
    count, _, columns = mine[0][0].shape
    width = same[0].shape[2]
    rows = sum(v.shape[1] for v in same)
    args = [*same, *cross, *sum(mine, []), *sum(theirs, []), *behind]
    out_shapes = [((halves, rows, columns), BF16)]
    for n in range(joined):
        more = rows + (behind[n].shape[1] if behind else 0)
        out_shapes.append(((count, more, width), BF16))
    return kernel_call(
        functools.partial(partial_kernel, shards, parts, joined, len(behind)),
        "partial",
        (1,),
        [WHOLE] * len(args),
        [WHOLE] * len(out_shapes),
        out_shapes,
        after=after,
    )(*args)


def pick_kernel(forth, back, same, cross):
    count = same.shape[0]
    _, group, _ = position(count)
    for j in range(count):
        same[j] = forth[group * count + j]
        cross[j] = back[(1 - group) * count + j]


def pick(forth, back, after=()):
    shape = (forth.shape[0] // 2,) + forth.shape[1:]
    return kernel_call(
        pick_kernel, "pick", (1,), [WHOLE] * 2, [WHOLE] * 2, [(shape, BF16)] * 2, after=after
    )(forth, back)


def nothing(*refs):
    pass


def wall(*arrays, cost=0.1):
    held = [pltpu.with_memory_space_constraint(a, pltpu.VMEM) for a in arrays]
    return pl.pallas_call(
        nothing,
        in_specs=[ANYWHERE] * len(held),
        out_specs=ANYWHERE,
        out_shape=pltpu.VMEM((8, 128), F32),
        compiler_params=pltpu.CompilerParams(vmem_limit_bytes=2**20),
        cost_estimate=estimate(cost),
        name="wall",
    )(*held)


def join_kernel(counts, *refs):
    out, at = refs[-1], 0
    for h, count in enumerate(counts):
        own, sent = refs[at : at + count], refs[at + count : at + 2 * count]
        at += 2 * count
        left, right = [
            jnp.concatenate([r[...] for r in v], axis=0) if count > 1 else v[0][...]
            for v in (own, sent)
        ]
        out[h] = (left.astype(F32) + right.astype(F32)).astype(BF16)


def join(*halves, after=()):
    args, in_specs = [], []
    for pairs in halves:
        for side in range(2):
            for pair in pairs:
                v, h = pair[side]
                args.append(v)
                in_specs.append(pl.BlockSpec((None,) + v.shape[1:], functools.partial(lambda h, k: (h, 0, 0), h)))
    rows = sum(pair[0][0].shape[1] for pair in halves[0])
    shape = (len(halves), rows, args[0].shape[2])
    (out,) = kernel_call(
        functools.partial(join_kernel, [len(pairs) for pairs in halves]),
        "join",
        (1,),
        in_specs,
        [WHOLE],
        [(shape, BF16)],
        after=after,
    )(*args)
    return out


def joined_rows(pieces):
    return jnp.concatenate(pieces, axis=0) if len(pieces) > 1 else pieces[0]


def diagonal_kernel(values, energy, first_energy, second_energy, own, off, held, done):
    count, columns, width = own.shape
    here, group, place = position(count)
    copies = []
    for h in range(2):
        tile = lax.rem(here + h, 2)
        rows = pl.ds(pl.multiple_of(tile * columns, 16), columns)
        for j in range(count):
            copies.append(pltpu.make_async_copy(values.at[j, rows], held.at[h, j], done.at[h, j]))
            copies[-1].start()
    for h, out in enumerate((own, off)):
        row_energy = energy[lax.rem(here + h, 2)]
        row_energy = jnp.broadcast_to(row_energy, (128, columns)).T[:, :1]
        for j in range(count):
            occupied = first_energy[place] + second_energy[group * count + j]
            copies[h * count + j].wait()
            out[j] = (row_energy - occupied + energy[here]) * held[h, j].astype(F32)


def diagonal(amplitudes, energy_virtual, energy_first, energy_second, after=()):
    count, rows, width = amplitudes.shape
    block = (count, rows // 2, width)
    return kernel_call(
        diagonal_kernel,
        "diagonal",
        (1,),
        [ANYWHERE, WHOLE] + [pl.BlockSpec(memory_space=pltpu.SMEM)] * 2,
        [WHOLE] * 2,
        [(block, F32)] * 2,
        [pltpu.VMEM((2,) + block, BF16), pltpu.SemaphoreType.DMA((2, count))],
        after=after,
        far=(0,),
    )(amplitudes, energy_virtual.reshape(2, 1, width), energy_first, energy_second)


def residual_kernel(rows_of, depths_of, halves, last, *refs):
    chunks, shards = len(rows_of), len(depths_of)
    middles, vectors, refs = refs[:chunks], refs[chunks : chunks + shards], refs[chunks + shards :]
    count, _, width = vectors[0].shape
    before, outs = refs[: len(halves)], refs[len(halves) :]
    if last:
        out, held, done = outs
    columns = middles[0].shape[2]
    copies = []
    for n, h in enumerate(halves):
        rows = pl.ds(pl.multiple_of(lax.rem(lax.axis_index("virt") + h, 2) * columns, 16), columns)
        parts = [m[h if m.shape[0] > 1 else 0, a:b] for m, (a, b) in zip(middles, rows_of)]
        left = joined_rows(parts).T
        for j in range(count):
            right = joined_rows([v[j, a:b] for v, (a, b) in zip(vectors, depths_of)])
            total = jnp.dot(left, right, preferred_element_type=F32)
            total += before[n][j]
            if last:
                held[n, j] = total.astype(BF16)
                copies.append(pltpu.make_async_copy(held.at[n, j], out.at[j, rows], done.at[n, j]))
                copies[-1].start()
            else:
                outs[n][j] = total
    for copy in copies:
        copy.wait()


def residual(middles, vectors, halves, before, last=False, after=()):
    whole = lambda v: v if isinstance(v, tuple) else (v, 0, v.shape[1])
    middles, rows_of = zip(*[(v, (a, b)) for v, a, b in map(whole, middles)])
    vectors, depths_of = zip(*[(v, (a, b)) for v, a, b in map(whole, vectors)])
    count, _, width = vectors[0].shape
    block = (count, middles[0].shape[2], width)
    args = [*middles, *vectors, *before]
    out_shapes, scratch = [(block, F32)] * len(halves), []
    if last:
        out_shapes = [((count, 2 * block[1], width), BF16)]
        scratch = [pltpu.VMEM((2,) + block, BF16), pltpu.SemaphoreType.DMA((2, count))]
    return kernel_call(
        functools.partial(residual_kernel, rows_of, depths_of, halves, last),
        "residual",
        (1,),
        [WHOLE] * len(args),
        [ANYWHERE if last else WHOLE] * len(out_shapes),
        out_shapes,
        scratch,
        after=after,
        out=pltpu.HBM if last else pltpu.VMEM,
    )(*args)


def two_tiles(amplitudes, cholesky, energy_first, energy_second, energy_virtual):
    count, virtual, width = amplitudes.shape
    groups = OCC // count
    places = lax.axis_size("pair") // groups
    ring = functools.partial(along_ring, groups=groups)
    to_core = functools.partial(swap, axis="pair", bit=0)
    to_tile = functools.partial(swap, axis="virt", bit=0)

    unit = width // 32
    pieces = [(0, 15 * unit), (15 * unit, 13 * unit), (28 * unit, 4 * unit)]
    sent = cut(amplitudes, pieces[:1])
    sent += cut(amplitudes, pieces[1:], after=sent)
    arrived = [to_tile(v) for v in sent]

    own = jnp.swapaxes(cholesky, 1, 2)
    vectors = [own]
    forth, back = own, own
    for step in range(1, places // 2):
        forth, back = ring(forth, 1), ring(back, -1)
        vectors += [forth, back]

    near, near_theirs, far_turned = [], [], []
    held = sent[1:]
    parts = 4
    for part in range(parts):
        v, w = turn(amplitudes, part, parts, after=held)
        near.append(v)
        far_turned.append(w)
        near_theirs.append(to_core(v))
        if part == parts // 2 - 1:
            wall_1 = wall(*vectors[1:3], arrived[0], *near_theirs, cost=WALLS[0])
            held = [wall_1]
    begun = diagonal(
        amplitudes, energy_virtual, energy_first, energy_second, after=near
    )
    wall_2 = wall(*vectors[3:5], arrived[1], *near_theirs[parts // 2 :], *begun, cost=WALLS[1])
    far_0 = mix(far_turned, arrived[:2], 0, after=[wall_2])
    far_0_theirs = to_core(far_0)
    near, near_theirs = [near], [near_theirs]
    n_a, same_a, cross_a = partial(
        vectors[:5], vectors[:5], near, near_theirs, joined=2, after=[far_0]
    )
    n_a_sent = to_tile(n_a)
    far_1 = mix(far_turned, arrived[2:], far_0.shape[1], after=[n_a], cost=MIXED)
    far_1_theirs = to_core(far_1)
    far, far_theirs = [far_0, far_1], [far_0_theirs, far_1_theirs]
    f_a, cross_a = partial([same_a], [cross_a], [far], [far_theirs], joined=1)
    f_a_sent = to_tile(f_a)
    handed_a = to_core(cross_a)
    picked = pick(*vectors[5:7], after=[f_a, n_a_sent])
    same_c, cross_c = ring(picked[0], 1), ring(picked[1], -1)
    wall_3 = wall(*picked, cost=WALLS[2])
    halves, halves_theirs = near + [far], near_theirs + [far_theirs]
    p_b, same_b, cross_b = partial(
        vectors[5:7], vectors[5:7], halves, halves_theirs, joined=2, after=[wall_3]
    )
    p_b_sent = to_tile(p_b)
    m_off = join([((f_a, 0), (n_a_sent, 0))], after=[p_b])
    (begun_off,) = residual([m_off], [same_a], [1], begun[1:])
    m_a = join([((n_a, 0), (f_a_sent, 0))], [((f_a, 0), (n_a_sent, 0))], after=[begun_off])
    m_a_theirs = to_core(m_a)
    (begun_own,) = residual([m_a], [same_a], [0], begun[:1])
    wall_4 = wall(same_c, cross_c, begun_own, cost=WALLS[3])
    p_c, same_d, cross_d = partial(
        [same_c],
        [cross_c],
        halves,
        halves_theirs,
        joined=2,
        behind=[same_b, cross_b],
        after=[wall_4],
    )
    p_c_sent = to_tile(p_c)
    handed_d = to_core(cross_d)
    m_b = join(*[[((p_b, h), (p_b_sent, 1 - h))] for h in range(2)], after=[p_c])
    m_b_theirs = to_core(m_b)
    wall_5 = wall(m_b, cost=WALLS[4])
    rows_b = m_b.shape[1]
    taken = min(-m_a.shape[1] % 256 // 16 * 16, rows_b)
    extra = bool(taken)
    begun = residual(
        [m_a_theirs] + [(m_b, 0, taken)] * extra,
        [handed_a] + [(same_d, 0, taken)] * extra,
        [0, 1],
        [begun_own, begun_off],
        after=[wall_5],
    )
    m_c = join(*[[((p_c, h), (p_c_sent, 1 - h))] for h in range(2)], after=begun)
    m_c_theirs = to_core(m_c)
    middles, vectors = [m_b_theirs], [(handed_d, 0, rows_b)]
    if taken < rows_b:
        middles = [(m_b, taken, rows_b)] + middles
        vectors = [(same_d, taken, rows_b)] + vectors
    begun = residual(middles, vectors, [0, 1], begun, after=[m_c])
    end = same_d.shape[1]
    vectors = [(same_d, rows_b, end), (handed_d, rows_b, end)]
    (out,) = residual([m_c, m_c_theirs], vectors, [0, 1], begun, last=True)
    return out


def from_partner(x, axis, bit):
    return lax.ppermute(x, axis, [(i, i ^ 1 << bit) for i in range(lax.axis_size(axis))])


def any_tiles(amplitudes, cholesky, energy_first, energy_second, energy_virtual):
    pair_count, virtual_count, local_virtual = amplitudes.shape
    tiles_count = lax.axis_size("virt")
    first_count = max(pair_count // OCC, 1)
    second_count = pair_count // first_count
    offset = lax.axis_index("pair") * pair_count
    first_start = offset // OCC
    second_start = offset % OCC
    column_start = lax.axis_index("virt") * local_virtual
    blocks = amplitudes.reshape(pair_count, tiles_count, local_virtual, local_virtual)
    arrived = lax.all_to_all(blocks, "virt", split_axis=1, concat_axis=1, tiled=True)
    mirrored = jnp.swapaxes(arrived, 2, 3).reshape(pair_count, virtual_count, local_virtual)
    combined = (2.0 * amplitudes.astype(F32) - mirrored.astype(F32)).astype(BF16)
    combined = combined.reshape(first_count, second_count, virtual_count, local_virtual)
    vectors = lax.all_gather(cholesky, "pair", axis=2, tiled=True)
    chosen = lax.dynamic_slice_in_dim(vectors, second_start, second_count, 0)
    partial_value = jnp.einsum("ilad,ldq->iaq", combined, chosen, preferred_element_type=F32)
    collected = lax.psum(partial_value.astype(BF16), "virt").astype(F32)
    for bit in range((OCC // second_count).bit_length() - 1):
        collected = collected + from_partner(collected.astype(BF16), "pair", bit).astype(F32)
    reduced = collected.astype(BF16)
    cycle_term = jnp.einsum("iaq,lbq->ilab", reduced, chosen, preferred_element_type=F32)
    first_energy = lax.dynamic_slice_in_dim(energy_first, first_start, first_count, 0)
    second_energy = lax.dynamic_slice_in_dim(energy_second, second_start, second_count, 0)
    column_energy = lax.dynamic_slice_in_dim(energy_virtual, column_start, local_virtual, 0)
    virtual_pairs = energy_virtual[:, None] + column_energy[None, :]
    diagonal = (
        virtual_pairs[None, None, :, :]
        - first_energy[:, None, None, None]
        - second_energy[None, :, None, None]
    )
    values = amplitudes.reshape(first_count, second_count, virtual_count, local_virtual)
    result = diagonal * values.astype(F32) + cycle_term
    return result.reshape(pair_count, virtual_count, local_virtual).astype(BF16)


def on_device(amplitudes, *others):
    ring = lax.axis_size("pair") * amplitudes.shape[0] // OCC
    fits = lax.axis_size("virt") == 2 and amplitudes.shape[0] * 2 == OCC and ring == 8
    return (two_tiles if fits else any_tiles)(amplitudes, *others)


def solution(mesh):
    return jax.shard_map(
        on_device,
        mesh=mesh,
        in_specs=(P("pair", None, "virt"), P(None, "virt", "pair"), P(), P(), P()),
        out_specs=P("pair", None, "virt"),
        check_vma=False,
    )
```

```python
import functools

import jax
import jax.numpy as jnp
from jax import lax
from jax.experimental import pallas as pl
from jax.experimental.pallas import tpu as pltpu
from jax.sharding import PartitionSpec as P

OCC = 8
BF16, F32 = jnp.bfloat16, jnp.float32
VMEM_LIMIT = 20 * 2**20
WALLS = (1, 1, 1, 1, 16)
MIXED = 3
WHOLE = pl.BlockSpec(memory_space=pltpu.VMEM)
ANYWHERE = pl.BlockSpec(memory_space=pl.ANY)


def estimate(cost):
    return pl.CostEstimate(flops=int(cost * 10**9) + 1, bytes_accessed=1, transcendentals=0)


def kernel_call(
    body,
    name,
    grid,
    in_specs,
    out_specs,
    out_shapes,
    scratch=(),
    after=(),
    far=(),
    out=pltpu.VMEM,
    cost=0,
    aliases=None,
):
    extra = len(after)

    def kernel(*refs):
        keep = len(in_specs)
        body(*refs[:keep], *refs[keep + extra :])

    def call(*args):
        held = [
            a if a.ndim == 1 else pltpu.with_memory_space_constraint(a, pltpu.HBM if n in far else pltpu.VMEM)
            for n, a in enumerate((*args, *after))
        ]
        return pl.pallas_call(
            kernel,
            grid=grid,
            in_specs=[*in_specs, *[ANYWHERE] * extra],
            out_specs=list(out_specs),
            scratch_shapes=list(scratch),
            out_shape=[out(shape, kind) for shape, kind in out_shapes],
            compiler_params=pltpu.CompilerParams(
                dimension_semantics=("arbitrary",) * len(grid), vmem_limit_bytes=VMEM_LIMIT
            ),
            cost_estimate=estimate(cost),
            input_output_aliases=aliases or {},
            name=name,
        )(*held)

    return call


def position(count):
    groups = OCC // count
    pair = lax.axis_index("pair")
    return lax.axis_index("virt"), lax.rem(pair, groups), lax.div(pair, groups)


def swap(x, axis, bit):
    return lax.ppermute(x, axis, [(i, i ^ 1 << bit) for i in range(lax.axis_size(axis))])


def ring_of(count, groups):
    places = count // groups
    return list(range(0, places, 2)) + list(range(places - 1, 0, -2))


def along_ring(x, step, groups):
    order = ring_of(lax.axis_size("pair"), groups)
    pairs = [
        (a * groups + g, order[(n + step) % len(order)] * groups + g)
        for n, a in enumerate(order)
        for g in range(groups)
    ]
    return lax.ppermute(x, "pair", pairs)


def turn_kernel(part, amplitudes, near, far, own, own_rows, other, done):
    count, rows, width = near.shape
    tile = lax.axis_index("virt")
    first, second = pl.multiple_of(tile * width, 16), pl.multiple_of((1 - tile) * width, 16)
    columns = pl.ds(part * rows, rows)
    copies = []
    for j in range(count):
        sources = [
            (amplitudes.at[j, pl.ds(first, width), columns], own),
            (amplitudes.at[j, pl.ds(pl.multiple_of(first + part * rows, 16), rows)], own_rows),
            (amplitudes.at[j, pl.ds(second, width), columns], other),
        ]
        for n, (source, held) in enumerate(sources):
            copies.append(pltpu.make_async_copy(source, held.at[j], done.at[n, j]))
            copies[-1].start()
    for j in range(count):
        for copy in copies[3 * j : 3 * j + 3]:
            copy.wait()
        near[j] = (2.0 * own[j].astype(F32).T - own_rows[j].astype(F32)).astype(BF16)
        far[j] = other[j].T


def turn(amplitudes, part, parts, after=()):
    count, _, width = amplitudes.shape
    rows = width // parts
    tall, flat = (count, width, rows), (count, rows, width)
    return kernel_call(
        functools.partial(turn_kernel, part),
        "turn",
        (1,),
        [ANYWHERE],
        [WHOLE] * 2,
        [(flat, BF16)] * 2,
        [
            pltpu.VMEM(tall, BF16),
            pltpu.VMEM(flat, BF16),
            pltpu.VMEM(tall, BF16),
            pltpu.SemaphoreType.DMA((3, count)),
        ],
        after=after,
        far=(0,),
    )(amplitudes)


def cut_kernel(starts, *refs):
    outs, done = refs[-1 - len(starts) : -1], refs[-1]
    tile = lax.axis_index("virt")
    copies = []
    for n, (start, out) in enumerate(zip(starts, outs)):
        at = pl.multiple_of((1 - tile) * out.shape[2] + start, 16)
        source = refs[0].at[:, pl.ds(at, out.shape[1]), :]
        copies.append(pltpu.make_async_copy(source, out, done.at[n]))
    for copy in copies:
        copy.start()
    for copy in copies:
        copy.wait()


def cut(amplitudes, pieces, after=()):
    count, _, width = amplitudes.shape
    return kernel_call(
        functools.partial(cut_kernel, [start for start, _ in pieces]),
        "cut",
        (1,),
        [ANYWHERE],
        [WHOLE] * len(pieces),
        [((count, rows, width), BF16) for _, rows in pieces],
        [pltpu.SemaphoreType.DMA((len(pieces),))],
        after=after,
        far=(0,),
    )(amplitudes)


def mix_kernel(parts, start, at, *refs):
    far, arrived, out = refs[:parts], refs[parts], refs[-1]
    step = far[0].shape[1]
    first, last = 0, arrived.shape[1]
    while first < last:
        part, row = divmod(start + first, step)
        here = min(last - first, step - row)
        value = 2.0 * far[part][:, row : row + here].astype(F32)
        value -= arrived[:, first : first + here].astype(F32)
        out[:, at + first : at + first + here] = value.astype(BF16)
        first += here


def mix(far, arrived, start, rows=None, into=None, after=(), cost=0):
    count, more, width = arrived.shape
    at = start if into is not None else 0
    shape = (count, rows or more, width) if into is None else into.shape
    args = [*far, arrived] + ([] if into is None else [into])
    (out,) = kernel_call(
        functools.partial(mix_kernel, len(far), start, at),
        "mix",
        (1,),
        [WHOLE] * len(args),
        [WHOLE],
        [(shape, BF16)],
        after=after,
        cost=cost,
        aliases=None if into is None else {len(args) - 1: 0},
    )(*args)
    return out


def partial_kernel(shards, parts, joined, extras, *refs):
    same, cross = refs[:shards], refs[shards : 2 * shards]
    refs = refs[2 * shards :]
    arrays = sum(parts)
    mine, theirs, refs = refs[:arrays], refs[arrays : 2 * arrays], refs[2 * arrays :]
    extra, outs = refs[:extras], refs[extras:]
    count = mine[0].shape[0]
    _, group, _ = position(count)

    def together(arrays, j, group=0):
        pieces = [r[j + (group * count if r.shape[0] > count else 0)] for r in arrays]
        return jnp.concatenate(pieces, axis=0) if len(pieces) > 1 else pieces[0]

    totals = [None] * len(parts)
    for j in range(count):
        left, right = together(same, j, group), together(cross, j, 1 - group)
        for n in range(joined):
            value = (left, right)[n - joined]
            outs[1 + n][j] = jnp.concatenate([extra[n][j], value], axis=0) if extras else value
        at = 0
        for h, split in enumerate(parts):
            for shard, half in ((left, mine), (right, theirs)):
                half = together(half[at : at + split], j)
                value = jnp.dot(shard, half, preferred_element_type=F32)
                totals[h] = value if totals[h] is None else totals[h] + value
            at += split
    for h, total in enumerate(totals):
        outs[0][h] = total.astype(BF16)


def partial(same, cross, mine, theirs, joined=0, behind=(), after=()):
    parts = [len(m) for m in mine]
    shards, halves = len(same), len(mine)
    count, _, columns = mine[0][0].shape
    width = same[0].shape[2]
    rows = sum(v.shape[1] for v in same)
    args = [*same, *cross, *sum(mine, []), *sum(theirs, []), *behind]
    out_shapes = [((halves, rows, columns), BF16)]
    for n in range(joined):
        more = rows + (behind[n].shape[1] if behind else 0)
        out_shapes.append(((count, more, width), BF16))
    return kernel_call(
        functools.partial(partial_kernel, shards, parts, joined, len(behind)),
        "partial",
        (1,),
        [WHOLE] * len(args),
        [WHOLE] * len(out_shapes),
        out_shapes,
        after=after,
    )(*args)


def pick_kernel(forth, back, same, cross):
    count = same.shape[0]
    _, group, _ = position(count)
    for j in range(count):
        same[j] = forth[group * count + j]
        cross[j] = back[(1 - group) * count + j]


def pick(forth, back, after=()):
    shape = (forth.shape[0] // 2,) + forth.shape[1:]
    return kernel_call(
        pick_kernel, "pick", (1,), [WHOLE] * 2, [WHOLE] * 2, [(shape, BF16)] * 2, after=after
    )(forth, back)


def nothing(*refs):
    pass


def wall(*arrays, cost=0.1):
    held = [pltpu.with_memory_space_constraint(a, pltpu.VMEM) for a in arrays]
    return pl.pallas_call(
        nothing,
        in_specs=[ANYWHERE] * len(held),
        out_specs=ANYWHERE,
        out_shape=pltpu.VMEM((8, 128), F32),
        compiler_params=pltpu.CompilerParams(vmem_limit_bytes=2**20),
        cost_estimate=estimate(cost),
        name="wall",
    )(*held)


def join_kernel(counts, *refs):
    out, at = refs[-1], 0
    for h, count in enumerate(counts):
        own, sent = refs[at : at + count], refs[at + count : at + 2 * count]
        at += 2 * count
        left, right = [
            jnp.concatenate([r[...] for r in v], axis=0) if count > 1 else v[0][...]
            for v in (own, sent)
        ]
        out[h] = (left.astype(F32) + right.astype(F32)).astype(BF16)


def join(*halves, after=()):
    args, in_specs = [], []
    for pairs in halves:
        for side in range(2):
            for pair in pairs:
                v, h = pair[side]
                args.append(v)
                in_specs.append(pl.BlockSpec((None,) + v.shape[1:], functools.partial(lambda h, k: (h, 0, 0), h)))
    rows = sum(pair[0][0].shape[1] for pair in halves[0])
    shape = (len(halves), rows, args[0].shape[2])
    (out,) = kernel_call(
        functools.partial(join_kernel, [len(pairs) for pairs in halves]),
        "join",
        (1,),
        in_specs,
        [WHOLE],
        [(shape, BF16)],
        after=after,
    )(*args)
    return out


def joined_rows(pieces):
    return jnp.concatenate(pieces, axis=0) if len(pieces) > 1 else pieces[0]


def diagonal_kernel(values, energy, first_energy, second_energy, own, off, held, done):
    count, columns, width = own.shape
    here, group, place = position(count)
    copies = []
    for h in range(2):
        tile = lax.rem(here + h, 2)
        rows = pl.ds(pl.multiple_of(tile * columns, 16), columns)
        for j in range(count):
            copies.append(pltpu.make_async_copy(values.at[j, rows], held.at[h, j], done.at[h, j]))
            copies[-1].start()
    for h, out in enumerate((own, off)):
        row_energy = energy[lax.rem(here + h, 2)]
        row_energy = jnp.broadcast_to(row_energy, (128, columns)).T[:, :1]
        for j in range(count):
            occupied = first_energy[place] + second_energy[group * count + j]
            copies[h * count + j].wait()
            out[j] = (row_energy - occupied + energy[here]) * held[h, j].astype(F32)


def diagonal(amplitudes, energy_virtual, energy_first, energy_second, after=()):
    count, rows, width = amplitudes.shape
    block = (count, rows // 2, width)
    return kernel_call(
        diagonal_kernel,
        "diagonal",
        (1,),
        [ANYWHERE, WHOLE] + [pl.BlockSpec(memory_space=pltpu.SMEM)] * 2,
        [WHOLE] * 2,
        [(block, F32)] * 2,
        [pltpu.VMEM((2,) + block, BF16), pltpu.SemaphoreType.DMA((2, count))],
        after=after,
        far=(0,),
    )(amplitudes, energy_virtual.reshape(2, 1, width), energy_first, energy_second)


def residual_kernel(rows_of, depths_of, halves, last, *refs):
    chunks, shards = len(rows_of), len(depths_of)
    middles, vectors, refs = refs[:chunks], refs[chunks : chunks + shards], refs[chunks + shards :]
    count, _, width = vectors[0].shape
    before, outs = refs[: len(halves)], refs[len(halves) :]
    if last:
        out, held, done = outs
    columns = middles[0].shape[2]
    copies = []
    for n, h in enumerate(halves):
        rows = pl.ds(pl.multiple_of(lax.rem(lax.axis_index("virt") + h, 2) * columns, 16), columns)
        parts = [m[h if m.shape[0] > 1 else 0, a:b] for m, (a, b) in zip(middles, rows_of)]
        left = joined_rows(parts).T
        for j in range(count):
            right = joined_rows([v[j, a:b] for v, (a, b) in zip(vectors, depths_of)])
            total = jnp.dot(left, right, preferred_element_type=F32)
            total += before[n][j]
            if last:
                held[n, j] = total.astype(BF16)
                copies.append(pltpu.make_async_copy(held.at[n, j], out.at[j, rows], done.at[n, j]))
                copies[-1].start()
            else:
                outs[n][j] = total
    for copy in copies:
        copy.wait()


def residual(middles, vectors, halves, before, last=False, after=()):
    whole = lambda v: v if isinstance(v, tuple) else (v, 0, v.shape[1])
    middles, rows_of = zip(*[(v, (a, b)) for v, a, b in map(whole, middles)])
    vectors, depths_of = zip(*[(v, (a, b)) for v, a, b in map(whole, vectors)])
    count, _, width = vectors[0].shape
    block = (count, middles[0].shape[2], width)
    args = [*middles, *vectors, *before]
    out_shapes, scratch = [(block, F32)] * len(halves), []
    if last:
        out_shapes = [((count, 2 * block[1], width), BF16)]
        scratch = [pltpu.VMEM((2,) + block, BF16), pltpu.SemaphoreType.DMA((2, count))]
    return kernel_call(
        functools.partial(residual_kernel, rows_of, depths_of, halves, last),
        "residual",
        (1,),
        [WHOLE] * len(args),
        [ANYWHERE if last else WHOLE] * len(out_shapes),
        out_shapes,
        scratch,
        after=after,
        out=pltpu.HBM if last else pltpu.VMEM,
    )(*args)


def two_tiles(amplitudes, cholesky, energy_first, energy_second, energy_virtual):
    count, virtual, width = amplitudes.shape
    groups = OCC // count
    places = lax.axis_size("pair") // groups
    ring = functools.partial(along_ring, groups=groups)
    to_core = functools.partial(swap, axis="pair", bit=0)
    to_tile = functools.partial(swap, axis="virt", bit=0)

    unit = width // 32
    pieces = [(0, 15 * unit), (15 * unit, 13 * unit), (28 * unit, 4 * unit)]
    sent = cut(amplitudes, pieces[:1])
    sent += cut(amplitudes, pieces[1:], after=sent)
    arrived = [to_tile(v) for v in sent]

    own = jnp.swapaxes(cholesky, 1, 2)
    vectors = [own]
    forth, back = own, own
    for step in range(1, places // 2):
        forth, back = ring(forth, 1), ring(back, -1)
        vectors += [forth, back]

    near, near_theirs, far_turned = [], [], []
    held = sent[1:]
    parts = 4
    for part in range(parts):
        v, w = turn(amplitudes, part, parts, after=held)
        near.append(v)
        far_turned.append(w)
        near_theirs.append(to_core(v))
        if part == parts // 2 - 1:
            wall_1 = wall(*vectors[1:3], arrived[0], *near_theirs, cost=WALLS[0])
            held = [wall_1]
    begun = diagonal(amplitudes, energy_virtual, energy_first, energy_second, after=near)
    cut_at, cut_end = (sum(v.shape[1] for v in sent[:n]) for n in (1, 2))
    far_0 = mix(far_turned, arrived[0], 0, rows=cut_end, after=begun)
    wall_2 = wall(
        *vectors[3:5], arrived[1], *near_theirs[parts // 2 :], far_0, cost=WALLS[1]
    )
    far_0 = mix(far_turned, arrived[1], cut_at, into=far_0, after=[wall_2])
    far_0_theirs = to_core(far_0)
    near, near_theirs = [near], [near_theirs]
    n_a, same_a, cross_a = partial(
        vectors[:5], vectors[:5], near, near_theirs, joined=2, after=[far_0]
    )
    n_a_sent = to_tile(n_a)
    far_1 = mix(far_turned, arrived[2], far_0.shape[1], after=[n_a], cost=MIXED)
    far_1_theirs = to_core(far_1)
    far, far_theirs = [far_0, far_1], [far_0_theirs, far_1_theirs]
    f_a, cross_a = partial([same_a], [cross_a], [far], [far_theirs], joined=1)
    f_a_sent = to_tile(f_a)
    handed_a = to_core(cross_a)
    picked = pick(*vectors[5:7], after=[f_a, n_a_sent])
    same_c, cross_c = ring(picked[0], 1), ring(picked[1], -1)
    wall_3 = wall(*picked, cost=WALLS[2])
    halves, halves_theirs = near + [far], near_theirs + [far_theirs]
    p_b, same_b, cross_b = partial(
        vectors[5:7], vectors[5:7], halves, halves_theirs, joined=2, after=[wall_3]
    )
    p_b_sent = to_tile(p_b)
    m_off = join([((f_a, 0), (n_a_sent, 0))], after=[p_b])
    (begun_off,) = residual([m_off], [same_a], [1], begun[1:])
    m_a = join([((n_a, 0), (f_a_sent, 0))], [((f_a, 0), (n_a_sent, 0))], after=[begun_off])
    m_a_theirs = to_core(m_a)
    (begun_own,) = residual([m_a], [same_a], [0], begun[:1])
    wall_4 = wall(same_c, cross_c, begun_own, cost=WALLS[3])
    p_c, same_d, cross_d = partial(
        [same_c],
        [cross_c],
        halves,
        halves_theirs,
        joined=2,
        behind=[same_b, cross_b],
        after=[wall_4],
    )
    p_c_sent = to_tile(p_c)
    handed_d = to_core(cross_d)
    m_b = join(*[[((p_b, h), (p_b_sent, 1 - h))] for h in range(2)], after=[p_c])
    m_b_theirs = to_core(m_b)
    wall_5 = wall(m_b, cost=WALLS[4])
    rows_b = m_b.shape[1]
    taken = min(-m_a.shape[1] % 256 // 16 * 16, rows_b)
    extra = bool(taken)
    begun = residual(
        [m_a_theirs] + [(m_b, 0, taken)] * extra,
        [handed_a] + [(same_d, 0, taken)] * extra,
        [0, 1],
        [begun_own, begun_off],
        after=[wall_5],
    )
    m_c = join(*[[((p_c, h), (p_c_sent, 1 - h))] for h in range(2)], after=begun)
    m_c_theirs = to_core(m_c)
    middles, vectors = [m_b_theirs], [(handed_d, 0, rows_b)]
    if taken < rows_b:
        middles = [(m_b, taken, rows_b)] + middles
        vectors = [(same_d, taken, rows_b)] + vectors
    begun = residual(middles, vectors, [0, 1], begun, after=[m_c])
    end = same_d.shape[1]
    vectors = [(same_d, rows_b, end), (handed_d, rows_b, end)]
    (out,) = residual([m_c, m_c_theirs], vectors, [0, 1], begun, last=True)
    return out


def from_partner(x, axis, bit):
    return lax.ppermute(x, axis, [(i, i ^ 1 << bit) for i in range(lax.axis_size(axis))])


def any_tiles(amplitudes, cholesky, energy_first, energy_second, energy_virtual):
    pair_count, virtual_count, local_virtual = amplitudes.shape
    tiles_count = lax.axis_size("virt")
    first_count = max(pair_count // OCC, 1)
    second_count = pair_count // first_count
    offset = lax.axis_index("pair") * pair_count
    first_start = offset // OCC
    second_start = offset % OCC
    column_start = lax.axis_index("virt") * local_virtual
    blocks = amplitudes.reshape(pair_count, tiles_count, local_virtual, local_virtual)
    arrived = lax.all_to_all(blocks, "virt", split_axis=1, concat_axis=1, tiled=True)
    mirrored = jnp.swapaxes(arrived, 2, 3).reshape(pair_count, virtual_count, local_virtual)
    combined = (2.0 * amplitudes.astype(F32) - mirrored.astype(F32)).astype(BF16)
    combined = combined.reshape(first_count, second_count, virtual_count, local_virtual)
    vectors = lax.all_gather(cholesky, "pair", axis=2, tiled=True)
    chosen = lax.dynamic_slice_in_dim(vectors, second_start, second_count, 0)
    partial_value = jnp.einsum("ilad,ldq->iaq", combined, chosen, preferred_element_type=F32)
    collected = lax.psum(partial_value.astype(BF16), "virt").astype(F32)
    for bit in range((OCC // second_count).bit_length() - 1):
        collected = collected + from_partner(collected.astype(BF16), "pair", bit).astype(F32)
    reduced = collected.astype(BF16)
    cycle_term = jnp.einsum("iaq,lbq->ilab", reduced, chosen, preferred_element_type=F32)
    first_energy = lax.dynamic_slice_in_dim(energy_first, first_start, first_count, 0)
    second_energy = lax.dynamic_slice_in_dim(energy_second, second_start, second_count, 0)
    column_energy = lax.dynamic_slice_in_dim(energy_virtual, column_start, local_virtual, 0)
    virtual_pairs = energy_virtual[:, None] + column_energy[None, :]
    diagonal = (
        virtual_pairs[None, None, :, :]
        - first_energy[:, None, None, None]
        - second_energy[None, :, None, None]
    )
    values = amplitudes.reshape(first_count, second_count, virtual_count, local_virtual)
    result = diagonal * values.astype(F32) + cycle_term
    return result.reshape(pair_count, virtual_count, local_virtual).astype(BF16)


def on_device(amplitudes, *others):
    ring = lax.axis_size("pair") * amplitudes.shape[0] // OCC
    fits = lax.axis_size("virt") == 2 and amplitudes.shape[0] * 2 == OCC and ring == 8
    return (two_tiles if fits else any_tiles)(amplitudes, *others)


def solution(mesh):
    return jax.shard_map(
        on_device,
        mesh=mesh,
        in_specs=(P("pair", None, "virt"), P(None, "virt", "pair"), P(), P(), P()),
        out_specs=P("pair", None, "virt"),
        check_vma=False,
    )
```

```python
import functools

import jax
import jax.numpy as jnp
from jax import lax
from jax.experimental import pallas as pl
from jax.experimental.pallas import tpu as pltpu
from jax.sharding import PartitionSpec as P

OCC = 8
BF16, F32 = jnp.bfloat16, jnp.float32
VMEM_LIMIT = 20 * 2**20
WALLS = (1, 1, 1, 1, 16)
MIXED = 3
WHOLE = pl.BlockSpec(memory_space=pltpu.VMEM)
ANYWHERE = pl.BlockSpec(memory_space=pl.ANY)


def estimate(cost):
    return pl.CostEstimate(flops=int(cost * 10**9) + 1, bytes_accessed=1, transcendentals=0)


def kernel_call(
    body,
    name,
    grid,
    in_specs,
    out_specs,
    out_shapes,
    scratch=(),
    after=(),
    far=(),
    out=pltpu.VMEM,
    cost=0,
    aliases=None,
):
    extra = len(after)

    def kernel(*refs):
        keep = len(in_specs)
        body(*refs[:keep], *refs[keep + extra :])

    def call(*args):
        held = [
            a if a.ndim == 1 else pltpu.with_memory_space_constraint(a, pltpu.HBM if n in far else pltpu.VMEM)
            for n, a in enumerate((*args, *after))
        ]
        return pl.pallas_call(
            kernel,
            grid=grid,
            in_specs=[*in_specs, *[ANYWHERE] * extra],
            out_specs=list(out_specs),
            scratch_shapes=list(scratch),
            out_shape=[out(shape, kind) for shape, kind in out_shapes],
            compiler_params=pltpu.CompilerParams(
                dimension_semantics=("arbitrary",) * len(grid), vmem_limit_bytes=VMEM_LIMIT
            ),
            cost_estimate=estimate(cost),
            input_output_aliases=aliases or {},
            name=name,
        )(*held)

    return call


def position(count):
    groups = OCC // count
    pair = lax.axis_index("pair")
    return lax.axis_index("virt"), lax.rem(pair, groups), lax.div(pair, groups)


def swap(x, axis, bit):
    return lax.ppermute(x, axis, [(i, i ^ 1 << bit) for i in range(lax.axis_size(axis))])


def ring_of(count, groups):
    places = count // groups
    return list(range(0, places, 2)) + list(range(places - 1, 0, -2))


def along_ring(x, step, groups):
    order = ring_of(lax.axis_size("pair"), groups)
    pairs = [
        (a * groups + g, order[(n + step) % len(order)] * groups + g)
        for n, a in enumerate(order)
        for g in range(groups)
    ]
    return lax.ppermute(x, "pair", pairs)


def turn_kernel(part, amplitudes, near, far, own, own_rows, other, done):
    count, rows, width = near.shape
    tile = lax.axis_index("virt")
    first, second = pl.multiple_of(tile * width, 16), pl.multiple_of((1 - tile) * width, 16)
    columns = pl.ds(part * rows, rows)
    copies = []
    for j in range(count):
        sources = [
            (amplitudes.at[j, pl.ds(first, width), columns], own),
            (amplitudes.at[j, pl.ds(pl.multiple_of(first + part * rows, 16), rows)], own_rows),
            (amplitudes.at[j, pl.ds(second, width), columns], other),
        ]
        for n, (source, held) in enumerate(sources):
            copies.append(pltpu.make_async_copy(source, held.at[j], done.at[n, j]))
            copies[-1].start()
    for j in range(count):
        for copy in copies[3 * j : 3 * j + 3]:
            copy.wait()
        near[j] = (2.0 * own[j].astype(F32).T - own_rows[j].astype(F32)).astype(BF16)
        far[j] = other[j].T


def turn(amplitudes, part, parts, after=()):
    count, _, width = amplitudes.shape
    rows = width // parts
    tall, flat = (count, width, rows), (count, rows, width)
    return kernel_call(
        functools.partial(turn_kernel, part),
        "turn",
        (1,),
        [ANYWHERE],
        [WHOLE] * 2,
        [(flat, BF16)] * 2,
        [
            pltpu.VMEM(tall, BF16),
            pltpu.VMEM(flat, BF16),
            pltpu.VMEM(tall, BF16),
            pltpu.SemaphoreType.DMA((3, count)),
        ],
        after=after,
        far=(0,),
    )(amplitudes)


def cut_kernel(starts, *refs):
    outs, done = refs[-1 - len(starts) : -1], refs[-1]
    tile = lax.axis_index("virt")
    copies = []
    for n, (start, out) in enumerate(zip(starts, outs)):
        at = pl.multiple_of((1 - tile) * out.shape[2] + start, 16)
        source = refs[0].at[:, pl.ds(at, out.shape[1]), :]
        copies.append(pltpu.make_async_copy(source, out, done.at[n]))
    for copy in copies:
        copy.start()
    for copy in copies:
        copy.wait()


def cut(amplitudes, pieces, after=()):
    count, _, width = amplitudes.shape
    return kernel_call(
        functools.partial(cut_kernel, [start for start, _ in pieces]),
        "cut",
        (1,),
        [ANYWHERE],
        [WHOLE] * len(pieces),
        [((count, rows, width), BF16) for _, rows in pieces],
        [pltpu.SemaphoreType.DMA((len(pieces),))],
        after=after,
        far=(0,),
    )(amplitudes)


def mix_kernel(parts, start, at, *refs):
    far, arrived, out = refs[:parts], refs[parts], refs[-1]
    step = far[0].shape[1]
    first, last = 0, arrived.shape[1]
    while first < last:
        part, row = divmod(start + first, step)
        here = min(last - first, step - row)
        value = 2.0 * far[part][:, row : row + here].astype(F32)
        value -= arrived[:, first : first + here].astype(F32)
        out[:, at + first : at + first + here] = value.astype(BF16)
        first += here


def mix(far, arrived, start, rows=None, into=None, after=(), cost=0):
    count, more, width = arrived.shape
    at = start if into is not None else 0
    shape = (count, rows or more, width) if into is None else into.shape
    args = [*far, arrived] + ([] if into is None else [into])
    (out,) = kernel_call(
        functools.partial(mix_kernel, len(far), start, at),
        "mix",
        (1,),
        [WHOLE] * len(args),
        [WHOLE],
        [(shape, BF16)],
        after=after,
        cost=cost,
        aliases=None if into is None else {len(args) - 1: 0},
    )(*args)
    return out


def partial_kernel(shards, parts, joined, extras, *refs):
    same, cross = refs[:shards], refs[shards : 2 * shards]
    refs = refs[2 * shards :]
    arrays = sum(parts)
    mine, theirs, refs = refs[:arrays], refs[arrays : 2 * arrays], refs[2 * arrays :]
    extra, outs = refs[:extras], refs[extras:]
    count = mine[0].shape[0]
    _, group, _ = position(count)

    def together(arrays, j, group=0):
        pieces = [r[j + (group * count if r.shape[0] > count else 0)] for r in arrays]
        return jnp.concatenate(pieces, axis=0) if len(pieces) > 1 else pieces[0]

    totals = [None] * len(parts)
    for j in range(count):
        left, right = together(same, j, group), together(cross, j, 1 - group)
        for n in range(joined):
            value = (left, right)[n - joined]
            outs[1 + n][j] = jnp.concatenate([extra[n][j], value], axis=0) if extras else value
        at = 0
        for h, split in enumerate(parts):
            for shard, half in ((left, mine), (right, theirs)):
                half = together(half[at : at + split], j)
                value = jnp.dot(shard, half, preferred_element_type=F32)
                totals[h] = value if totals[h] is None else totals[h] + value
            at += split
    for h, total in enumerate(totals):
        outs[0][h] = total.astype(BF16)


def partial(same, cross, mine, theirs, joined=0, behind=(), after=()):
    parts = [len(m) for m in mine]
    shards, halves = len(same), len(mine)
    count, _, columns = mine[0][0].shape
    width = same[0].shape[2]
    rows = sum(v.shape[1] for v in same)
    args = [*same, *cross, *sum(mine, []), *sum(theirs, []), *behind]
    out_shapes = [((halves, rows, columns), BF16)]
    for n in range(joined):
        more = rows + (behind[n].shape[1] if behind else 0)
        out_shapes.append(((count, more, width), BF16))
    return kernel_call(
        functools.partial(partial_kernel, shards, parts, joined, len(behind)),
        "partial",
        (1,),
        [WHOLE] * len(args),
        [WHOLE] * len(out_shapes),
        out_shapes,
        after=after,
    )(*args)


def pick_kernel(forth, back, same, cross):
    count = same.shape[0]
    _, group, _ = position(count)
    for j in range(count):
        same[j] = forth[group * count + j]
        cross[j] = back[(1 - group) * count + j]


def pick(forth, back, after=()):
    shape = (forth.shape[0] // 2,) + forth.shape[1:]
    return kernel_call(
        pick_kernel, "pick", (1,), [WHOLE] * 2, [WHOLE] * 2, [(shape, BF16)] * 2, after=after
    )(forth, back)


def nothing(*refs):
    pass


def wall(*arrays, cost=0.1):
    held = [pltpu.with_memory_space_constraint(a, pltpu.VMEM) for a in arrays]
    return pl.pallas_call(
        nothing,
        in_specs=[ANYWHERE] * len(held),
        out_specs=ANYWHERE,
        out_shape=pltpu.VMEM((8, 128), F32),
        compiler_params=pltpu.CompilerParams(vmem_limit_bytes=2**20),
        cost_estimate=estimate(cost),
        name="wall",
    )(*held)


def join_kernel(counts, *refs):
    out, at = refs[-1], 0
    for h, count in enumerate(counts):
        own, sent = refs[at : at + count], refs[at + count : at + 2 * count]
        at += 2 * count
        left, right = [
            jnp.concatenate([r[...] for r in v], axis=0) if count > 1 else v[0][...]
            for v in (own, sent)
        ]
        out[h] = (left.astype(F32) + right.astype(F32)).astype(BF16)


def join(*halves, after=()):
    args, in_specs = [], []
    for pairs in halves:
        for side in range(2):
            for pair in pairs:
                v, h = pair[side]
                args.append(v)
                in_specs.append(pl.BlockSpec((None,) + v.shape[1:], functools.partial(lambda h, k: (h, 0, 0), h)))
    rows = sum(pair[0][0].shape[1] for pair in halves[0])
    shape = (len(halves), rows, args[0].shape[2])
    (out,) = kernel_call(
        functools.partial(join_kernel, [len(pairs) for pairs in halves]),
        "join",
        (1,),
        in_specs,
        [WHOLE],
        [(shape, BF16)],
        after=after,
    )(*args)
    return out


def joined_rows(pieces):
    return jnp.concatenate(pieces, axis=0) if len(pieces) > 1 else pieces[0]


def diagonal_kernel(values, energy, first_energy, second_energy, own, off, held, done):
    count, columns, width = own.shape
    here, group, place = position(count)
    copies = []
    for h in range(2):
        tile = lax.rem(here + h, 2)
        rows = pl.ds(pl.multiple_of(tile * columns, 16), columns)
        for j in range(count):
            copies.append(pltpu.make_async_copy(values.at[j, rows], held.at[h, j], done.at[h, j]))
            copies[-1].start()
    for h, out in enumerate((own, off)):
        row_energy = energy[lax.rem(here + h, 2)]
        row_energy = jnp.broadcast_to(row_energy, (128, columns)).T[:, :1]
        for j in range(count):
            occupied = first_energy[place] + second_energy[group * count + j]
            copies[h * count + j].wait()
            out[j] = (row_energy - occupied + energy[here]) * held[h, j].astype(F32)


def diagonal(amplitudes, energy_virtual, energy_first, energy_second, after=()):
    count, rows, width = amplitudes.shape
    block = (count, rows // 2, width)
    return kernel_call(
        diagonal_kernel,
        "diagonal",
        (1,),
        [ANYWHERE, WHOLE] + [pl.BlockSpec(memory_space=pltpu.SMEM)] * 2,
        [WHOLE] * 2,
        [(block, F32)] * 2,
        [pltpu.VMEM((2,) + block, BF16), pltpu.SemaphoreType.DMA((2, count))],
        after=after,
        far=(0,),
    )(amplitudes, energy_virtual.reshape(2, 1, width), energy_first, energy_second)


def residual_kernel(rows_of, depths_of, halves, last, *refs):
    chunks, shards = len(rows_of), len(depths_of)
    middles, vectors, refs = refs[:chunks], refs[chunks : chunks + shards], refs[chunks + shards :]
    count, _, width = vectors[0].shape
    before, outs = refs[: len(halves)], refs[len(halves) :]
    if last:
        out, held, done = outs
    columns = middles[0].shape[2]
    copies = []
    for n, h in enumerate(halves):
        rows = pl.ds(pl.multiple_of(lax.rem(lax.axis_index("virt") + h, 2) * columns, 16), columns)
        parts = [m[h if m.shape[0] > 1 else 0, a:b] for m, (a, b) in zip(middles, rows_of)]
        left = joined_rows(parts).T
        for j in range(count):
            right = joined_rows([v[j, a:b] for v, (a, b) in zip(vectors, depths_of)])
            total = jnp.dot(left, right, preferred_element_type=F32)
            total += before[n][j]
            if last:
                held[n, j] = total.astype(BF16)
                copies.append(pltpu.make_async_copy(held.at[n, j], out.at[j, rows], done.at[n, j]))
                copies[-1].start()
            else:
                outs[n][j] = total
    for copy in copies:
        copy.wait()


def residual(middles, vectors, halves, before, last=False, after=()):
    whole = lambda v: v if isinstance(v, tuple) else (v, 0, v.shape[1])
    middles, rows_of = zip(*[(v, (a, b)) for v, a, b in map(whole, middles)])
    vectors, depths_of = zip(*[(v, (a, b)) for v, a, b in map(whole, vectors)])
    count, _, width = vectors[0].shape
    block = (count, middles[0].shape[2], width)
    args = [*middles, *vectors, *before]
    out_shapes, scratch = [(block, F32)] * len(halves), []
    if last:
        out_shapes = [((count, 2 * block[1], width), BF16)]
        scratch = [pltpu.VMEM((2,) + block, BF16), pltpu.SemaphoreType.DMA((2, count))]
    return kernel_call(
        functools.partial(residual_kernel, rows_of, depths_of, halves, last),
        "residual",
        (1,),
        [WHOLE] * len(args),
        [ANYWHERE if last else WHOLE] * len(out_shapes),
        out_shapes,
        scratch,
        after=after,
        out=pltpu.HBM if last else pltpu.VMEM,
    )(*args)


def two_tiles(amplitudes, cholesky, energy_first, energy_second, energy_virtual):
    count, virtual, width = amplitudes.shape
    groups = OCC // count
    places = lax.axis_size("pair") // groups
    ring = functools.partial(along_ring, groups=groups)
    to_core = functools.partial(swap, axis="pair", bit=0)
    to_tile = functools.partial(swap, axis="virt", bit=0)

    unit = width // 32
    pieces = [(0, 17 * unit), (17 * unit, 11 * unit), (28 * unit, 4 * unit)]
    sent = cut(amplitudes, pieces[:1])
    sent += cut(amplitudes, pieces[1:], after=sent)
    arrived = [to_tile(v) for v in sent]

    own = jnp.swapaxes(cholesky, 1, 2)
    vectors = [own]
    forth, back = own, own
    for step in range(1, places // 2):
        forth, back = ring(forth, 1), ring(back, -1)
        vectors += [forth, back]

    near, near_theirs, far_turned = [], [], []
    held = sent[1:]
    parts = 4
    for part in range(parts):
        v, w = turn(amplitudes, part, parts, after=held)
        near.append(v)
        far_turned.append(w)
        near_theirs.append(to_core(v))
        if part == parts // 2 - 1:
            wall_1 = wall(*vectors[1:3], arrived[0], *near_theirs, cost=WALLS[0])
            held = [wall_1]
    begun = diagonal(amplitudes, energy_virtual, energy_first, energy_second, after=near)
    cut_at, cut_end = (sum(v.shape[1] for v in sent[:n]) for n in (1, 2))
    far_0 = mix(far_turned, arrived[0], 0, rows=cut_end, after=begun)
    wall_2 = wall(
        *vectors[3:5], arrived[1], *near_theirs[parts // 2 :], far_0, cost=WALLS[1]
    )
    far_0 = mix(far_turned, arrived[1], cut_at, into=far_0, after=[wall_2])
    far_0_theirs = to_core(far_0)
    near, near_theirs = [near], [near_theirs]
    n_a, same_a, cross_a = partial(
        vectors[:5], vectors[:5], near, near_theirs, joined=2, after=[far_0]
    )
    n_a_sent = to_tile(n_a)
    far_1 = mix(far_turned, arrived[2], far_0.shape[1], after=[n_a], cost=MIXED)
    far_1_theirs = to_core(far_1)
    far, far_theirs = [far_0, far_1], [far_0_theirs, far_1_theirs]
    f_a, cross_a = partial([same_a], [cross_a], [far], [far_theirs], joined=1)
    f_a_sent = to_tile(f_a)
    handed_a = to_core(cross_a)
    picked = pick(*vectors[5:7], after=[f_a, n_a_sent])
    same_c, cross_c = ring(picked[0], 1), ring(picked[1], -1)
    wall_3 = wall(*picked, cost=WALLS[2])
    halves, halves_theirs = near + [far], near_theirs + [far_theirs]
    p_b, same_b, cross_b = partial(
        vectors[5:7], vectors[5:7], halves, halves_theirs, joined=2, after=[wall_3]
    )
    p_b_sent = to_tile(p_b)
    m_off = join([((f_a, 0), (n_a_sent, 0))], after=[p_b])
    (begun_off,) = residual([m_off], [same_a], [1], begun[1:])
    m_a = join([((n_a, 0), (f_a_sent, 0))], [((f_a, 0), (n_a_sent, 0))], after=[begun_off])
    m_a_theirs = to_core(m_a)
    (begun_own,) = residual([m_a], [same_a], [0], begun[:1])
    wall_4 = wall(same_c, cross_c, begun_own, cost=WALLS[3])
    p_c, same_d, cross_d = partial(
        [same_c],
        [cross_c],
        halves,
        halves_theirs,
        joined=2,
        behind=[same_b, cross_b],
        after=[wall_4],
    )
    p_c_sent = to_tile(p_c)
    handed_d = to_core(cross_d)
    m_b = join(*[[((p_b, h), (p_b_sent, 1 - h))] for h in range(2)], after=[p_c])
    m_b_theirs = to_core(m_b)
    wall_5 = wall(m_b, cost=WALLS[4])
    rows_b = m_b.shape[1]
    taken = min(-m_a.shape[1] % 256 // 16 * 16, rows_b)
    extra = bool(taken)
    begun = residual(
        [m_a_theirs] + [(m_b, 0, taken)] * extra,
        [handed_a] + [(same_d, 0, taken)] * extra,
        [0, 1],
        [begun_own, begun_off],
        after=[wall_5],
    )
    m_c = join(*[[((p_c, h), (p_c_sent, 1 - h))] for h in range(2)], after=begun)
    m_c_theirs = to_core(m_c)
    middles, vectors = [m_b_theirs], [(handed_d, 0, rows_b)]
    if taken < rows_b:
        middles = [(m_b, taken, rows_b)] + middles
        vectors = [(same_d, taken, rows_b)] + vectors
    begun = residual(middles, vectors, [0, 1], begun, after=[m_c])
    end = same_d.shape[1]
    vectors = [(same_d, rows_b, end), (handed_d, rows_b, end)]
    (out,) = residual([m_c, m_c_theirs], vectors, [0, 1], begun, last=True)
    return out


def from_partner(x, axis, bit):
    return lax.ppermute(x, axis, [(i, i ^ 1 << bit) for i in range(lax.axis_size(axis))])


def any_tiles(amplitudes, cholesky, energy_first, energy_second, energy_virtual):
    pair_count, virtual_count, local_virtual = amplitudes.shape
    tiles_count = lax.axis_size("virt")
    first_count = max(pair_count // OCC, 1)
    second_count = pair_count // first_count
    offset = lax.axis_index("pair") * pair_count
    first_start = offset // OCC
    second_start = offset % OCC
    column_start = lax.axis_index("virt") * local_virtual
    blocks = amplitudes.reshape(pair_count, tiles_count, local_virtual, local_virtual)
    arrived = lax.all_to_all(blocks, "virt", split_axis=1, concat_axis=1, tiled=True)
    mirrored = jnp.swapaxes(arrived, 2, 3).reshape(pair_count, virtual_count, local_virtual)
    combined = (2.0 * amplitudes.astype(F32) - mirrored.astype(F32)).astype(BF16)
    combined = combined.reshape(first_count, second_count, virtual_count, local_virtual)
    vectors = lax.all_gather(cholesky, "pair", axis=2, tiled=True)
    chosen = lax.dynamic_slice_in_dim(vectors, second_start, second_count, 0)
    partial_value = jnp.einsum("ilad,ldq->iaq", combined, chosen, preferred_element_type=F32)
    collected = lax.psum(partial_value.astype(BF16), "virt").astype(F32)
    for bit in range((OCC // second_count).bit_length() - 1):
        collected = collected + from_partner(collected.astype(BF16), "pair", bit).astype(F32)
    reduced = collected.astype(BF16)
    cycle_term = jnp.einsum("iaq,lbq->ilab", reduced, chosen, preferred_element_type=F32)
    first_energy = lax.dynamic_slice_in_dim(energy_first, first_start, first_count, 0)
    second_energy = lax.dynamic_slice_in_dim(energy_second, second_start, second_count, 0)
    column_energy = lax.dynamic_slice_in_dim(energy_virtual, column_start, local_virtual, 0)
    virtual_pairs = energy_virtual[:, None] + column_energy[None, :]
    diagonal = (
        virtual_pairs[None, None, :, :]
        - first_energy[:, None, None, None]
        - second_energy[None, :, None, None]
    )
    values = amplitudes.reshape(first_count, second_count, virtual_count, local_virtual)
    result = diagonal * values.astype(F32) + cycle_term
    return result.reshape(pair_count, virtual_count, local_virtual).astype(BF16)


def on_device(amplitudes, *others):
    ring = lax.axis_size("pair") * amplitudes.shape[0] // OCC
    fits = lax.axis_size("virt") == 2 and amplitudes.shape[0] * 2 == OCC and ring == 8
    return (two_tiles if fits else any_tiles)(amplitudes, *others)


def solution(mesh):
    return jax.shard_map(
        on_device,
        mesh=mesh,
        in_specs=(P("pair", None, "virt"), P(None, "virt", "pair"), P(), P(), P()),
        out_specs=P("pair", None, "virt"),
        check_vma=False,
    )
```

```python
import functools

import jax
import jax.numpy as jnp
from jax import lax
from jax.experimental import pallas as pl
from jax.experimental.pallas import tpu as pltpu
from jax.sharding import PartitionSpec as P

OCC = 8
BF16, F32 = jnp.bfloat16, jnp.float32
VMEM_LIMIT = 20 * 2**20
WALLS = (1, 1, 1, 1, 16)
MIXED = 3
WHOLE = pl.BlockSpec(memory_space=pltpu.VMEM)
ANYWHERE = pl.BlockSpec(memory_space=pl.ANY)


def estimate(cost):
    return pl.CostEstimate(flops=int(cost * 10**9) + 1, bytes_accessed=1, transcendentals=0)


def kernel_call(
    body,
    name,
    grid,
    in_specs,
    out_specs,
    out_shapes,
    scratch=(),
    after=(),
    far=(),
    out=pltpu.VMEM,
    cost=0,
    aliases=None,
):
    extra = len(after)

    def kernel(*refs):
        keep = len(in_specs)
        body(*refs[:keep], *refs[keep + extra :])

    def call(*args):
        held = [
            a if a.ndim == 1 else pltpu.with_memory_space_constraint(a, pltpu.HBM if n in far else pltpu.VMEM)
            for n, a in enumerate((*args, *after))
        ]
        return pl.pallas_call(
            kernel,
            grid=grid,
            in_specs=[*in_specs, *[ANYWHERE] * extra],
            out_specs=list(out_specs),
            scratch_shapes=list(scratch),
            out_shape=[out(shape, kind) for shape, kind in out_shapes],
            compiler_params=pltpu.CompilerParams(
                dimension_semantics=("arbitrary",) * len(grid), vmem_limit_bytes=VMEM_LIMIT
            ),
            cost_estimate=estimate(cost),
            input_output_aliases=aliases or {},
            name=name,
        )(*held)

    return call


def position(count):
    groups = OCC // count
    pair = lax.axis_index("pair")
    return lax.axis_index("virt"), lax.rem(pair, groups), lax.div(pair, groups)


def swap(x, axis, bit):
    return lax.ppermute(x, axis, [(i, i ^ 1 << bit) for i in range(lax.axis_size(axis))])


def ring_of(count, groups):
    places = count // groups
    return list(range(0, places, 2)) + list(range(places - 1, 0, -2))


def along_ring(x, step, groups):
    order = ring_of(lax.axis_size("pair"), groups)
    pairs = [
        (a * groups + g, order[(n + step) % len(order)] * groups + g)
        for n, a in enumerate(order)
        for g in range(groups)
    ]
    return lax.ppermute(x, "pair", pairs)


def turn_kernel(part, amplitudes, near, far, own, own_rows, other, done):
    count, rows, width = near.shape
    tile = lax.axis_index("virt")
    first, second = pl.multiple_of(tile * width, 16), pl.multiple_of((1 - tile) * width, 16)
    columns = pl.ds(part * rows, rows)
    copies = []
    for j in range(count):
        sources = [
            (amplitudes.at[j, pl.ds(first, width), columns], own),
            (amplitudes.at[j, pl.ds(pl.multiple_of(first + part * rows, 16), rows)], own_rows),
            (amplitudes.at[j, pl.ds(second, width), columns], other),
        ]
        for n, (source, held) in enumerate(sources):
            copies.append(pltpu.make_async_copy(source, held.at[j], done.at[n, j]))
            copies[-1].start()
    for j in range(count):
        for copy in copies[3 * j : 3 * j + 3]:
            copy.wait()
        near[j] = (2.0 * own[j].astype(F32).T - own_rows[j].astype(F32)).astype(BF16)
        far[j] = other[j].T


def turn(amplitudes, part, parts, after=()):
    count, _, width = amplitudes.shape
    rows = width // parts
    tall, flat = (count, width, rows), (count, rows, width)
    return kernel_call(
        functools.partial(turn_kernel, part),
        "turn",
        (1,),
        [ANYWHERE],
        [WHOLE] * 2,
        [(flat, BF16)] * 2,
        [
            pltpu.VMEM(tall, BF16),
            pltpu.VMEM(flat, BF16),
            pltpu.VMEM(tall, BF16),
            pltpu.SemaphoreType.DMA((3, count)),
        ],
        after=after,
        far=(0,),
    )(amplitudes)


def cut_kernel(starts, *refs):
    outs, done = refs[-1 - len(starts) : -1], refs[-1]
    tile = lax.axis_index("virt")
    copies = []
    for n, (start, out) in enumerate(zip(starts, outs)):
        at = pl.multiple_of((1 - tile) * out.shape[2] + start, 16)
        source = refs[0].at[:, pl.ds(at, out.shape[1]), :]
        copies.append(pltpu.make_async_copy(source, out, done.at[n]))
    for copy in copies:
        copy.start()
    for copy in copies:
        copy.wait()


def cut(amplitudes, pieces, after=()):
    count, _, width = amplitudes.shape
    return kernel_call(
        functools.partial(cut_kernel, [start for start, _ in pieces]),
        "cut",
        (1,),
        [ANYWHERE],
        [WHOLE] * len(pieces),
        [((count, rows, width), BF16) for _, rows in pieces],
        [pltpu.SemaphoreType.DMA((len(pieces),))],
        after=after,
        far=(0,),
    )(amplitudes)


def mix_kernel(parts, start, at, *refs):
    far, arrived, out = refs[:parts], refs[parts], refs[-1]
    step = far[0].shape[1]
    first, last = 0, arrived.shape[1]
    while first < last:
        part, row = divmod(start + first, step)
        here = min(last - first, step - row)
        value = 2.0 * far[part][:, row : row + here].astype(F32)
        value -= arrived[:, first : first + here].astype(F32)
        out[:, at + first : at + first + here] = value.astype(BF16)
        first += here


def mix(far, arrived, start, rows=None, into=None, after=(), cost=0):
    count, more, width = arrived.shape
    at = start if into is not None else 0
    shape = (count, rows or more, width) if into is None else into.shape
    args = [*far, arrived] + ([] if into is None else [into])
    (out,) = kernel_call(
        functools.partial(mix_kernel, len(far), start, at),
        "mix",
        (1,),
        [WHOLE] * len(args),
        [WHOLE],
        [(shape, BF16)],
        after=after,
        cost=cost,
        aliases=None if into is None else {len(args) - 1: 0},
    )(*args)
    return out


def partial_kernel(shards, parts, joined, extras, *refs):
    same, cross = refs[:shards], refs[shards : 2 * shards]
    refs = refs[2 * shards :]
    arrays = sum(parts)
    mine, theirs, refs = refs[:arrays], refs[arrays : 2 * arrays], refs[2 * arrays :]
    extra, outs = refs[:extras], refs[extras:]
    count = mine[0].shape[0]
    _, group, _ = position(count)

    def together(arrays, j, group=0):
        pieces = [r[j + (group * count if r.shape[0] > count else 0)] for r in arrays]
        return jnp.concatenate(pieces, axis=0) if len(pieces) > 1 else pieces[0]

    totals = [None] * len(parts)
    for j in range(count):
        left, right = together(same, j, group), together(cross, j, 1 - group)
        for n in range(joined):
            value = (left, right)[n - joined]
            outs[1 + n][j] = jnp.concatenate([extra[n][j], value], axis=0) if extras else value
        at = 0
        for h, split in enumerate(parts):
            for shard, half in ((left, mine), (right, theirs)):
                half = together(half[at : at + split], j)
                value = jnp.dot(shard, half, preferred_element_type=F32)
                totals[h] = value if totals[h] is None else totals[h] + value
            at += split
    for h, total in enumerate(totals):
        outs[0][h] = total.astype(BF16)


def partial(same, cross, mine, theirs, joined=0, behind=(), after=()):
    parts = [len(m) for m in mine]
    shards, halves = len(same), len(mine)
    count, _, columns = mine[0][0].shape
    width = same[0].shape[2]
    rows = sum(v.shape[1] for v in same)
    args = [*same, *cross, *sum(mine, []), *sum(theirs, []), *behind]
    out_shapes = [((halves, rows, columns), BF16)]
    for n in range(joined):
        more = rows + (behind[n].shape[1] if behind else 0)
        out_shapes.append(((count, more, width), BF16))
    return kernel_call(
        functools.partial(partial_kernel, shards, parts, joined, len(behind)),
        "partial",
        (1,),
        [WHOLE] * len(args),
        [WHOLE] * len(out_shapes),
        out_shapes,
        after=after,
    )(*args)


def pick_kernel(forth, back, same, cross):
    count = same.shape[0]
    _, group, _ = position(count)
    for j in range(count):
        same[j] = forth[group * count + j]
        cross[j] = back[(1 - group) * count + j]


def pick(forth, back, after=()):
    shape = (forth.shape[0] // 2,) + forth.shape[1:]
    return kernel_call(
        pick_kernel, "pick", (1,), [WHOLE] * 2, [WHOLE] * 2, [(shape, BF16)] * 2, after=after
    )(forth, back)


def nothing(*refs):
    pass


def wall(*arrays, cost=0.1):
    held = [pltpu.with_memory_space_constraint(a, pltpu.VMEM) for a in arrays]
    return pl.pallas_call(
        nothing,
        in_specs=[ANYWHERE] * len(held),
        out_specs=ANYWHERE,
        out_shape=pltpu.VMEM((8, 128), F32),
        compiler_params=pltpu.CompilerParams(vmem_limit_bytes=2**20),
        cost_estimate=estimate(cost),
        name="wall",
    )(*held)


def join_kernel(counts, *refs):
    out, at = refs[-1], 0
    for h, count in enumerate(counts):
        own, sent = refs[at : at + count], refs[at + count : at + 2 * count]
        at += 2 * count
        left, right = [
            jnp.concatenate([r[...] for r in v], axis=0) if count > 1 else v[0][...]
            for v in (own, sent)
        ]
        out[h] = (left.astype(F32) + right.astype(F32)).astype(BF16)


def join(*halves, after=()):
    args, in_specs = [], []
    for pairs in halves:
        for side in range(2):
            for pair in pairs:
                v, h = pair[side]
                args.append(v)
                in_specs.append(pl.BlockSpec((None,) + v.shape[1:], functools.partial(lambda h, k: (h, 0, 0), h)))
    rows = sum(pair[0][0].shape[1] for pair in halves[0])
    shape = (len(halves), rows, args[0].shape[2])
    (out,) = kernel_call(
        functools.partial(join_kernel, [len(pairs) for pairs in halves]),
        "join",
        (1,),
        in_specs,
        [WHOLE],
        [(shape, BF16)],
        after=after,
    )(*args)
    return out


def joined_rows(pieces):
    return jnp.concatenate(pieces, axis=0) if len(pieces) > 1 else pieces[0]


def diagonal_kernel(values, energy, first_energy, second_energy, own, off, held, done):
    count, columns, width = own.shape
    here, group, place = position(count)
    copies = []
    for h in range(2):
        tile = lax.rem(here + h, 2)
        rows = pl.ds(pl.multiple_of(tile * columns, 16), columns)
        for j in range(count):
            copies.append(pltpu.make_async_copy(values.at[j, rows], held.at[h, j], done.at[h, j]))
            copies[-1].start()
    for h, out in enumerate((own, off)):
        row_energy = energy[lax.rem(here + h, 2)]
        row_energy = jnp.broadcast_to(row_energy, (128, columns)).T[:, :1]
        for j in range(count):
            occupied = first_energy[place] + second_energy[group * count + j]
            copies[h * count + j].wait()
            out[j] = (row_energy - occupied + energy[here]) * held[h, j].astype(F32)


def diagonal(amplitudes, energy_virtual, energy_first, energy_second, after=()):
    count, rows, width = amplitudes.shape
    block = (count, rows // 2, width)
    return kernel_call(
        diagonal_kernel,
        "diagonal",
        (1,),
        [ANYWHERE, WHOLE] + [pl.BlockSpec(memory_space=pltpu.SMEM)] * 2,
        [WHOLE] * 2,
        [(block, F32)] * 2,
        [pltpu.VMEM((2,) + block, BF16), pltpu.SemaphoreType.DMA((2, count))],
        after=after,
        far=(0,),
    )(amplitudes, energy_virtual.reshape(2, 1, width), energy_first, energy_second)


def residual_kernel(rows_of, depths_of, halves, last, *refs):
    chunks, shards = len(rows_of), len(depths_of)
    middles, vectors, refs = refs[:chunks], refs[chunks : chunks + shards], refs[chunks + shards :]
    count, _, width = vectors[0].shape
    before, outs = refs[: len(halves)], refs[len(halves) :]
    if last:
        out, held, done = outs
    columns = middles[0].shape[2]
    copies = []
    for n, h in enumerate(halves):
        rows = pl.ds(pl.multiple_of(lax.rem(lax.axis_index("virt") + h, 2) * columns, 16), columns)
        parts = [m[h if m.shape[0] > 1 else 0, a:b] for m, (a, b) in zip(middles, rows_of)]
        left = joined_rows(parts).T
        for j in range(count):
            right = joined_rows([v[j, a:b] for v, (a, b) in zip(vectors, depths_of)])
            total = jnp.dot(left, right, preferred_element_type=F32)
            total += before[n][j]
            if last:
                held[n, j] = total.astype(BF16)
                copies.append(pltpu.make_async_copy(held.at[n, j], out.at[j, rows], done.at[n, j]))
                copies[-1].start()
            else:
                outs[n][j] = total
    for copy in copies:
        copy.wait()


def residual(middles, vectors, halves, before, last=False, after=()):
    whole = lambda v: v if isinstance(v, tuple) else (v, 0, v.shape[1])
    middles, rows_of = zip(*[(v, (a, b)) for v, a, b in map(whole, middles)])
    vectors, depths_of = zip(*[(v, (a, b)) for v, a, b in map(whole, vectors)])
    count, _, width = vectors[0].shape
    block = (count, middles[0].shape[2], width)
    args = [*middles, *vectors, *before]
    out_shapes, scratch = [(block, F32)] * len(halves), []
    if last:
        out_shapes = [((count, 2 * block[1], width), BF16)]
        scratch = [pltpu.VMEM((2,) + block, BF16), pltpu.SemaphoreType.DMA((2, count))]
    return kernel_call(
        functools.partial(residual_kernel, rows_of, depths_of, halves, last),
        "residual",
        (1,),
        [WHOLE] * len(args),
        [ANYWHERE if last else WHOLE] * len(out_shapes),
        out_shapes,
        scratch,
        after=after,
        out=pltpu.HBM if last else pltpu.VMEM,
    )(*args)


def two_tiles(amplitudes, cholesky, energy_first, energy_second, energy_virtual):
    count, virtual, width = amplitudes.shape
    groups = OCC // count
    places = lax.axis_size("pair") // groups
    ring = functools.partial(along_ring, groups=groups)
    to_core = functools.partial(swap, axis="pair", bit=0)
    to_tile = functools.partial(swap, axis="virt", bit=0)

    unit = width // 32
    pieces = [(0, 16 * unit), (16 * unit, 12 * unit), (28 * unit, 4 * unit)]
    sent = cut(amplitudes, pieces[:1])
    sent += cut(amplitudes, pieces[1:], after=sent)
    arrived = [to_tile(v) for v in sent]

    own = jnp.swapaxes(cholesky, 1, 2)
    vectors = [own]
    forth, back = own, own
    for step in range(1, places // 2):
        forth, back = ring(forth, 1), ring(back, -1)
        vectors += [forth, back]

    near, near_theirs, far_turned = [], [], []
    held = sent[1:]
    parts = 4
    for part in range(parts):
        v, w = turn(amplitudes, part, parts, after=held)
        near.append(v)
        far_turned.append(w)
        near_theirs.append(to_core(v))
        if part == parts // 2 - 1:
            wall_1 = wall(*vectors[1:3], arrived[0], *near_theirs, cost=WALLS[0])
            held = [wall_1]
    begun = diagonal(amplitudes, energy_virtual, energy_first, energy_second, after=near)
    cut_at, cut_end = (sum(v.shape[1] for v in sent[:n]) for n in (1, 2))
    far_0 = mix(far_turned, arrived[0], 0, rows=cut_end, after=begun)
    wall_2 = wall(
        *vectors[3:5], arrived[1], *near_theirs[parts // 2 :], far_0, cost=WALLS[1]
    )
    far_0 = mix(far_turned, arrived[1], cut_at, into=far_0, after=[wall_2])
    far_0_theirs = to_core(far_0)
    near, near_theirs = [near], [near_theirs]
    n_a, same_a, cross_a = partial(
        vectors[:5], vectors[:5], near, near_theirs, joined=2, after=[far_0]
    )
    n_a_sent = to_tile(n_a)
    far_1 = mix(far_turned, arrived[2], far_0.shape[1], after=[n_a], cost=MIXED)
    far_1_theirs = to_core(far_1)
    far, far_theirs = [far_0, far_1], [far_0_theirs, far_1_theirs]
    f_a, cross_a = partial([same_a], [cross_a], [far], [far_theirs], joined=1)
    f_a_sent = to_tile(f_a)
    handed_a = to_core(cross_a)
    picked = pick(*vectors[5:7], after=[f_a, n_a_sent])
    same_c, cross_c = ring(picked[0], 1), ring(picked[1], -1)
    wall_3 = wall(*picked, cost=WALLS[2])
    halves, halves_theirs = near + [far], near_theirs + [far_theirs]
    p_b, same_b, cross_b = partial(
        vectors[5:7], vectors[5:7], halves, halves_theirs, joined=2, after=[wall_3]
    )
    p_b_sent = to_tile(p_b)
    m_off = join([((f_a, 0), (n_a_sent, 0))], after=[p_b])
    (begun_off,) = residual([m_off], [same_a], [1], begun[1:])
    m_a = join([((n_a, 0), (f_a_sent, 0))], [((f_a, 0), (n_a_sent, 0))], after=[begun_off])
    m_a_theirs = to_core(m_a)
    (begun_own,) = residual([m_a], [same_a], [0], begun[:1])
    wall_4 = wall(same_c, cross_c, begun_own, cost=WALLS[3])
    p_c, same_d, cross_d = partial(
        [same_c],
        [cross_c],
        halves,
        halves_theirs,
        joined=2,
        behind=[same_b, cross_b],
        after=[wall_4],
    )
    p_c_sent = to_tile(p_c)
    handed_d = to_core(cross_d)
    m_b = join(*[[((p_b, h), (p_b_sent, 1 - h))] for h in range(2)], after=[p_c])
    m_b_theirs = to_core(m_b)
    wall_5 = wall(m_b, cost=WALLS[4])
    rows_b = m_b.shape[1]
    taken = min(-m_a.shape[1] % 256 // 16 * 16, rows_b)
    extra = bool(taken)
    begun = residual(
        [m_a_theirs] + [(m_b, 0, taken)] * extra,
        [handed_a] + [(same_d, 0, taken)] * extra,
        [0, 1],
        [begun_own, begun_off],
        after=[wall_5],
    )
    m_c = join(*[[((p_c, h), (p_c_sent, 1 - h))] for h in range(2)], after=begun)
    m_c_theirs = to_core(m_c)
    middles, vectors = [m_b_theirs], [(handed_d, 0, rows_b)]
    if taken < rows_b:
        middles = [(m_b, taken, rows_b)] + middles
        vectors = [(same_d, taken, rows_b)] + vectors
    begun = residual(middles, vectors, [0, 1], begun, after=[m_c])
    end = same_d.shape[1]
    vectors = [(same_d, rows_b, end), (handed_d, rows_b, end)]
    (out,) = residual([m_c, m_c_theirs], vectors, [0, 1], begun, last=True)
    return out


def from_partner(x, axis, bit):
    return lax.ppermute(x, axis, [(i, i ^ 1 << bit) for i in range(lax.axis_size(axis))])


def any_tiles(amplitudes, cholesky, energy_first, energy_second, energy_virtual):
    pair_count, virtual_count, local_virtual = amplitudes.shape
    tiles_count = lax.axis_size("virt")
    first_count = max(pair_count // OCC, 1)
    second_count = pair_count // first_count
    offset = lax.axis_index("pair") * pair_count
    first_start = offset // OCC
    second_start = offset % OCC
    column_start = lax.axis_index("virt") * local_virtual
    blocks = amplitudes.reshape(pair_count, tiles_count, local_virtual, local_virtual)
    arrived = lax.all_to_all(blocks, "virt", split_axis=1, concat_axis=1, tiled=True)
    mirrored = jnp.swapaxes(arrived, 2, 3).reshape(pair_count, virtual_count, local_virtual)
    combined = (2.0 * amplitudes.astype(F32) - mirrored.astype(F32)).astype(BF16)
    combined = combined.reshape(first_count, second_count, virtual_count, local_virtual)
    vectors = lax.all_gather(cholesky, "pair", axis=2, tiled=True)
    chosen = lax.dynamic_slice_in_dim(vectors, second_start, second_count, 0)
    partial_value = jnp.einsum("ilad,ldq->iaq", combined, chosen, preferred_element_type=F32)
    collected = lax.psum(partial_value.astype(BF16), "virt").astype(F32)
    for bit in range((OCC // second_count).bit_length() - 1):
        collected = collected + from_partner(collected.astype(BF16), "pair", bit).astype(F32)
    reduced = collected.astype(BF16)
    cycle_term = jnp.einsum("iaq,lbq->ilab", reduced, chosen, preferred_element_type=F32)
    first_energy = lax.dynamic_slice_in_dim(energy_first, first_start, first_count, 0)
    second_energy = lax.dynamic_slice_in_dim(energy_second, second_start, second_count, 0)
    column_energy = lax.dynamic_slice_in_dim(energy_virtual, column_start, local_virtual, 0)
    virtual_pairs = energy_virtual[:, None] + column_energy[None, :]
    diagonal = (
        virtual_pairs[None, None, :, :]
        - first_energy[:, None, None, None]
        - second_energy[None, :, None, None]
    )
    values = amplitudes.reshape(first_count, second_count, virtual_count, local_virtual)
    result = diagonal * values.astype(F32) + cycle_term
    return result.reshape(pair_count, virtual_count, local_virtual).astype(BF16)


def on_device(amplitudes, *others):
    ring = lax.axis_size("pair") * amplitudes.shape[0] // OCC
    fits = lax.axis_size("virt") == 2 and amplitudes.shape[0] * 2 == OCC and ring == 8
    return (two_tiles if fits else any_tiles)(amplitudes, *others)


def solution(mesh):
    return jax.shard_map(
        on_device,
        mesh=mesh,
        in_specs=(P("pair", None, "virt"), P(None, "virt", "pair"), P(), P(), P()),
        out_specs=P("pair", None, "virt"),
        check_vma=False,
    )
```
